512 devices in a mesh: aln: 4 (over x), rows: 128 (over z, y, core).
Axes of the slice: x: 4, y: 8, z: 8, core: 2. Of those that a mesh axis runs over, the one named last changes fastest.
Arguments:
- sequence_stack: bfloat16 [512, 128, 768], P(('aln', 'rows')), parts along dimension 0, may hold values from -6 to 6
- protein_spans: int32 [4], P('aln'), parts along dimension 0, may hold values from 1 to 128
- twofold_contacts: bfloat16 [512, 128, 128], P(('aln', 'rows')), parts along dimension 0, may hold values from -6 to 6
- horizontal_projection_triple: bfloat16 [768, 2304], P(None, 'rows'), may hold values from -0.21875 to 0.21875
- horizontal_projection_out: bfloat16 [768, 768], P(None, 'rows'), may hold values from -0.21875 to 0.21875
- vertical_projection_triple: bfloat16 [768, 2304], P(None, 'rows'), may hold values from -0.21875 to 0.21875
- vertical_projection_out: bfloat16 [768, 768], P(None, 'rows'), may hold values from -0.21875 to 0.21875
- contact_logit_offsets: bfloat16 [128, 12], replicated, may hold values from -0.5 to 0.5
- contact_projection_weights: bfloat16 [12, 128], replicated, may hold values from -1.75 to 1.75
Outputs:
- alignment_output: bfloat16 [512, 128, 768], P('aln', 'rows'), parts along dimension 0
- pair_feature_output: bfloat16 [512, 128, 128], P(('aln', 'rows')), parts along dimension 0
The draws below stay inside these ranges and needn't reach their ends.
There are 4 independent parts, one for each index of `aln`. The reference program is written for one: setup_inputs(seed, part) draws one part's arguments, and reference() takes and returns one part's arrays. A program takes and returns all parts, laid end to end along the dimension named above; an argument that names none is the same for every part. Nothing has to cross between parts.
All inputs are finite; a program needn't handle non-finite values.
Results may differ from the reference program's by a relative error of at most 0.0075.
Values may be sent and summed in bfloat16 or wider, within the bound.
No kernel may reach another device: no remote copies, remote signals or barrier semaphores. Data moves between devices by JAX's collectives and lax.ppermute only.
A program may use at most 64 MiB of HBM per device.

```python
import jax
import jax.numpy as jnp
from jax import lax

D = 768
H = 12
P_SIZE = 128
R = 128
L = 128


def draw_sequence_stack(key, part):
    first = jax.random.fold_in(jax.random.fold_in(key, 11), 0)
    base = jnp.clip(jax.random.normal(first, (R, L, D), jnp.float32), -6.0, 6.0)
    return base.astype(jnp.bfloat16)


def levels(rng, dims, shards, least, high):
    loudness, own = 1.0, jax.random.fold_in(rng, 6)
    for axis_at, blocks in shards:
        heights = jnp.exp(jax.random.uniform(jax.random.fold_in(own, axis_at), (blocks,), jnp.float32, least / len(shards), high / len(shards)))
        loudness = loudness * jnp.repeat(heights, dims[axis_at] // blocks).reshape([-1 if axis == axis_at else 1 for axis in range(len(dims))])
    return loudness


def bell_draw(stream_key, extent, width, most, pieces=(), held_as=jnp.bfloat16):
    drawn = width * jax.random.normal(stream_key, extent, jnp.float32)
    if pieces:
        drawn = drawn * levels(stream_key, extent, pieces, -0.22, 0.18)
    return jnp.clip(drawn, -most, most).astype(held_as)


def setup_inputs(seed: int = 0, part: int = 0) -> dict:
    key_of = jax.random.split(jax.random.key(seed), 10)
    part_keys = jax.random.split(jax.random.fold_in(key_of[9], part), 10)
    return {
        "sequence_stack": draw_sequence_stack(jax.random.fold_in(jax.random.fold_in(key_of[9], part), 71), part),
        "protein_spans": jax.random.randint(part_keys[1], (1,), 1, L + 1).astype(jnp.int32),
        "twofold_contacts": bell_draw(part_keys[2], (L, L, P_SIZE), 1.0, 6.0, ((0, 128),)),
        "horizontal_projection_triple": bell_draw(key_of[3], (D, 3 * D), D ** -0.5, 0.21875, ((1, 128),)),
        "horizontal_projection_out": bell_draw(key_of[4], (D, D), D ** -0.5, 0.21875, ((1, 128),)),
        "vertical_projection_triple": bell_draw(key_of[5], (D, 3 * D), D ** -0.5, 0.21875, ((1, 128),)),
        "vertical_projection_out": bell_draw(key_of[6], (D, D), D ** -0.5, 0.21875, ((1, 128),)),
        "contact_logit_offsets": bell_draw(key_of[7], (P_SIZE, H), P_SIZE ** -0.5, 0.5),
        "contact_projection_weights": bell_draw(key_of[8], (H, P_SIZE), H ** -0.5, 1.75),
    }


def normalize(incoming_sequence_stack):
    center = lax.optimization_barrier(jnp.mean(incoming_sequence_stack, axis=-1, keepdims=True))
    spread = lax.optimization_barrier(jnp.mean(jnp.square(incoming_sequence_stack - center), axis=-1, keepdims=True))
    return (incoming_sequence_stack - center) * lax.rsqrt(spread + 1e-05)

def project_three(normed, weights, hidden_channel_size, head_count, shape_rows, shape_res):
    head_dim = hidden_channel_size // head_count
    packed = jnp.dot(normed, weights, preferred_element_type=jnp.float32)
    queries = (packed[:, :hidden_channel_size] * head_dim ** (-0.5)).astype(jnp.bfloat16)
    key_rows = packed[:, hidden_channel_size:2 * hidden_channel_size].astype(jnp.bfloat16)
    value_rows = packed[:, 2 * hidden_channel_size:].astype(jnp.bfloat16)
    input_dimensions = (shape_rows, shape_res, head_count, head_dim)
    return (queries.reshape(input_dimensions), key_rows.reshape(input_dimensions), value_rows.reshape(input_dimensions))

def reference(sequence_stack, protein_spans, twofold_contacts, horizontal_projection_triple, horizontal_projection_out, vertical_projection_triple, vertical_projection_out, contact_logit_offsets, contact_projection_weights):
    overall_sequence_number, sequence_positions, hidden_channel_size = sequence_stack.shape
    head_count = contact_logit_offsets.shape[1]
    channels = contact_logit_offsets.shape[0]
    incoming_sequence_stack = sequence_stack.astype(jnp.float32)
    normed = normalize(incoming_sequence_stack).astype(jnp.bfloat16).reshape(-1, hidden_channel_size)
    queries, key_rows, value_rows = project_three(normed, horizontal_projection_triple, hidden_channel_size, head_count, overall_sequence_number, sequence_positions)
    tied = jnp.einsum('rihe,rjhe->hij', queries.astype(jnp.float32), key_rows.astype(jnp.float32))
    bias_all = jnp.dot(twofold_contacts.reshape(-1, channels), contact_logit_offsets, preferred_element_type=jnp.float32)
    bias_all = bias_all.reshape(sequence_positions, sequence_positions, head_count).transpose(2, 0, 1)
    scores = tied * float(overall_sequence_number) ** (-0.5) + bias_all
    flat_scores = scores.astype(jnp.bfloat16).transpose(1, 2, 0).reshape(-1, head_count)
    pair_feature_output = (twofold_contacts.astype(jnp.float32) + jnp.dot(flat_scores, contact_projection_weights, preferred_element_type=jnp.float32).reshape(sequence_positions, sequence_positions, channels)).astype(jnp.bfloat16)
    key_valid = jnp.arange(sequence_positions, dtype=jnp.int32) < protein_spans[0]
    row_probs = jax.nn.softmax(jnp.where(key_valid[None, None, :], scores, -1e+30), axis=-1).astype(jnp.bfloat16)
    blended = jnp.einsum('hij,rjhe->rihe', row_probs.astype(jnp.float32), value_rows.astype(jnp.float32))
    blended = blended.astype(jnp.bfloat16).reshape(-1, hidden_channel_size)
    updated_alignment = (incoming_sequence_stack + jnp.dot(blended, horizontal_projection_out, preferred_element_type=jnp.float32).reshape(overall_sequence_number, sequence_positions, hidden_channel_size)).astype(jnp.bfloat16)
    col_normed = normalize(updated_alignment.astype(jnp.float32)).astype(jnp.bfloat16).reshape(-1, hidden_channel_size)
    col_queries, col_keys, col_values = project_three(col_normed, vertical_projection_triple, hidden_channel_size, head_count, overall_sequence_number, sequence_positions)

    def one_head(head):
        query_head = col_queries[:, :, head, :].astype(jnp.float32)
        key_head = col_keys[:, :, head, :].astype(jnp.float32)
        value_head = col_values[:, :, head, :].astype(jnp.float32)
        logits = jnp.einsum('ale,ble->lab', query_head, key_head)
        col_probs = jax.nn.softmax(logits, axis=-1).astype(jnp.bfloat16)
        return jnp.einsum('lab,ble->ale', col_probs.astype(jnp.float32), value_head)
    per_head = lax.map(one_head, jnp.arange(head_count, dtype=jnp.int32))
    column_mixed_output = per_head.transpose(1, 2, 0, 3).astype(jnp.bfloat16).reshape(-1, hidden_channel_size)
    alignment_output = (updated_alignment.astype(jnp.float32) + jnp.dot(column_mixed_output, vertical_projection_out, preferred_element_type=jnp.float32).reshape(overall_sequence_number, sequence_positions, hidden_channel_size)).astype(jnp.bfloat16)
    return (alignment_output, pair_feature_output)
```

```python
import functools

import jax
import jax.numpy as jnp
from jax import lax
from jax.experimental import pallas as pl
from jax.experimental.pallas import tpu as pltpu
from jax.sharding import Mesh
from jax.sharding import PartitionSpec as P

ALL = ("a", "z", "y", "c")
ROWS = ("z", "y", "c")
CHIPS = ("z", "y")
D, H, E, L, R = 768, 12, 64, 128, 128
BF, F32 = jnp.bfloat16, jnp.float32
VMEM = pl.BlockSpec(memory_space=pltpu.VMEM)
SMEM = pl.BlockSpec(memory_space=pltpu.SMEM)


def params():
    return pltpu.CompilerParams(vmem_limit_bytes=48 << 20)


def dot_nt(a, b):
    return lax.dot_general(a, b, (((1,), (1,)), ((), ())), preferred_element_type=F32)


def dot_tn(a, b):
    return lax.dot_general(a, b, (((0,), (0,)), ((), ())), preferred_element_type=F32)


def first_head(y):
    return 3 * (y // 2) + y % 2


def normalize(x):
    center = jnp.mean(x, axis=-1, keepdims=True)
    spread = jnp.mean(jnp.square(x - center), axis=-1, keepdims=True)
    return (x - center) * lax.rsqrt(spread + 1e-05)


def project_and_tie(y_ref, w_ref, *refs):
    row_refs, (tied_ref, v_ref) = refs[:9], refs[9:]
    w = w_ref[...]
    lane = lax.broadcasted_iota(jnp.int32, (L, 2 * E), 1)
    offsets = (0, -1, 1, -2, 2, -3, 3, 4)
    tied = [jnp.zeros((L, L), F32), jnp.zeros((L, L), F32)]
    for n, offset in enumerate(offsets):
        if n < 7:
            x = row_refs[n][...]
        else:
            x = jnp.concatenate([row_refs[7][...], row_refs[8][...]], axis=0)
        packed = jnp.dot(x, w, preferred_element_type=F32)
        q = packed[:, : 2 * E] * E**-0.5
        k = packed[:, 2 * E : 4 * E].astype(BF)
        v_ref[lax.rem(y_ref[0] + (8 + offset), 8)] = packed[:, 4 * E :].astype(BF)
        tied[0] += dot_nt(jnp.where(lane < E, q, 0.0).astype(BF), k)
        tied[1] += dot_nt(jnp.where(lane < E, 0.0, q).astype(BF), k)
    for h in range(2):
        tied_ref[h] = tied[h] * R**-0.5


def attend(span_ref, part_ref, bias_ref, out_ref):
    scores = bias_ref[...].astype(F32)
    for n in range(8):
        scores += part_ref[n].astype(F32)
    j = lax.broadcasted_iota(jnp.int32, (L, L), 1)
    masked = jnp.where(j < span_ref[0], scores, -1e30)
    e = jnp.exp(masked - jnp.max(masked, axis=1, keepdims=True))
    out_ref[0] = (e / jnp.sum(e, axis=1, keepdims=True)).astype(BF)
    out_ref[1] = scores.astype(BF)


def blend(y_ref, probs_ref, v_ref, out_ref, held):
    lane = lax.broadcasted_iota(jnp.int32, (L, 2 * E), 1)
    low = lane < E
    odd = lax.rem(y_ref[0], 2) == 1
    plain = [probs_ref[h, 1].astype(F32) for h in range(2)]
    moved = [pltpu.roll(s, E, 1) for s in plain]
    for n in range(8):
        v = v_ref[n]
        o = jnp.where(
            low,
            jnp.dot(probs_ref[0, 0], v, preferred_element_type=F32),
            jnp.dot(probs_ref[1, 0], v, preferred_element_type=F32),
        )
        h, half = (n % 4) // 2, n % 2
        if n < 4:
            extra = moved[h] if half else plain[h]
            o = jnp.where(jnp.logical_and(low, odd), extra, o)
        else:
            extra = plain[h] if half else moved[h]
            o = jnp.where(jnp.logical_or(low, odd), o, extra)
        held[:, n, :] = o
    out_ref[...] = held[...].astype(BF)


def column_block(
    c_ref, bl_ref, stack_ref, g_ref, pair_ref, cw_ref, out_ref, pair_out_ref, tall, feat, packed, mixed
):
    mine = c_ref[0]
    lane = lax.broadcasted_iota(jnp.int32, (L, L), 1)
    row = lax.broadcasted_iota(jnp.int32, (L, L), 0)
    low = lane < E
    early = lax.rem(row, 8) < 4

    def tile(c, z, y):
        both = bl_ref[c, z * 8 + y].astype(F32)
        return jnp.where(mine == 0, both[:8], both[8:])

    tiles = [[tile(c, z, y) for c in range(2) for z in range(8)] for y in range(8)]
    blocks = [jnp.concatenate(t, axis=0) for t in tiles]
    parts = []
    for n in range(2):
        e0, o0, e1, o1 = blocks[4 * n : 4 * n + 4]
        ro0, re1 = pltpu.roll(o0, E, 1), pltpu.roll(e1, E, 1)
        parts.append(jnp.where(jnp.logical_or(low, early), e0, ro0))
        parts.append(jnp.where(low, ro0, re1))
        parts.append(jnp.where(jnp.logical_and(low, early), re1, o1))
    blended = jnp.concatenate(parts, axis=1).astype(BF)

    tail = g_ref[:, 16:32, :].reshape(2048, D)
    tall[...] = dot_nt(tail, blended)
    for d in range(128):
        feat[6 * d : 6 * d + 6, :] = tall[16 * d + 8 : 16 * d + 14, :]
    for n in range(6):
        own = jnp.concatenate([stack_ref[:, 128 * n : 128 * n + 128]], axis=1).astype(F32).T
        feat[128 * n : 128 * n + 128, :] += own
    updated = feat[...].astype(BF).astype(F32)
    feat[...] = updated
    center = jnp.mean(updated, axis=0, keepdims=True)
    spread = jnp.mean(jnp.square(updated - center), axis=0, keepdims=True)
    normed = ((updated - center) * lax.rsqrt(spread + 1e-05)).astype(BF)

    tall[...] = jnp.dot(g_ref[:, 0:16, :].reshape(2048, D), normed, preferred_element_type=F32)
    for d in range(128):
        packed[18 * d : 18 * d + 16, :] = tall[16 * d : 16 * d + 16, :]
    tall[...] = jnp.dot(tail, normed, preferred_element_type=F32)
    for d in range(128):
        packed[18 * d + 16 : 18 * d + 18, :] = tall[16 * d : 16 * d + 2, :]

    for h in range(H):
        q = (packed[E * h : E * h + E, :] * E**-0.5).astype(BF)
        k = packed[D + E * h : D + E * h + E, :].astype(BF)
        v = packed[2 * D + E * h : 2 * D + E * h + E, :].astype(BF)
        logits = dot_tn(k, q)
        e = jnp.exp(logits - jnp.max(logits, axis=0, keepdims=True))
        probs = (e / jnp.sum(e, axis=0, keepdims=True)).astype(BF)
        mixed[E * h : E * h + E, :] = jnp.dot(v, probs, preferred_element_type=F32).astype(BF)

    tall[...] = jnp.dot(tail, mixed[...], preferred_element_type=F32)
    for d in range(128):
        feat[6 * d : 6 * d + 6, :] += tall[16 * d + 2 : 16 * d + 8, :]
    place = (lax.rem(row, 2) * E + row // 2 == lane).astype(BF)
    out_ref[...] = dot_nt(place, feat[...].astype(BF)).astype(BF)

    one = lax.broadcasted_iota(jnp.int32, (1, L), 1) < E
    lines = []
    for n in range(4):
        e, o = tiles[2 * n][0], tiles[2 * n + 1][0]
        re, ro = pltpu.roll(e, E, 1), pltpu.roll(o, E, 1)
        lines.append(jnp.where(one, re[4:5], e[5:6]))
        lines.append(jnp.where(one, re[6:7], e[7:8]))
        lines.append(jnp.where(one, o[2:3], ro[3:4]))
    scores = jnp.concatenate(lines + [jnp.zeros((L - H, L), F32)], axis=0).T
    weights = jnp.concatenate([cw_ref[...].astype(F32), jnp.zeros((L - H, L), F32)], axis=0)
    pair = pair_ref[...].astype(F32) + jnp.dot(
        scores.astype(BF), weights.astype(BF), preferred_element_type=F32
    )
    pair_out_ref[...] = pair.astype(BF)


def ring_rows(x):
    right = [(i, (i + 1) % 8) for i in range(8)]
    left = [(i, (i + 7) % 8) for i in range(8)]
    from_left, from_right = [x], [x]
    for step in range(3):
        from_left.append(lax.ppermute(from_left[-1], "y", right))
        from_right.append(lax.ppermute(from_right[-1], "y", left))
    far = [
        lax.ppermute(from_left[-1][: L // 2], "y", right),
        lax.ppermute(from_right[-1][L // 2 :], "y", left),
    ]
    return [x] + [t[n] for n in (1, 2, 3) for t in (from_left, from_right)] + far


def per_device(stack, spans, pair, w_triple, w_out, v_triple, v_out, offsets, contact_w):
    y, c = lax.axis_index("y"), lax.axis_index("c")
    y1, c1 = y[None].astype(jnp.int32), c[None].astype(jnp.int32)
    pair_own = pair.reshape(L, 128)
    own_row = stack.reshape(L, D)

    column_weights = jnp.concatenate([v_triple.T, v_out.T, w_out.T, jnp.zeros((2, D), BF)], axis=0)
    gathered = lax.all_gather(column_weights, ROWS, axis=0, tiled=False)

    normed = normalize(own_row.astype(F32)).astype(BF)
    rows = ring_rows(normed)

    bias = lax.dot_general(offsets, pair_own, (((0,), (1,)), ((), ())), preferred_element_type=F32).astype(BF)
    bias_pairs = jnp.stack([bias[first_head(n) : first_head(n) + 2] for n in range(8)])
    slices = w_triple.T.reshape(18, 2, 8, 48).transpose(2, 0, 1, 3).reshape(8, 1, 18, 96)
    slices = jnp.pad(slices, ((0, 0), (0, 0), (0, 0), (0, 32)))
    message = jnp.concatenate(
        [
            jnp.broadcast_to(slices, (8, 8, 18, 128)).reshape(64, 18, 128),
            own_row.reshape(64, 12, 128),
            jnp.broadcast_to(bias_pairs[None], (8, 8, 2, 128)).reshape(64, 2, 128),
        ],
        axis=1,
    )
    came = lax.all_to_all(message, CHIPS, 0, 0, tiled=True)

    source = lax.broadcasted_iota(jnp.int32, (2048, 384), 0)
    target = lax.broadcasted_iota(jnp.int32, (2048, 384), 1)
    column = (source // 32 * 2 + c) * 18 + source % 32
    wanted = target // 128 * D + first_head(y) * E + target % 128
    pick = jnp.logical_and(column == wanted, source % 32 < 18).astype(BF)
    picked = dot_tn(came.reshape(2048, 128), pick)[:96].astype(BF)
    picked = lax.all_gather(picked, "c", axis=0, tiled=False)
    half = lax.dynamic_slice_in_dim(picked, c * 48, 48, axis=1)
    half = half[0] + half[1]
    over_z = lax.all_to_all(jnp.broadcast_to(half, (8, 48, 384)), "z", 0, 0, tiled=True)
    w_heads = lax.all_gather(over_z, "c", axis=0, tiled=False).reshape(D, 384)

    rest = lax.all_gather(came[:, 18:, :], "c", axis=0, tiled=False)
    stack_own = rest[:, :, :12].reshape(2, 64, 2, D)
    stack_own = lax.dynamic_index_in_dim(stack_own, c, 2, keepdims=False).reshape(R, D)
    bias_own = lax.dynamic_index_in_dim(rest[:, :, 12:], c, 2, keepdims=False)
    bias_own = bias_own.transpose(1, 0, 2).reshape(L, L)

    tied, values = pl.pallas_call(
        project_and_tie,
        out_shape=(
            jax.ShapeDtypeStruct((2, L, L), F32),
            jax.ShapeDtypeStruct((8, L, 2 * E), BF),
        ),
        in_specs=[SMEM] + [VMEM] * 10,
        out_specs=(VMEM, VMEM),
        compiler_params=params(),
    )(y1, w_heads, *rows)

    tied = lax.all_gather(tied, "c", axis=0, tiled=False)
    tied = lax.dynamic_index_in_dim(tied, c, 1, keepdims=False)
    tied = (tied[0] + tied[1]).astype(BF)
    parts = lax.all_to_all(jnp.broadcast_to(tied, (8, L, L)), "z", 0, 0, tiled=True)
    head = pl.pallas_call(
        attend,
        out_shape=jax.ShapeDtypeStruct((2, L, L), BF),
        in_specs=[SMEM, VMEM, VMEM],
        out_specs=VMEM,
        compiler_params=params(),
    )(spans, parts, bias_own)
    heads = lax.all_gather(head, "c", axis=0, tiled=False)
    message = pl.pallas_call(
        blend,
        out_shape=jax.ShapeDtypeStruct((L, 8, 2 * E), BF),
        in_specs=[SMEM, VMEM, VMEM],
        out_specs=VMEM,
        scratch_shapes=[pltpu.VMEM((L, 8, 2 * E), F32)],
        compiler_params=params(),
    )(y1, heads, values)
    came = lax.all_to_all(message.reshape(64, 16, 128), CHIPS, 0, 0, tiled=True)
    blended = lax.all_gather(came, "c", axis=0, tiled=False)

    alignment, pair_out = pl.pallas_call(
        column_block,
        out_shape=(jax.ShapeDtypeStruct((R, D), BF), jax.ShapeDtypeStruct((L, 128), BF)),
        in_specs=[SMEM] + [VMEM] * 5,
        out_specs=(VMEM, VMEM),
        scratch_shapes=[
            pltpu.VMEM((2048, L), F32),
            pltpu.VMEM((D, L), F32),
            pltpu.VMEM((3 * D, L), F32),
            pltpu.VMEM((D, L), BF),
        ],
        compiler_params=params(),
    )(c1, blended, stack_own, gathered, pair_own, contact_w)
    return alignment.reshape(R, 1, D), pair_out.reshape(1, L, 128)


def solution(mesh):
    torus = Mesh(mesh.devices.reshape(mesh.shape["aln"], 8, 8, 2), ALL)
    in_specs = (
        P(ALL, None, None),
        P("a"),
        P(ALL, None, None),
        P(None, ROWS),
        P(None, ROWS),
        P(None, ROWS),
        P(None, ROWS),
        P(),
        P(),
    )
    out_specs = (P("a", ROWS, None), P(ALL, None, None))
    return jax.shard_map(
        per_device, mesh=torus, in_specs=in_specs, out_specs=out_specs, check_vma=False
    )
```

```python
import functools

import jax
import jax.numpy as jnp
from jax import lax
from jax.experimental import pallas as pl
from jax.experimental.pallas import tpu as pltpu
from jax.sharding import Mesh
from jax.sharding import PartitionSpec as P

ALL = ("a", "z", "y", "c")
ROWS = ("z", "y", "c")
CHIPS = ("z", "y")
D, H, E, L, R = 768, 12, 64, 128, 128
BF, F32 = jnp.bfloat16, jnp.float32
VMEM = pl.BlockSpec(memory_space=pltpu.VMEM)
SMEM = pl.BlockSpec(memory_space=pltpu.SMEM)


def params():
    return pltpu.CompilerParams(vmem_limit_bytes=48 << 20)


def dot_nt(a, b):
    return lax.dot_general(a, b, (((1,), (1,)), ((), ())), preferred_element_type=F32)


def dot_tn(a, b):
    return lax.dot_general(a, b, (((0,), (0,)), ((), ())), preferred_element_type=F32)


def first_head(y):
    return 3 * (y // 2) + y % 2


def normalize(x):
    center = jnp.mean(x, axis=-1, keepdims=True)
    spread = jnp.mean(jnp.square(x - center), axis=-1, keepdims=True)
    return (x - center) * lax.rsqrt(spread + 1e-05)


def project_and_tie(y_ref, w_ref, *refs):
    row_refs, (left_ref, right_ref, tied_ref, v_ref) = refs[:5], refs[5:]
    w = w_ref[...]
    lane = lax.broadcasted_iota(jnp.int32, (L, 2 * E), 1)
    offsets = (0, -1, 1, -2, 2, -3, 3, 4)
    tied = [jnp.zeros((L, L), F32), jnp.zeros((L, L), F32)]
    for n, offset in enumerate(offsets):
        if n < 5:
            x = row_refs[n][...]
        elif n < 7:
            x = refs[n][:L]
        else:
            x = jnp.concatenate([left_ref[L:], right_ref[L:]], axis=0)
        packed = jnp.dot(x, w, preferred_element_type=F32)
        q = packed[:, : 2 * E] * E**-0.5
        k = packed[:, 2 * E : 4 * E].astype(BF)
        v_ref[lax.rem(y_ref[0] + (8 + offset), 8)] = packed[:, 4 * E :].astype(BF)
        tied[0] += dot_nt(jnp.where(lane < E, q, 0.0).astype(BF), k)
        tied[1] += dot_nt(jnp.where(lane < E, 0.0, q).astype(BF), k)
    for h in range(2):
        tied_ref[h] = tied[h] * R**-0.5


def attend(span_ref, part_ref, bias_ref, out_ref):
    scores = bias_ref[...].astype(F32)
    for n in range(8):
        scores += part_ref[n].astype(F32)
    j = lax.broadcasted_iota(jnp.int32, (L, L), 1)
    masked = jnp.where(j < span_ref[0], scores, -1e30)
    e = jnp.exp(masked - jnp.max(masked, axis=1, keepdims=True))
    out_ref[0] = (e / jnp.sum(e, axis=1, keepdims=True)).astype(BF)
    out_ref[1] = scores.astype(BF)


def blend(y_ref, probs_ref, v_ref, out_ref, held):
    lane = lax.broadcasted_iota(jnp.int32, (L, 2 * E), 1)
    low = lane < E
    odd = lax.rem(y_ref[0], 2) == 1
    plain = [probs_ref[h, 1].astype(F32) for h in range(2)]
    moved = [pltpu.roll(s, E, 1) for s in plain]
    for n in range(8):
        v = v_ref[n]
        o = jnp.where(
            low,
            jnp.dot(probs_ref[0, 0], v, preferred_element_type=F32),
            jnp.dot(probs_ref[1, 0], v, preferred_element_type=F32),
        )
        h, half = (n % 4) // 2, n % 2
        if n < 4:
            extra = moved[h] if half else plain[h]
            o = jnp.where(jnp.logical_and(low, odd), extra, o)
        else:
            extra = plain[h] if half else moved[h]
            o = jnp.where(jnp.logical_or(low, odd), o, extra)
        held[:, n, :] = o
    out_ref[...] = held[...].astype(BF)


def column_block(c_ref, bl_ref, stack_ref, who_ref, wv_ref, wvo_ref, pair_ref, cw_ref, out_ref, pair_out_ref):
    mine = c_ref[0]
    lane = lax.broadcasted_iota(jnp.int32, (L, L), 1)
    row = lax.broadcasted_iota(jnp.int32, (L, L), 0)
    low = lane < E
    early = lax.rem(row, 8) < 4

    def tile(c, z, y):
        both = bl_ref[c, z * 8 + y].astype(F32)
        return jnp.where(mine == 0, both[:8], both[8:])

    tiles = [[tile(c, z, y) for c in range(2) for z in range(8)] for y in range(8)]
    blocks = [jnp.concatenate(t, axis=0) for t in tiles]
    parts = []
    for n in range(2):
        e0, o0, e1, o1 = blocks[4 * n : 4 * n + 4]
        ro0, re1 = pltpu.roll(o0, E, 1), pltpu.roll(e1, E, 1)
        parts.append(jnp.where(jnp.logical_or(low, early), e0, ro0))
        parts.append(jnp.where(low, ro0, re1))
        parts.append(jnp.where(jnp.logical_and(low, early), re1, o1))
    blended = jnp.concatenate(parts, axis=1).astype(BF)

    updated = (dot_nt(who_ref[...], blended) + stack_ref[...].astype(F32)).astype(BF).astype(F32)
    center = jnp.mean(updated, axis=0, keepdims=True)
    spread = jnp.mean(jnp.square(updated - center), axis=0, keepdims=True)
    normed = ((updated - center) * lax.rsqrt(spread + 1e-05)).astype(BF)
    packed = jnp.dot(wv_ref[...], normed, preferred_element_type=F32)

    mixed = []
    for h in range(H):
        q = (packed[E * h : E * h + E] * E**-0.5).astype(BF)
        k = packed[D + E * h : D + E * h + E].astype(BF)
        v = packed[2 * D + E * h : 2 * D + E * h + E].astype(BF)
        logits = dot_tn(k, q)
        e = jnp.exp(logits - jnp.max(logits, axis=0, keepdims=True))
        probs = (e / jnp.sum(e, axis=0, keepdims=True)).astype(BF)
        mixed.append(jnp.dot(v, probs, preferred_element_type=F32).astype(BF))
    mixed = jnp.concatenate(mixed, axis=0)

    result = (updated + jnp.dot(wvo_ref[...], mixed, preferred_element_type=F32)).astype(BF)
    place = (lax.rem(row, 2) * E + row // 2 == lane).astype(BF)
    out_ref[...] = dot_nt(place, result).astype(BF)

    one = lax.broadcasted_iota(jnp.int32, (1, L), 1) < E
    lines = []
    for n in range(4):
        e, o = tiles[2 * n][0], tiles[2 * n + 1][0]
        re, ro = pltpu.roll(e, E, 1), pltpu.roll(o, E, 1)
        lines.append(jnp.where(one, re[4:5], e[5:6]))
        lines.append(jnp.where(one, re[6:7], e[7:8]))
        lines.append(jnp.where(one, o[2:3], ro[3:4]))
    scores = jnp.concatenate(lines + [jnp.zeros((L - H, L), F32)], axis=0).T
    weights = jnp.concatenate([cw_ref[...].astype(F32), jnp.zeros((L - H, L), F32)], axis=0)
    pair = pair_ref[...].astype(F32) + jnp.dot(
        scores.astype(BF), weights.astype(BF), preferred_element_type=F32
    )
    pair_out_ref[...] = pair.astype(BF)


def moved(x, step):
    return lax.ppermute(x, "y", [(i, (i + step) % 8) for i in range(8)])


def per_device(stack, spans, pair, w_triple, w_out, v_triple, v_out, offsets, contact_w):
    y, c = lax.axis_index("y"), lax.axis_index("c")
    y1, c1 = y[None].astype(jnp.int32), c[None].astype(jnp.int32)
    pair_own = pair.reshape(L, 128)
    own_row = stack.reshape(L, D)

    column_weights = jnp.concatenate([v_triple.T, v_out.T, w_out.T, jnp.zeros((2, D), BF)], axis=0)
    gathered = lax.all_gather(column_weights, ROWS, axis=0, tiled=False)

    normed = normalize(own_row.astype(F32)).astype(BF)
    near = [moved(normed, step) for step in (1, -1, 2, -2)]

    bias = lax.dot_general(offsets, pair_own, (((0,), (1,)), ((), ())), preferred_element_type=F32).astype(BF)
    bias_pairs = jnp.stack([bias[first_head(n) : first_head(n) + 2] for n in range(8)])
    slices = w_triple.T.reshape(18, 2, 8, 48).transpose(2, 0, 1, 3).reshape(8, 1, 18, 96)
    slices = jnp.pad(slices, ((0, 0), (0, 0), (0, 0), (0, 32)))
    message = jnp.concatenate(
        [
            jnp.broadcast_to(slices, (8, 8, 18, 128)).reshape(64, 18, 128),
            own_row.reshape(64, 12, 128),
            jnp.broadcast_to(bias_pairs[None], (8, 8, 2, 128)).reshape(64, 2, 128),
        ],
        axis=1,
    )
    came = lax.all_to_all(message, CHIPS, 0, 0, tiled=True)
    far = [
        moved(jnp.concatenate([near[0], near[2][: L // 2]]), 2),
        moved(jnp.concatenate([near[1], near[3][L // 2 :]]), -2),
    ]
    came, *near = lax.optimization_barrier((came, *near))

    source = lax.broadcasted_iota(jnp.int32, (2048, 384), 0)
    target = lax.broadcasted_iota(jnp.int32, (2048, 384), 1)
    column = (source // 32 * 2 + c) * 18 + source % 32
    wanted = target // 128 * D + first_head(y) * E + target % 128
    pick = jnp.logical_and(column == wanted, source % 32 < 18).astype(BF)
    picked = dot_tn(came.reshape(2048, 128), pick)[:96].astype(BF)
    picked = lax.all_gather(picked, "c", axis=0, tiled=False)
    half = lax.dynamic_slice_in_dim(picked, c * 48, 48, axis=1)
    half = half[0] + half[1]
    over_z = lax.all_to_all(jnp.broadcast_to(half, (8, 48, 384)), "z", 0, 0, tiled=True)
    w_heads = lax.all_gather(over_z, "c", axis=0, tiled=False).reshape(D, 384)

    rest = lax.all_gather(came[:, 18:, :], "c", axis=0, tiled=False)
    stack_own = rest[:, :, :12].reshape(2, 64, 2, D)
    stack_own = lax.dynamic_index_in_dim(stack_own, c, 2, keepdims=False).reshape(R, D)
    bias_own = lax.dynamic_index_in_dim(rest[:, :, 12:], c, 2, keepdims=False)
    bias_own = bias_own.transpose(1, 0, 2).reshape(L, L)

    tied, values = pl.pallas_call(
        project_and_tie,
        out_shape=(
            jax.ShapeDtypeStruct((2, L, L), F32),
            jax.ShapeDtypeStruct((8, L, 2 * E), BF),
        ),
        in_specs=[SMEM] + [VMEM] * 8,
        out_specs=(VMEM, VMEM),
        compiler_params=params(),
    )(y1, w_heads, normed, *near, *far)

    tied = lax.all_gather(tied, "c", axis=0, tiled=False)
    tied = lax.dynamic_index_in_dim(tied, c, 1, keepdims=False)
    tied = (tied[0] + tied[1]).astype(BF)
    parts = lax.all_to_all(jnp.broadcast_to(tied, (8, L, L)), "z", 0, 0, tiled=True)
    head = pl.pallas_call(
        attend,
        out_shape=jax.ShapeDtypeStruct((2, L, L), BF),
        in_specs=[SMEM, VMEM, VMEM],
        out_specs=VMEM,
        compiler_params=params(),
    )(spans, parts, bias_own)
    heads = lax.all_gather(head, "c", axis=0, tiled=False)
    message = pl.pallas_call(
        blend,
        out_shape=jax.ShapeDtypeStruct((L, 8, 2 * E), BF),
        in_specs=[SMEM, VMEM, VMEM],
        out_specs=VMEM,
        scratch_shapes=[pltpu.VMEM((L, 8, 2 * E), F32)],
        compiler_params=params(),
    )(y1, heads, values)
    came = lax.all_to_all(message.reshape(64, 16, 128), CHIPS, 0, 0, tiled=True)
    column_triple = gathered[:, :18].reshape(3 * D, D)
    column_out = gathered[:, 18:24].reshape(D, D)
    row_out = gathered[:, 24:30].reshape(D, D)
    came, column_triple, column_out, row_out = lax.optimization_barrier(
        (came, column_triple, column_out, row_out)
    )
    blended = lax.all_gather(came, "c", axis=0, tiled=False)

    alignment, pair_out = pl.pallas_call(
        column_block,
        out_shape=(jax.ShapeDtypeStruct((R, D), BF), jax.ShapeDtypeStruct((L, 128), BF)),
        in_specs=[SMEM] + [VMEM] * 7,
        out_specs=(VMEM, VMEM),
        compiler_params=params(),
    )(c1, blended, stack_own.T, row_out, column_triple, column_out, pair_own, contact_w)
    return alignment.reshape(R, 1, D), pair_out.reshape(1, L, 128)


def solution(mesh):
    torus = Mesh(mesh.devices.reshape(mesh.shape["aln"], 8, 8, 2), ALL)
    in_specs = (
        P(ALL, None, None),
        P("a"),
        P(ALL, None, None),
        P(None, ROWS),
        P(None, ROWS),
        P(None, ROWS),
        P(None, ROWS),
        P(),
        P(),
    )
    out_specs = (P("a", ROWS, None), P(ALL, None, None))
    return jax.shard_map(
        per_device, mesh=torus, in_specs=in_specs, out_specs=out_specs, check_vma=False
    )
```

```python
import jax
import jax.numpy as jnp
from jax import lax
from jax.experimental import pallas as pl
from jax.experimental.pallas import tpu as pltpu
from jax.sharding import Mesh
from jax.sharding import PartitionSpec as P

ROWS = ("zh", "zl", "yh", "yl", "c")
ALL = ("a",) + ROWS
CHIPS = ROWS[:4]
FAR = ("zh", "yh")
D, H, E, L, R = 768, 12, 64, 128, 128
BF, F32 = jnp.bfloat16, jnp.float32
VMEM = pl.BlockSpec(memory_space=pltpu.VMEM)
SMEM = pl.BlockSpec(memory_space=pltpu.SMEM)


def params():
    return pltpu.CompilerParams(vmem_limit_bytes=48 << 20)


def dot_nt(a, b):
    return lax.dot_general(a, b, (((1,), (1,)), ((), ())), preferred_element_type=F32)


def dot_tn(a, b):
    return lax.dot_general(a, b, (((0,), (0,)), ((), ())), preferred_element_type=F32)


def normalize(x):
    center = jnp.mean(x, axis=-1, keepdims=True)
    spread = jnp.mean(jnp.square(x - center), axis=-1, keepdims=True)
    return (x - center) * lax.rsqrt(spread + 1e-05)


def spread_columns(c_ref, picked_ref, out_ref):
    both = picked_ref[0].astype(F32) + picked_ref[1].astype(F32)
    second = c_ref[0] == 1
    parts = []
    for n in range(3):
        three = both[:, 192 * n : 192 * n + 192]
        parts.append(jnp.where(second, three[:, 64:], three[:, :128]))
    mine = jnp.concatenate(parts, axis=1).astype(BF)
    for n in range(16):
        out_ref[n] = mine


def project_and_tie(at_ref, w_ref, near_ref, far_ref, tied_ref, v_ref):
    w = w_ref[...]
    lane = lax.broadcasted_iota(jnp.int32, (L, 2 * E), 1)
    zl, yl = at_ref[0], at_ref[1]
    tied = [jnp.zeros((L, L), F32), jnp.zeros((L, L), F32)]
    for n, ref in enumerate((near_ref, far_ref)):
        for core in range(2):
            for m in range(2):
                packed = jnp.dot(ref[core, m], w, preferred_element_type=F32)
                q = packed[:, : 2 * E] * E**-0.5
                k = packed[:, 2 * E : 4 * E].astype(BF)
                slot = 4 * lax.rem(zl + n, 2) + 2 * lax.rem(yl + m, 2) + core
                v_ref[slot] = packed[:, 4 * E :].astype(BF)
                tied[0] += dot_nt(jnp.where(lane < E, q, 0.0).astype(BF), k)
                tied[1] += dot_nt(jnp.where(lane < E, 0.0, q).astype(BF), k)
    for h in range(2):
        part = (tied[h] * R**-0.5).astype(BF)
        for n in range(4):
            tied_ref[n, h] = part


def add_four(part_ref, out_ref):
    total = part_ref[0].astype(F32)
    for n in range(1, 4):
        total += part_ref[n].astype(F32)
    total = total.astype(BF)
    for n in range(4):
        out_ref[n] = total


def attend(c_ref, span_ref, part_ref, bias_ref, v_ref, out_ref, held):
    lane = lax.broadcasted_iota(jnp.int32, (L, 2 * E), 1)
    low = lane < E
    odd = c_ref[0] == 1
    probs, plain, turned = [], [], []
    for h in range(2):
        scores = bias_ref[h].astype(F32)
        for n in range(4):
            scores += part_ref[n, h].astype(F32)
        masked = jnp.where(lane < span_ref[0], scores, -1e30)
        e = jnp.exp(masked - jnp.max(masked, axis=1, keepdims=True))
        probs.append((e / jnp.sum(e, axis=1, keepdims=True)).astype(BF))
        plain.append(scores)
        turned.append(pltpu.roll(scores, E, 1))
    for n in range(8):
        v = v_ref[n]
        o = jnp.where(
            low,
            jnp.dot(probs[0], v, preferred_element_type=F32),
            jnp.dot(probs[1], v, preferred_element_type=F32),
        )
        h, half = (n % 4) // 2, n % 2
        if n < 4:
            extra = turned[h] if half else plain[h]
            o = jnp.where(jnp.logical_and(low, odd), extra, o)
        else:
            extra = plain[h] if half else turned[h]
            o = jnp.where(jnp.logical_or(low, odd), o, extra)
        held[:, n, :] = o
    out_ref[...] = held[...].astype(BF)


def column_block(c_ref, bl_ref, stack_ref, who_ref, wv_ref, wvo_ref, pair_ref, cw_ref, out_ref, pair_out_ref):
    mine = c_ref[0]
    lane = lax.broadcasted_iota(jnp.int32, (L, L), 1)
    row = lax.broadcasted_iota(jnp.int32, (L, L), 0)
    low = lane < E
    early = lax.rem(row, 8) < 4

    def tile(pair, far):
        zl, yl, c = pair // 4, pair // 2 % 2, pair % 2
        both = bl_ref[c, far // 4 * 16 + zl * 8 + far % 4 * 2 + yl].astype(F32)
        return jnp.where(mine == 0, both[:8], both[8:])

    tiles = [[tile(pair, far) for far in range(16)] for pair in range(8)]
    blocks = [jnp.concatenate(t, axis=0) for t in tiles]
    parts = []
    for n in range(2):
        e0, o0, e1, o1 = blocks[4 * n : 4 * n + 4]
        ro0, re1 = pltpu.roll(o0, E, 1), pltpu.roll(e1, E, 1)
        parts.append(jnp.where(jnp.logical_or(low, early), e0, ro0))
        parts.append(jnp.where(low, ro0, re1))
        parts.append(jnp.where(jnp.logical_and(low, early), re1, o1))
    blended = jnp.concatenate(parts, axis=1).astype(BF)

    updated = (dot_nt(who_ref[...], blended) + stack_ref[...].astype(F32)).astype(BF).astype(F32)
    center = jnp.mean(updated, axis=0, keepdims=True)
    spread = jnp.mean(jnp.square(updated - center), axis=0, keepdims=True)
    normed = ((updated - center) * lax.rsqrt(spread + 1e-05)).astype(BF)
    packed = jnp.dot(wv_ref[...], normed, preferred_element_type=F32)

    mixed = []
    for h in range(H):
        q = (packed[E * h : E * h + E] * E**-0.5).astype(BF)
        k = packed[D + E * h : D + E * h + E].astype(BF)
        v = packed[2 * D + E * h : 2 * D + E * h + E].astype(BF)
        logits = dot_tn(k, q)
        e = jnp.exp(logits - jnp.max(logits, axis=0, keepdims=True))
        probs = (e / jnp.sum(e, axis=0, keepdims=True)).astype(BF)
        mixed.append(jnp.dot(v, probs, preferred_element_type=F32).astype(BF))
    mixed = jnp.concatenate(mixed, axis=0)

    result = (updated + jnp.dot(wvo_ref[...], mixed, preferred_element_type=F32)).astype(BF)
    place = (row // 32 * 32 + row // 4 % 4 * 8 + row // 16 % 2 * 4 + row % 4 == lane).astype(BF)
    out_ref[...] = dot_nt(place, result).astype(BF)

    one = lax.broadcasted_iota(jnp.int32, (1, L), 1) < E
    lines = []
    for n in range(4):
        e, o = tiles[2 * n][0], tiles[2 * n + 1][0]
        re, ro = pltpu.roll(e, E, 1), pltpu.roll(o, E, 1)
        lines.append(jnp.where(one, re[4:5], e[5:6]))
        lines.append(jnp.where(one, re[6:7], e[7:8]))
        lines.append(jnp.where(one, o[2:3], ro[3:4]))
    scores = jnp.concatenate(lines + [jnp.zeros((L - H, L), F32)], axis=0).T
    weights = jnp.concatenate([cw_ref[...].astype(F32), jnp.zeros((L - H, L), F32)], axis=0)
    pair = pair_ref[...].astype(F32) + jnp.dot(
        scores.astype(BF), weights.astype(BF), preferred_element_type=F32
    )
    pair_out_ref[...] = pair.astype(BF)


def swapped(x, axis):
    return lax.ppermute(x, axis, [(0, 1), (1, 0)])


def call(kernel, out_shape, *args, scalars=0, scratch=()):
    return pl.pallas_call(
        kernel,
        out_shape=out_shape,
        in_specs=[SMEM] * scalars + [VMEM] * (len(args) - scalars),
        out_specs=jax.tree.map(lambda _: VMEM, out_shape),
        scratch_shapes=scratch,
        compiler_params=params(),
    )(*args)


def like(*dims, dtype=BF):
    return jax.ShapeDtypeStruct(dims, dtype)


def per_device(stack, spans, pair, w_triple, w_out, v_triple, v_out, offsets, contact_w):
    zl, yl, c = (lax.axis_index(n).astype(jnp.int32) for n in ("zl", "yl", "c"))
    c1 = c[None]
    pair_own = pair.reshape(L, 128)
    own_row = stack.reshape(L, D)

    column_weights = jnp.concatenate([v_triple.T, v_out.T, w_out.T, jnp.zeros((2, D), BF)], axis=0)
    gathered = lax.all_gather(column_weights, ROWS, axis=0, tiled=False)

    normed = normalize(own_row.astype(F32)).astype(BF)
    near = jnp.concatenate([normed, swapped(normed, "yl")])
    far = swapped(near, "zl")

    bias = lax.dot_general(offsets, pair_own, (((0,), (1,)), ((), ())), preferred_element_type=F32).astype(BF)
    bias = jnp.pad(bias.reshape(4, 6, E), ((0, 0), (0, 12), (0, 0)))
    slices = jnp.pad(w_triple.T.reshape(18, 16, 48).transpose(1, 0, 2), ((0, 0), (0, 0), (0, 16)))
    front = jnp.concatenate(
        [
            jnp.broadcast_to(slices.reshape(4, 1, 4, 1, 18, E), (4, 2, 4, 2, 18, E)),
            jnp.broadcast_to(bias.reshape(1, 2, 1, 2, 18, E), (4, 2, 4, 2, 18, E)),
        ],
        axis=-1,
    ).reshape(64, 18, 128)
    message = jnp.concatenate([front, own_row.reshape(64, 12, 128), jnp.zeros((64, 2, 128), BF)], axis=1)
    came = lax.all_to_all(message, CHIPS, 0, 0, tiled=True)

    source = lax.broadcasted_iota(jnp.int32, (2048, 576), 0)
    target = lax.broadcasted_iota(jnp.int32, (2048, 576), 1)
    column = (source // 32 * 2 + c) * 18 + source % 32
    wanted = target // 192 * D + (2 * zl + yl) * 192 + target % 192
    pick = jnp.logical_and(column == wanted, source % 32 < 18).astype(BF)
    came, near, pick = lax.optimization_barrier((came, near, pick))
    picked = dot_tn(came.reshape(2048, 128), pick)[:48].astype(BF)
    picked = lax.all_gather(picked, "c", axis=0, tiled=False)
    copies = call(spread_columns, like(16, 48, 384), c1, picked, scalars=1)
    w_heads = lax.all_to_all(copies, FAR, 0, 0, tiled=True).reshape(D, 384)
    near = lax.all_gather(near.reshape(2, L, D), "c", axis=0, tiled=False)
    far = lax.all_gather(far.reshape(2, L, D), "c", axis=0, tiled=False)

    rest = lax.all_gather(came[:, :30], "c", axis=0, tiled=False)
    stack_own = rest[:, :, 18:].reshape(2, 64, 2, D)
    stack_own = lax.dynamic_index_in_dim(stack_own, c, 2, keepdims=False).reshape(2, 4, 2, 4, 2, D)
    stack_own = stack_own.transpose(1, 3, 2, 4, 0, 5).reshape(R, D).T
    bias_own = rest[:, :, :6, E:].reshape(2, 64, 3, L)
    bias_own = lax.dynamic_slice_in_dim(bias_own, c, 2, axis=2).transpose(2, 1, 0, 3).reshape(2, L, L)

    at = jnp.stack([zl, yl])
    tied, values = call(
        project_and_tie, (like(4, 2, L, L), like(8, L, 2 * E)), at, w_heads, near, far, scalars=1
    )
    parts = lax.all_to_all(tied, "zh", 0, 0, tiled=True)
    parts = call(add_four, like(4, 2, L, L), parts)
    parts = lax.all_to_all(parts, "yh", 0, 0, tiled=True)
    message = call(
        attend,
        like(L, 8, 2 * E),
        c1,
        spans,
        parts,
        bias_own,
        values,
        scalars=2,
        scratch=[pltpu.VMEM((L, 8, 2 * E), F32)],
    )
    came = lax.all_to_all(message.reshape(64, 16, 128), CHIPS, 0, 0, tiled=True)

    column_triple = gathered[:, :18].reshape(3 * D, D)
    column_out = gathered[:, 18:24].reshape(D, D)
    row_out = gathered[:, 24:30].reshape(D, D)
    came, column_triple, column_out, row_out = lax.optimization_barrier(
        (came, column_triple, column_out, row_out)
    )
    blended = lax.all_gather(came, "c", axis=0, tiled=False)

    alignment, pair_out = call(
        column_block,
        (like(R, D), like(L, 128)),
        c1,
        blended,
        stack_own,
        row_out,
        column_triple,
        column_out,
        pair_own,
        contact_w,
        scalars=1,
    )
    return alignment.reshape(R, 1, D), pair_out.reshape(1, L, 128)


def solution(mesh):
    torus = Mesh(mesh.devices.reshape(mesh.shape["aln"], 4, 2, 4, 2, 2), ALL)
    in_specs = (
        P(ALL, None, None),
        P("a"),
        P(ALL, None, None),
        P(None, ROWS),
        P(None, ROWS),
        P(None, ROWS),
        P(None, ROWS),
        P(),
        P(),
    )
    out_specs = (P("a", ROWS, None), P(ALL, None, None))
    return jax.shard_map(
        per_device, mesh=torus, in_specs=in_specs, out_specs=out_specs, check_vma=False
    )
```

```python
import jax
import jax.numpy as jnp
from jax import lax
from jax.experimental import pallas as pl
from jax.experimental.pallas import tpu as pltpu
from jax.sharding import Mesh
from jax.sharding import PartitionSpec as P

ROWS = ("z", "y", "c")
ALL = ("a",) + ROWS
CHIPS = ("z", "y")
D, H, E, L, R = 768, 12, 64, 128, 128
BF, F32 = jnp.bfloat16, jnp.float32
VMEM = pl.BlockSpec(memory_space=pltpu.VMEM)
SMEM = pl.BlockSpec(memory_space=pltpu.SMEM)


def params():
    return pltpu.CompilerParams(vmem_limit_bytes=48 << 20)


def dot_nt(a, b):
    return lax.dot_general(a, b, (((1,), (1,)), ((), ())), preferred_element_type=F32)


def dot_tn(a, b):
    return lax.dot_general(a, b, (((0,), (0,)), ((), ())), preferred_element_type=F32)


def normalize(x):
    center = jnp.mean(x, axis=-1, keepdims=True)
    spread = jnp.mean(jnp.square(x - center), axis=-1, keepdims=True)
    return (x - center) * lax.rsqrt(spread + 1e-05)


def first_head(y):
    return 3 * (y // 2) + y % 2


def spread_columns(at_ref, picked_ref, out_ref):
    both = picked_ref[0].astype(F32) + picked_ref[1].astype(F32)
    second = at_ref[1] == 1
    parts = [
        jnp.where(second, both[:, 128 * n + E : 128 * n + 128], both[:, 128 * n : 128 * n + E]) for n in range(3)
    ]
    mine = jnp.concatenate(parts, axis=1).astype(BF)
    for n in range(8):
        out_ref[n] = mine


def project_and_tie(at_ref, w_ref, own_ref, *refs):
    near_refs, far_ref, tied_ref, v_ref = refs[:3], refs[3], refs[4], refs[5]
    w = w_ref[...]
    low = lax.broadcasted_iota(jnp.int32, (L, 2 * E), 1) < E
    total = jnp.zeros((L, L), F32)

    def rows_of(offset):
        if offset == 0:
            return [own_ref[core] for core in range(2)]
        if abs(offset) < 4:
            return [near_refs[abs(offset) - 1][int(offset > 0), core] for core in range(2)]
        return [jnp.concatenate([far_ref[0, core], far_ref[1, core]], axis=0) for core in range(2)]

    for offset in (0, -1, 1, -2, 2, -3, 3, 4):
        values = []
        for x in rows_of(offset):
            packed = jnp.dot(x, w, preferred_element_type=F32)
            both = packed[:, : 2 * E]
            q = jnp.where(low, both * E**-0.5, 0.0).astype(BF)
            k = pltpu.roll(both, E, 1).astype(BF)
            total += dot_nt(q, k)
            values.append(packed[:, 2 * E :])
        v_ref[lax.rem(at_ref[0] + (8 + offset), 8)] = jnp.concatenate(values, axis=1).astype(BF)
    part = (total * R**-0.5).astype(BF)
    for n in range(8):
        tied_ref[n] = part


def attend(span_ref, part_ref, bias_ref, probs_ref, scores_ref):
    scores = bias_ref[...].astype(F32)
    for n in range(8):
        scores += part_ref[n].astype(F32)
    j = lax.broadcasted_iota(jnp.int32, (L, L), 1)
    masked = jnp.where(j < span_ref[0], scores, -1e30)
    e = jnp.exp(masked - jnp.max(masked, axis=1, keepdims=True))
    probs_ref[...] = (e / jnp.sum(e, axis=1, keepdims=True)).astype(BF)
    scores_ref[...] = scores.astype(BF)


def blend(at_ref, probs_ref, scores_ref, v_ref, out_ref, held):
    parity = lax.rem(at_ref[0], 2)
    even = jnp.logical_and(parity == 0, at_ref[1] == 1)
    odd = jnp.logical_and(parity == 1, at_ref[1] == 0)
    for n in range(8):
        o = jnp.dot(probs_ref[...], v_ref[n], preferred_element_type=F32)
        if n in (0, 1):
            o = jnp.where(odd, scores_ref[n].astype(F32), o)
        if n in (4, 5):
            o = jnp.where(even, scores_ref[n - 4].astype(F32), o)
        held[:, n, :] = o
    out_ref[...] = held[...].astype(BF)


def column_block(c_ref, bl_ref, stack_ref, who_ref, wv_ref, wvo_ref, pair_ref, cw_ref, out_ref, pair_out_ref):
    mine = c_ref[0]
    lane = lax.broadcasted_iota(jnp.int32, (L, L), 1)
    row = lax.broadcasted_iota(jnp.int32, (L, L), 0)
    low = lax.broadcasted_iota(jnp.int32, (E, L), 1) < E
    early = lax.rem(lax.broadcasted_iota(jnp.int32, (E, L), 0), 8) < 4

    def tile(y, c, z):
        both = bl_ref[c, z * 8 + y].astype(F32)
        return jnp.where(mine == 0, both[:8], both[8:])

    def block(y, c):
        return jnp.concatenate([tile(y, c, z) for z in range(8)], axis=0)

    heads = []
    for n in range(4):
        shared = jnp.where(early, block(2 * n, 1), block(2 * n + 1, 0))
        heads += [block(2 * n, 0), shared, block(2 * n + 1, 1)]
    parts = []
    for n in range(6):
        first, second = heads[2 * n], heads[2 * n + 1]
        top = jnp.where(low, first, pltpu.roll(second, E, 1))
        bottom = jnp.where(low, pltpu.roll(first, E, 1), second)
        parts.append(jnp.concatenate([top, bottom], axis=0))
    blended = jnp.concatenate(parts, axis=1).astype(BF)

    updated = (dot_nt(who_ref[...], blended) + stack_ref[...].astype(F32)).astype(BF).astype(F32)
    center = jnp.mean(updated, axis=0, keepdims=True)
    spread = jnp.mean(jnp.square(updated - center), axis=0, keepdims=True)
    normed = ((updated - center) * lax.rsqrt(spread + 1e-05)).astype(BF)
    packed = jnp.dot(wv_ref[...], normed, preferred_element_type=F32)

    mixed = []
    for h in range(H):
        q = (packed[E * h : E * h + E] * E**-0.5).astype(BF)
        k = packed[D + E * h : D + E * h + E].astype(BF)
        v = packed[2 * D + E * h : 2 * D + E * h + E].astype(BF)
        logits = dot_tn(k, q)
        e = jnp.exp(logits - jnp.max(logits, axis=0, keepdims=True))
        probs = (e / jnp.sum(e, axis=0, keepdims=True)).astype(BF)
        mixed.append(jnp.dot(v, probs, preferred_element_type=F32).astype(BF))
    mixed = jnp.concatenate(mixed, axis=0)

    result = (updated + jnp.dot(wvo_ref[...], mixed, preferred_element_type=F32)).astype(BF)
    place = (row % 2 * E + row // 2 == lane).astype(BF)
    out_ref[...] = dot_nt(place, result).astype(BF)

    lines = []
    for n in range(4):
        even, odd = tile(2 * n, 1, 0), tile(2 * n + 1, 0, 0)
        lines += [even[4:5], even[5:6], odd[1:2]]
    scores = jnp.concatenate(lines + [jnp.zeros((L - H, L), F32)], axis=0).T
    weights = jnp.concatenate([cw_ref[...].astype(F32), jnp.zeros((L - H, L), F32)], axis=0)
    pair = pair_ref[...].astype(F32) + jnp.dot(
        scores.astype(BF), weights.astype(BF), preferred_element_type=F32
    )
    pair_out_ref[...] = pair.astype(BF)


def around(x):
    pairs = [(2 * y + c, (y + 1 - 2 * c) % 8 * 2 + c) for y in range(8) for c in range(2)]
    return lax.ppermute(x, ("y", "c"), pairs)


def both_cores(x):
    return lax.all_gather(x, "c", axis=0, tiled=False)


def call(kernel, out_shape, *args, scalars=0, scratch=()):
    return pl.pallas_call(
        kernel,
        out_shape=out_shape,
        in_specs=[SMEM] * scalars + [VMEM] * (len(args) - scalars),
        out_specs=jax.tree.map(lambda _: VMEM, out_shape),
        scratch_shapes=scratch,
        compiler_params=params(),
    )(*args)


def like(*dims, dtype=BF):
    return jax.ShapeDtypeStruct(dims, dtype)


def per_device(stack, spans, pair, w_triple, w_out, v_triple, v_out, offsets, contact_w):
    y, c = lax.axis_index("y").astype(jnp.int32), lax.axis_index("c").astype(jnp.int32)
    at, c1 = jnp.stack([y, c]), c[None]
    pair_own = pair.reshape(L, 128)
    own_row = stack.reshape(L, D)

    column_weights = jnp.concatenate([v_triple.T, v_out.T, w_out.T, jnp.zeros((2, D), BF)], axis=0)
    gathered = lax.all_gather(column_weights, ROWS, axis=0, tiled=False)

    bias = lax.dot_general(offsets, pair_own, (((0,), (1,)), ((), ())), preferred_element_type=F32).astype(BF)
    bias_pairs = jnp.stack([bias[first_head(n) : first_head(n) + 2] for n in range(8)])
    slices = w_triple.T.reshape(18, 8, 96).transpose(1, 0, 2).reshape(8, 1, 18, 96)
    slices = jnp.pad(slices, ((0, 0), (0, 0), (0, 0), (0, 32)))
    message = jnp.concatenate(
        [
            jnp.broadcast_to(slices, (8, 8, 18, 128)).reshape(64, 18, 128),
            own_row.reshape(64, 12, 128),
            jnp.broadcast_to(bias_pairs[None], (8, 8, 2, 128)).reshape(64, 2, 128),
        ],
        axis=1,
    )
    came = lax.all_to_all(message, CHIPS, 0, 0, tiled=True)

    normed = normalize(own_row.astype(F32)).astype(BF)
    own = both_cores(normed)
    first = around(own)
    second = around(first)
    third = around(second)
    fourth = around(jnp.where(c == 0, third[:, : L // 2], third[:, L // 2 :]))

    source = lax.broadcasted_iota(jnp.int32, (2048, 384), 0)
    target = lax.broadcasted_iota(jnp.int32, (2048, 384), 1)
    column = (source // 32 * 2 + c) * 18 + source % 32
    wanted = target // 128 * D + first_head(y) * E + target % 128
    pick = jnp.logical_and(column == wanted, source % 32 < 18).astype(BF)
    came, second, pick = lax.optimization_barrier((came, second, pick))
    picked = both_cores(dot_tn(came.reshape(2048, 128), pick)[:96].astype(BF))
    copies = call(spread_columns, like(8, 96, 192), at, picked, scalars=1)
    w_head = lax.all_to_all(copies, "z", 0, 0, tiled=True).reshape(D, 192)

    rest = both_cores(came[:, 18:])
    stack_own = rest[:, :, :12].reshape(2, 64, 2, D)
    stack_own = lax.dynamic_index_in_dim(stack_own, c, 2, keepdims=False).reshape(R, D).T
    bias_own = lax.dynamic_index_in_dim(rest[:, :, 12:], c, 2, keepdims=False)
    bias_own = bias_own.transpose(1, 0, 2).reshape(L, L)

    tied, values = call(
        project_and_tie,
        (like(8, L, L), like(8, L, 2 * E)),
        at,
        w_head,
        own,
        both_cores(first),
        both_cores(second),
        both_cores(third),
        both_cores(fourth),
        scalars=1,
    )
    parts = lax.all_to_all(tied, "z", 0, 0, tiled=True)
    probs, scores = call(attend, (like(L, L), like(L, L)), spans, parts, bias_own, scalars=1)
    message = call(
        blend,
        like(L, 8, 2 * E),
        at,
        probs,
        both_cores(scores),
        values,
        scalars=1,
        scratch=[pltpu.VMEM((L, 8, 2 * E), F32)],
    )
    came = lax.all_to_all(message.reshape(64, 16, 128), CHIPS, 0, 0, tiled=True)

    column_triple = gathered[:, :18].reshape(3 * D, D)
    column_out = gathered[:, 18:24].reshape(D, D)
    row_out = gathered[:, 24:30].reshape(D, D)
    came, column_triple, column_out, row_out = lax.optimization_barrier(
        (came, column_triple, column_out, row_out)
    )
    blended = lax.all_gather(came, "c", axis=0, tiled=False)

    alignment, pair_out = call(
        column_block,
        (like(R, D), like(L, 128)),
        c1,
        blended,
        stack_own,
        row_out,
        column_triple,
        column_out,
        pair_own,
        contact_w,
        scalars=1,
    )
    return alignment.reshape(R, 1, D), pair_out.reshape(1, L, 128)


def solution(mesh):
    torus = Mesh(mesh.devices.reshape(mesh.shape["aln"], 8, 8, 2), ALL)
    in_specs = (
        P(ALL, None, None),
        P("a"),
        P(ALL, None, None),
        P(None, ROWS),
        P(None, ROWS),
        P(None, ROWS),
        P(None, ROWS),
        P(),
        P(),
    )
    out_specs = (P("a", ROWS, None), P(ALL, None, None))
    return jax.shard_map(
        per_device, mesh=torus, in_specs=in_specs, out_specs=out_specs, check_vma=False
    )
```

```python
import jax
import jax.numpy as jnp
from jax import lax
from jax.experimental import pallas as pl
from jax.experimental.pallas import tpu as pltpu
from jax.sharding import Mesh
from jax.sharding import PartitionSpec as P

ROWS = ("z", "y", "c")
ALL = ("a",) + ROWS
CHIPS = ("z", "y")
D, H, E, L, R = 768, 12, 64, 128, 128
BF, F32 = jnp.bfloat16, jnp.float32
VMEM = pl.BlockSpec(memory_space=pltpu.VMEM)
SMEM = pl.BlockSpec(memory_space=pltpu.SMEM)


def params():
    return pltpu.CompilerParams(vmem_limit_bytes=48 << 20)


def dot_nt(a, b):
    return lax.dot_general(a, b, (((1,), (1,)), ((), ())), preferred_element_type=F32)


def dot_tn(a, b):
    return lax.dot_general(a, b, (((0,), (0,)), ((), ())), preferred_element_type=F32)


def normalize(x):
    center = jnp.mean(x, axis=-1, keepdims=True)
    spread = jnp.mean(jnp.square(x - center), axis=-1, keepdims=True)
    return (x - center) * lax.rsqrt(spread + 1e-05)


def first_head(y):
    return 3 * (y // 2) + y % 2


def own_columns(at_ref, picked_ref, out_ref):
    both = picked_ref[0].astype(F32) + picked_ref[1].astype(F32)
    second = at_ref[1] == 1
    parts = [
        jnp.where(second, both[:, 128 * n + E : 128 * n + 128], both[:, 128 * n : 128 * n + E]) for n in range(3)
    ]
    out_ref[...] = jnp.concatenate(parts, axis=1).astype(BF)


def project_and_tie(at_ref, w_ref, own_ref, *refs):
    near_refs, far_ref, tied_ref, v_ref = refs[:3], refs[3], refs[4], refs[5]
    w = w_ref[...]
    low = lax.broadcasted_iota(jnp.int32, (L, 2 * E), 1) < E
    total = jnp.zeros((L, L), F32)

    def rows_of(offset):
        if offset == 0:
            return [own_ref[core] for core in range(2)]
        if abs(offset) < 4:
            return [near_refs[abs(offset) - 1][int(offset > 0), core] for core in range(2)]
        return [jnp.concatenate([far_ref[0, core], far_ref[1, core]], axis=0) for core in range(2)]

    for offset in (0, -1, 1, -2, 2, -3, 3, 4):
        values = []
        for x in rows_of(offset):
            packed = jnp.dot(x, w, preferred_element_type=F32)
            both = packed[:, : 2 * E]
            q = jnp.where(low, both * E**-0.5, 0.0).astype(BF)
            k = pltpu.roll(both, E, 1).astype(BF)
            total += dot_nt(q, k)
            values.append(packed[:, 2 * E :])
        v_ref[lax.rem(at_ref[0] + (8 + offset), 8)] = jnp.concatenate(values, axis=1).astype(BF)
    part = (total * R**-0.5).astype(BF)
    for n in range(8):
        tied_ref[n] = part


def attend(span_ref, part_ref, bias_ref, probs_ref, scores_ref):
    scores = bias_ref[...].astype(F32)
    for n in range(8):
        scores += part_ref[n].astype(F32)
    j = lax.broadcasted_iota(jnp.int32, (L, L), 1)
    masked = jnp.where(j < span_ref[0], scores, -1e30)
    e = jnp.exp(masked - jnp.max(masked, axis=1, keepdims=True))
    probs_ref[...] = (e / jnp.sum(e, axis=1, keepdims=True)).astype(BF)
    scores_ref[...] = scores.astype(BF)


def blend(at_ref, probs_ref, scores_ref, v_ref, out_ref, held):
    parity = lax.rem(at_ref[0], 2)
    even = jnp.logical_and(parity == 0, at_ref[1] == 1)
    odd = jnp.logical_and(parity == 1, at_ref[1] == 0)
    for n in range(8):
        o = jnp.dot(probs_ref[...], v_ref[n], preferred_element_type=F32)
        if n in (0, 1):
            o = jnp.where(odd, scores_ref[n].astype(F32), o)
        if n in (4, 5):
            o = jnp.where(even, scores_ref[n - 4].astype(F32), o)
        held[:, n, :] = o
    out_ref[...] = held[...].astype(BF)


def column_block(c_ref, bl_ref, stack_ref, who_ref, wv_ref, wvo_ref, pair_ref, cw_ref, out_ref, pair_out_ref):
    mine = c_ref[0]
    lane = lax.broadcasted_iota(jnp.int32, (L, L), 1)
    row = lax.broadcasted_iota(jnp.int32, (L, L), 0)
    low = lax.broadcasted_iota(jnp.int32, (E, L), 1) < E
    early = lax.rem(lax.broadcasted_iota(jnp.int32, (E, L), 0), 8) < 4

    def tile(y, c, z):
        both = bl_ref[c, z * 8 + y].astype(F32)
        return jnp.where(mine == 0, both[:8], both[8:])

    def block(y, c):
        return jnp.concatenate([tile(y, c, z) for z in range(8)], axis=0)

    heads = []
    for n in range(4):
        shared = jnp.where(early, block(2 * n, 1), block(2 * n + 1, 0))
        heads += [block(2 * n, 0), shared, block(2 * n + 1, 1)]
    parts = []
    for n in range(6):
        first, second = heads[2 * n], heads[2 * n + 1]
        top = jnp.where(low, first, pltpu.roll(second, E, 1))
        bottom = jnp.where(low, pltpu.roll(first, E, 1), second)
        parts.append(jnp.concatenate([top, bottom], axis=0))
    blended = jnp.concatenate(parts, axis=1).astype(BF)

    updated = (dot_nt(who_ref[...], blended) + stack_ref[...].astype(F32)).astype(BF).astype(F32)
    center = jnp.mean(updated, axis=0, keepdims=True)
    spread = jnp.mean(jnp.square(updated - center), axis=0, keepdims=True)
    normed = ((updated - center) * lax.rsqrt(spread + 1e-05)).astype(BF)
    packed = jnp.dot(wv_ref[...], normed, preferred_element_type=F32)

    mixed = []
    for h in range(H):
        q = (packed[E * h : E * h + E] * E**-0.5).astype(BF)
        k = packed[D + E * h : D + E * h + E].astype(BF)
        v = packed[2 * D + E * h : 2 * D + E * h + E].astype(BF)
        logits = dot_tn(k, q)
        e = jnp.exp(logits - jnp.max(logits, axis=0, keepdims=True))
        probs = (e / jnp.sum(e, axis=0, keepdims=True)).astype(BF)
        mixed.append(jnp.dot(v, probs, preferred_element_type=F32).astype(BF))
    mixed = jnp.concatenate(mixed, axis=0)

    result = (updated + jnp.dot(wvo_ref[...], mixed, preferred_element_type=F32)).astype(BF)
    place = (row % 2 * E + row // 2 == lane).astype(BF)
    out_ref[...] = dot_nt(place, result).astype(BF)

    lines = []
    for n in range(4):
        even, odd = tile(2 * n, 1, 0), tile(2 * n + 1, 0, 0)
        lines += [even[4:5], even[5:6], odd[1:2]]
    scores = jnp.concatenate(lines + [jnp.zeros((L - H, L), F32)], axis=0).T
    weights = jnp.concatenate([cw_ref[...].astype(F32), jnp.zeros((L - H, L), F32)], axis=0)
    pair = pair_ref[...].astype(F32) + jnp.dot(
        scores.astype(BF), weights.astype(BF), preferred_element_type=F32
    )
    pair_out_ref[...] = pair.astype(BF)


def around(x):
    pairs = [(2 * y + c, (y + 1 - 2 * c) % 8 * 2 + c) for y in range(8) for c in range(2)]
    return lax.ppermute(x, ("y", "c"), pairs)


def both_cores(x):
    return lax.all_gather(x, "c", axis=0, tiled=False)


def call(kernel, out_shape, *args, scalars=0, scratch=()):
    return pl.pallas_call(
        kernel,
        out_shape=out_shape,
        in_specs=[SMEM] * scalars + [VMEM] * (len(args) - scalars),
        out_specs=jax.tree.map(lambda _: VMEM, out_shape),
        scratch_shapes=scratch,
        compiler_params=params(),
    )(*args)


def like(*dims, dtype=BF):
    return jax.ShapeDtypeStruct(dims, dtype)


def per_device(stack, spans, pair, w_triple, w_out, v_triple, v_out, offsets, contact_w):
    y, c = lax.axis_index("y").astype(jnp.int32), lax.axis_index("c").astype(jnp.int32)
    at, c1 = jnp.stack([y, c]), c[None]
    pair_own = pair.reshape(L, 128)
    own_row = stack.reshape(L, D)

    column_weights = jnp.concatenate([v_triple.T, v_out.T, w_out.T, jnp.zeros((2, D), BF)], axis=0)
    gathered = lax.all_gather(column_weights, ROWS, axis=0, tiled=False)

    normed = normalize(own_row.astype(F32)).astype(BF)
    own = both_cores(normed)
    first = around(own)
    second = around(first)
    third = around(second)
    last = jnp.where(c == 0, third[:, : L // 2], third[:, L // 2 :])

    bias = lax.dot_general(offsets, pair_own, (((0,), (1,)), ((), ())), preferred_element_type=F32).astype(BF)
    bias_pairs = jnp.stack([bias[first_head(n) : first_head(n) + 2] for n in range(8)])
    quarter = lax.dynamic_slice_in_dim(w_triple, lax.axis_index("a") * 192, 192, axis=0).T
    tail = jnp.concatenate([quarter[:9, 128:], quarter[9:, 128:]], axis=1)
    quarter = jnp.concatenate([quarter[:, :128], tail], axis=0)
    message = jnp.concatenate(
        [
            jnp.broadcast_to(quarter, (64, 27, 128)),
            jnp.zeros((64, 5, 128), BF),
            own_row.reshape(64, 12, 128),
            jnp.broadcast_to(bias_pairs[None], (8, 8, 2, 128)).reshape(64, 2, 128),
            jnp.zeros((64, 2, 128), BF),
        ],
        axis=1,
    )
    message, own = lax.optimization_barrier((message, own))
    came = lax.all_to_all(message, CHIPS, 0, 0, tiled=True)

    def wanted_at(source_rows, columns):
        source = lax.broadcasted_iota(jnp.int32, (64 * source_rows, 384), 0)
        target = lax.broadcasted_iota(jnp.int32, (64 * source_rows, 384), 1)
        wanted = target // 128 * D + first_head(y) * E + target % 128
        low, high, start = columns
        inside = source % source_rows + start
        found = (source // source_rows * 2 + c) * 18 + inside == wanted
        return jnp.logical_and(found, jnp.logical_and(inside >= low, inside < high)).astype(BF)

    pick = [wanted_at(24, (0, 18, 0)), wanted_at(16, (0, 9, -2)), wanted_at(16, (9, 18, 7))]
    came, second, *pick = lax.optimization_barrier((came, second, *pick))
    front = dot_tn(came[:, :24].reshape(1536, 128), pick[0])
    back = came[:, 16:32].reshape(1024, 128)
    back = dot_tn(back, pick[1])[:E] + dot_tn(back, pick[2])[E:]
    picked = both_cores(jnp.concatenate([front, back], axis=0).astype(BF))
    picked, last = lax.optimization_barrier((picked, last))
    fourth = around(last)
    mine = call(own_columns, like(192, 192), at, picked, scalars=1)
    w_head = lax.all_gather(mine, "a", axis=0, tiled=True)

    rest = both_cores(came[:, 32:46])
    stack_own = rest[:, :, :12].reshape(2, 64, 2, D)
    stack_own = lax.dynamic_index_in_dim(stack_own, c, 2, keepdims=False).reshape(R, D).T
    bias_own = lax.dynamic_index_in_dim(rest[:, :, 12:], c, 2, keepdims=False)
    bias_own = bias_own.transpose(1, 0, 2).reshape(L, L)

    tied, values = call(
        project_and_tie,
        (like(8, L, L), like(8, L, 2 * E)),
        at,
        w_head,
        own,
        both_cores(first),
        both_cores(second),
        both_cores(third),
        both_cores(fourth),
        scalars=1,
    )
    parts = lax.all_to_all(tied, "z", 0, 0, tiled=True)
    probs, scores = call(attend, (like(L, L), like(L, L)), spans, parts, bias_own, scalars=1)
    message = call(
        blend,
        like(L, 8, 2 * E),
        at,
        probs,
        both_cores(scores),
        values,
        scalars=1,
        scratch=[pltpu.VMEM((L, 8, 2 * E), F32)],
    )
    came = lax.all_to_all(message.reshape(64, 16, 128), CHIPS, 0, 0, tiled=True)

    column_triple = gathered[:, :18].reshape(3 * D, D)
    column_out = gathered[:, 18:24].reshape(D, D)
    row_out = gathered[:, 24:30].reshape(D, D)
    came, column_triple, column_out, row_out = lax.optimization_barrier(
        (came, column_triple, column_out, row_out)
    )
    blended = lax.all_gather(came, "c", axis=0, tiled=False)

    alignment, pair_out = call(
        column_block,
        (like(R, D), like(L, 128)),
        c1,
        blended,
        stack_own,
        row_out,
        column_triple,
        column_out,
        pair_own,
        contact_w,
        scalars=1,
    )
    return alignment.reshape(R, 1, D), pair_out.reshape(1, L, 128)


def solution(mesh):
    torus = Mesh(mesh.devices.reshape(mesh.shape["aln"], 8, 8, 2), ALL)
    in_specs = (
        P(ALL, None, None),
        P("a"),
        P(ALL, None, None),
        P(None, ROWS),
        P(None, ROWS),
        P(None, ROWS),
        P(None, ROWS),
        P(),
        P(),
    )
    out_specs = (P("a", ROWS, None), P(ALL, None, None))
    return jax.shard_map(
        per_device, mesh=torus, in_specs=in_specs, out_specs=out_specs, check_vma=False
    )
```

```python
import jax
import jax.numpy as jnp
from jax import lax
from jax.experimental import pallas as pl
from jax.experimental.pallas import tpu as pltpu
from jax.sharding import Mesh
from jax.sharding import PartitionSpec as P

ALL = ("a", "z", "y", "c")
ROWS = ("z", "y", "c")
CHIPS = ("z", "y")
D, H, E, L, R = 768, 12, 64, 128, 128
BF, F32 = jnp.bfloat16, jnp.float32
VMEM = pl.BlockSpec(memory_space=pltpu.VMEM)
SMEM = pl.BlockSpec(memory_space=pltpu.SMEM)


def params():
    return pltpu.CompilerParams(vmem_limit_bytes=28 << 20)


def dot_nt(a, b):
    return lax.dot_general(a, b, (((1,), (1,)), ((), ())), preferred_element_type=F32)


def dot_tn(a, b):
    return lax.dot_general(a, b, (((0,), (0,)), ((), ())), preferred_element_type=F32)


def first_head(y):
    return 3 * (y // 2) + y % 2


def normalize(x):
    center = jnp.mean(x, axis=-1, keepdims=True)
    spread = jnp.mean(jnp.square(x - center), axis=-1, keepdims=True)
    return (x - center) * lax.rsqrt(spread + 1e-05)


def project_and_tie(at_ref, w_ref, own_ref, one_ref, two_ref, three_ref, four_ref, tied_ref, v_ref):
    w = w_ref[...]
    lane = lax.broadcasted_iota(jnp.int32, (L, 2 * E), 1)
    y, c = at_ref[0], at_ref[1]
    step = 2 * c - 1
    rows = [(own_ref, None, 0, c), (four_ref, None, 4, 1 - c)]
    for n, ref in enumerate((one_ref, two_ref, three_ref)):
        rows += [(ref, core, (n + 1) * step, core) for core in range(2)]
    tied = [jnp.zeros((L, L), F32), jnp.zeros((L, L), F32)]
    for ref, core, offset, source in rows:
        x = ref[...] if core is None else ref[core]
        packed = jnp.dot(x, w, preferred_element_type=F32)
        q = packed[:, : 2 * E] * E**-0.5
        k = packed[:, 2 * E : 4 * E].astype(BF)
        v_ref[2 * lax.rem(y + 8 + offset, 4) + source] = packed[:, 4 * E :].astype(BF)
        tied[0] += dot_nt(jnp.where(lane < E, q, 0.0).astype(BF), k)
        tied[1] += dot_nt(jnp.where(lane < E, 0.0, q).astype(BF), k)
    for h in range(2):
        tied_ref[h] = tied[h] * R**-0.5


def attend(span_ref, part_ref, bias_ref, out_ref):
    scores = bias_ref[...].astype(F32)
    for n in range(8):
        scores += part_ref[n].astype(F32)
    j = lax.broadcasted_iota(jnp.int32, (L, L), 1)
    masked = jnp.where(j < span_ref[0], scores, -1e30)
    e = jnp.exp(masked - jnp.max(masked, axis=1, keepdims=True))
    out_ref[0] = (e / jnp.sum(e, axis=1, keepdims=True)).astype(BF)
    out_ref[1] = scores.astype(BF)


def blend(y_ref, probs_ref, v_ref, out_ref, held):
    lane = lax.broadcasted_iota(jnp.int32, (L, 2 * E), 1)
    low = lane < E
    odd = lax.rem(y_ref[0], 2) == 1
    plain = [probs_ref[h, 1].astype(F32) for h in range(2)]
    moved = [pltpu.roll(s, E, 1) for s in plain]
    for n in range(8):
        v = v_ref[n]
        o = jnp.where(
            low,
            jnp.dot(probs_ref[0, 0], v, preferred_element_type=F32),
            jnp.dot(probs_ref[1, 0], v, preferred_element_type=F32),
        )
        h, half = (n % 4) // 2, n % 2
        if n < 4:
            extra = moved[h] if half else plain[h]
            o = jnp.where(jnp.logical_and(low, odd), extra, o)
        else:
            extra = plain[h] if half else moved[h]
            o = jnp.where(jnp.logical_or(low, odd), o, extra)
        held[:, n, :] = o
    out_ref[...] = held[...].astype(BF)


def column_block(c_ref, bl_ref, stack_ref, who_ref, wv_ref, wvo_ref, pair_ref, cw_ref, out_ref, pair_out_ref):
    mine = c_ref[0]
    lane = lax.broadcasted_iota(jnp.int32, (L, L), 1)
    row = lax.broadcasted_iota(jnp.int32, (L, L), 0)
    low = lane < E
    early = lax.rem(row, 8) < 4

    slot = lax.rem(lax.broadcasted_iota(jnp.int32, (E, L), 0), 8)

    def tile(c, z, y):
        both = bl_ref[c, z * 8 + y].astype(F32)
        return jnp.where(mine == 0, both[:8], both[8:])

    def block(y):
        left, right = (jnp.concatenate([tile(c, z, y) for z in range(8)], axis=0) for c in range(2))
        halves = []
        for high in range(2):
            from_left = jnp.zeros((E, L), jnp.bool_)
            for s in range(8):
                away = (4 * high + s // 2 - y) % 8
                if away > 4 or (away == 0 and s % 2 == 0) or (away == 4 and s % 2 == 1):
                    from_left = jnp.logical_or(from_left, slot == s)
            halves.append(jnp.where(from_left, left, right))
        return jnp.concatenate(halves, axis=0)

    blocks = [block(y) for y in range(8)]
    parts = []
    for n in range(2):
        e0, o0, e1, o1 = blocks[4 * n : 4 * n + 4]
        ro0, re1 = pltpu.roll(o0, E, 1), pltpu.roll(e1, E, 1)
        parts.append(jnp.where(jnp.logical_or(low, early), e0, ro0))
        parts.append(jnp.where(low, ro0, re1))
        parts.append(jnp.where(jnp.logical_and(low, early), re1, o1))
    blended = jnp.concatenate(parts, axis=1).astype(BF)

    updated = (dot_nt(who_ref[...], blended) + stack_ref[...].astype(F32)).astype(BF).astype(F32)
    center = jnp.mean(updated, axis=0, keepdims=True)
    spread = jnp.mean(jnp.square(updated - center), axis=0, keepdims=True)
    normed = ((updated - center) * lax.rsqrt(spread + 1e-05)).astype(BF)
    packed = jnp.dot(wv_ref[...], normed, preferred_element_type=F32)

    mixed = []
    for h in range(H):
        q = (packed[E * h : E * h + E] * E**-0.5).astype(BF)
        k = packed[D + E * h : D + E * h + E].astype(BF)
        v = packed[2 * D + E * h : 2 * D + E * h + E].astype(BF)
        logits = dot_tn(k, q)
        e = jnp.exp(logits - jnp.max(logits, axis=0, keepdims=True))
        probs = (e / jnp.sum(e, axis=0, keepdims=True)).astype(BF)
        mixed.append(jnp.dot(v, probs, preferred_element_type=F32).astype(BF))
    mixed = jnp.concatenate(mixed, axis=0)

    result = (updated + jnp.dot(wvo_ref[...], mixed, preferred_element_type=F32)).astype(BF)
    place = (row // 8 % 2 * E + row // 16 * 8 + row % 8 == lane).astype(BF)
    out_ref[...] = dot_nt(place, result).astype(BF)

    one = lax.broadcasted_iota(jnp.int32, (1, L), 1) < E
    lines = []
    for n in range(4):
        e, o = tile(0, 0, 2 * n), tile(0, 0, 2 * n + 1)
        re, ro = pltpu.roll(e, E, 1), pltpu.roll(o, E, 1)
        lines.append(jnp.where(one, re[4:5], e[5:6]))
        lines.append(jnp.where(one, re[6:7], e[7:8]))
        lines.append(jnp.where(one, o[2:3], ro[3:4]))
    scores = jnp.concatenate(lines + [jnp.zeros((L - H, L), F32)], axis=0).T
    weights = jnp.concatenate([cw_ref[...].astype(F32), jnp.zeros((L - H, L), F32)], axis=0)
    pair = pair_ref[...].astype(F32) + jnp.dot(
        scores.astype(BF), weights.astype(BF), preferred_element_type=F32
    )
    pair_out_ref[...] = pair.astype(BF)


def around(x):
    pairs = [(2 * y + c, (y + 1 - 2 * c) % 8 * 2 + c) for y in range(8) for c in range(2)]
    return lax.ppermute(x, ("y", "c"), pairs)


def per_device(stack, spans, pair, w_triple, w_out, v_triple, v_out, offsets, contact_w):
    y, c = lax.axis_index("y"), lax.axis_index("c")
    y1, c1 = y[None].astype(jnp.int32), c[None].astype(jnp.int32)
    at = jnp.concatenate([y1, c1])
    pair_own = pair.reshape(L, 128)
    own_row = stack.reshape(L, D)

    column_weights = jnp.concatenate([v_triple.T, v_out.T, w_out.T, jnp.zeros((2, D), BF)], axis=0)
    gathered = lax.all_gather(column_weights, ROWS, axis=0, tiled=False)

    normed = normalize(own_row.astype(F32)).astype(BF)
    one = around(lax.all_gather(normed, "c", axis=0, tiled=False))
    two = around(one)
    three = around(two)
    four = around(jnp.where(c == 0, three[1], three[0]))

    bias = lax.dot_general(offsets, pair_own, (((0,), (1,)), ((), ())), preferred_element_type=F32).astype(BF)
    bias_pairs = jnp.stack([bias[first_head(n) : first_head(n) + 2] for n in range(8)])
    slices = w_triple.T.reshape(18, 2, 8, 48).transpose(2, 0, 1, 3).reshape(8, 1, 18, 96)
    slices = jnp.pad(slices, ((0, 0), (0, 0), (0, 0), (0, 32)))
    message = jnp.concatenate(
        [
            jnp.broadcast_to(slices, (8, 8, 18, 128)).reshape(64, 18, 128),
            own_row.reshape(64, 12, 128),
            jnp.broadcast_to(bias_pairs[None], (8, 8, 2, 128)).reshape(64, 2, 128),
        ],
        axis=1,
    )
    came = lax.all_to_all(message, CHIPS, 0, 0, tiled=True)
    came, one = lax.optimization_barrier((came, one))

    source = lax.broadcasted_iota(jnp.int32, (2048, 384), 0)
    target = lax.broadcasted_iota(jnp.int32, (2048, 384), 1)
    column = (source // 32 * 2 + c) * 18 + source % 32
    wanted = target // 128 * D + first_head(y) * E + target % 128
    pick = jnp.logical_and(column == wanted, source % 32 < 18).astype(BF)
    picked = dot_tn(came.reshape(2048, 128), pick)[:96].astype(BF)
    picked = lax.all_gather(picked, "c", axis=0, tiled=False)
    half = lax.dynamic_slice_in_dim(picked, c * 48, 48, axis=1)
    half = half[0] + half[1]
    over_z = lax.all_to_all(jnp.broadcast_to(half, (8, 48, 384)), "z", 0, 0, tiled=True)
    w_heads = lax.all_gather(over_z, "c", axis=0, tiled=False).reshape(D, 384)

    rest = lax.all_gather(came[:, 18:, :], "c", axis=0, tiled=False)
    stack_own = rest[:, :, :12].reshape(2, 64, 2, D)
    stack_own = lax.dynamic_index_in_dim(stack_own, c, 2, keepdims=False).reshape(2, 8, 2, 4, D)
    stack_own = stack_own.transpose(2, 1, 3, 0, 4).reshape(R, D)
    bias_own = lax.dynamic_index_in_dim(rest[:, :, 12:], c, 2, keepdims=False)
    bias_own = bias_own.transpose(1, 0, 2).reshape(L, L)

    tied, values = pl.pallas_call(
        project_and_tie,
        out_shape=(
            jax.ShapeDtypeStruct((2, L, L), F32),
            jax.ShapeDtypeStruct((8, L, 2 * E), BF),
        ),
        in_specs=[SMEM] + [VMEM] * 6,
        out_specs=(VMEM, VMEM),
        compiler_params=params(),
    )(at, w_heads, normed, one, two, three, four)

    tied = lax.all_gather(tied, "c", axis=0, tiled=False)
    tied = lax.dynamic_index_in_dim(tied, c, 1, keepdims=False)
    tied = (tied[0] + tied[1]).astype(BF)
    parts = lax.all_to_all(jnp.broadcast_to(tied, (8, L, L)), "z", 0, 0, tiled=True)
    head = pl.pallas_call(
        attend,
        out_shape=jax.ShapeDtypeStruct((2, L, L), BF),
        in_specs=[SMEM, VMEM, VMEM],
        out_specs=VMEM,
        compiler_params=params(),
    )(spans, parts, bias_own)
    heads = lax.all_gather(head, "c", axis=0, tiled=False)
    message = pl.pallas_call(
        blend,
        out_shape=jax.ShapeDtypeStruct((L, 8, 2 * E), BF),
        in_specs=[SMEM, VMEM, VMEM],
        out_specs=VMEM,
        scratch_shapes=[pltpu.VMEM((L, 8, 2 * E), F32)],
        compiler_params=params(),
    )(y1, heads, values)
    came = lax.all_to_all(message.reshape(64, 16, 128), CHIPS, 0, 0, tiled=True)
    column_triple = gathered[:, :18].reshape(3 * D, D)
    column_out = gathered[:, 18:24].reshape(D, D)
    row_out = gathered[:, 24:30].reshape(D, D)
    came, column_triple, column_out, row_out = lax.optimization_barrier(
        (came, column_triple, column_out, row_out)
    )
    blended = lax.all_gather(came, "c", axis=0, tiled=False)

    alignment, pair_out = pl.pallas_call(
        column_block,
        out_shape=(jax.ShapeDtypeStruct((R, D), BF), jax.ShapeDtypeStruct((L, 128), BF)),
        in_specs=[SMEM] + [VMEM] * 7,
        out_specs=(VMEM, VMEM),
        compiler_params=params(),
    )(c1, blended, stack_own.T, row_out, column_triple, column_out, pair_own, contact_w)
    return alignment.reshape(R, 1, D), pair_out.reshape(1, L, 128)


def solution(mesh):
    torus = Mesh(mesh.devices.reshape(mesh.shape["aln"], 8, 8, 2), ALL)
    in_specs = (
        P(ALL, None, None),
        P("a"),
        P(ALL, None, None),
        P(None, ROWS),
        P(None, ROWS),
        P(None, ROWS),
        P(None, ROWS),
        P(),
        P(),
    )
    out_specs = (P("a", ROWS, None), P(ALL, None, None))
    return jax.shard_map(
        per_device, mesh=torus, in_specs=in_specs, out_specs=out_specs, check_vma=False
    )
```

```python
import jax
import jax.numpy as jnp
from jax import lax
from jax.experimental import pallas as pl
from jax.experimental.pallas import tpu as pltpu
from jax.sharding import Mesh
from jax.sharding import PartitionSpec as P

ALL = ("a", "z", "y", "c")
ROWS = ("z", "y", "c")
CHIPS = ("z", "y")
D, H, E, L, R = 768, 12, 64, 128, 128
BF, F32 = jnp.bfloat16, jnp.float32
VMEM = pl.BlockSpec(memory_space=pltpu.VMEM)
SMEM = pl.BlockSpec(memory_space=pltpu.SMEM)


def params(mib=16):
    return pltpu.CompilerParams(vmem_limit_bytes=mib << 20)


ANY = pl.BlockSpec(memory_space=pl.ANY)


def dot_nt(a, b):
    return lax.dot_general(a, b, (((1,), (1,)), ((), ())), preferred_element_type=F32)


def dot_tn(a, b):
    return lax.dot_general(a, b, (((0,), (0,)), ((), ())), preferred_element_type=F32)


def first_head(y):
    return 3 * (y // 2) + y % 2


def normalize(x):
    center = jnp.mean(x, axis=-1, keepdims=True)
    spread = jnp.mean(jnp.square(x - center), axis=-1, keepdims=True)
    return (x - center) * lax.rsqrt(spread + 1e-05)


def project_and_tie(at_ref, w_ref, own_ref, one_ref, two_ref, three_ref, four_ref, tied_ref, v_ref):
    w = w_ref[...]
    lane = lax.broadcasted_iota(jnp.int32, (L, 2 * E), 1)
    y, c = at_ref[0], at_ref[1]
    step = 2 * c - 1
    rows = [(own_ref, None, 0, c), (four_ref, None, 4, 1 - c)]
    for n, ref in enumerate((one_ref, two_ref, three_ref)):
        rows += [(ref, core, (n + 1) * step, core) for core in range(2)]
    tied = [jnp.zeros((L, L), F32), jnp.zeros((L, L), F32)]
    for ref, core, offset, source in rows:
        x = ref[...] if core is None else ref[core]
        packed = jnp.dot(x, w, preferred_element_type=F32)
        q = packed[:, : 2 * E] * E**-0.5
        k = packed[:, 2 * E : 4 * E].astype(BF)
        v_ref[2 * lax.rem(y + 8 + offset, 4) + source] = packed[:, 4 * E :].astype(BF)
        tied[0] += dot_nt(jnp.where(lane < E, q, 0.0).astype(BF), k)
        tied[1] += dot_nt(jnp.where(lane < E, 0.0, q).astype(BF), k)
    for h in range(2):
        tied_ref[h] = tied[h] * R**-0.5


def attend(span_ref, part_ref, bias_ref, out_ref):
    scores = bias_ref[...].astype(F32)
    for n in range(8):
        scores += part_ref[n].astype(F32)
    j = lax.broadcasted_iota(jnp.int32, (L, L), 1)
    masked = jnp.where(j < span_ref[0], scores, -1e30)
    e = jnp.exp(masked - jnp.max(masked, axis=1, keepdims=True))
    out_ref[0] = (e / jnp.sum(e, axis=1, keepdims=True)).astype(BF)
    out_ref[1] = scores.astype(BF)


def blend(y_ref, probs_ref, v_ref, out_ref, held):
    lane = lax.broadcasted_iota(jnp.int32, (L, 2 * E), 1)
    low = lane < E
    odd = lax.rem(y_ref[0], 2) == 1
    plain = [probs_ref[h, 1].astype(F32) for h in range(2)]
    moved = [pltpu.roll(s, E, 1) for s in plain]
    for n in range(8):
        v = v_ref[n]
        o = jnp.where(
            low,
            jnp.dot(probs_ref[0, 0], v, preferred_element_type=F32),
            jnp.dot(probs_ref[1, 0], v, preferred_element_type=F32),
        )
        h, half = (n % 4) // 2, n % 2
        if n < 4:
            extra = moved[h] if half else plain[h]
            o = jnp.where(jnp.logical_and(low, odd), extra, o)
        else:
            extra = plain[h] if half else moved[h]
            o = jnp.where(jnp.logical_or(low, odd), o, extra)
        held[:, n, :] = o
    out_ref[...] = held[...].astype(BF)


def column_block(c_ref, bl_ref, *refs):
    far_refs, (out_ref, pair_out_ref), held, sems = refs[:6], refs[6:8], refs[8:14], refs[14]
    copies = [pltpu.make_async_copy(far_refs[n], held[n], sems.at[n]) for n in range(6)]
    for copy in copies:
        copy.start()
    stack_ref, who_ref, wv_ref, wvo_ref, pair_ref, cw_ref = held
    mine = c_ref[0]
    lane = lax.broadcasted_iota(jnp.int32, (L, L), 1)
    row = lax.broadcasted_iota(jnp.int32, (L, L), 0)
    low = lane < E
    early = lax.rem(row, 8) < 4

    slot = lax.rem(lax.broadcasted_iota(jnp.int32, (E, L), 0), 8)

    def tile(c, z, y):
        both = bl_ref[c, z * 8 + y].astype(F32)
        return jnp.where(mine == 0, both[:8], both[8:])

    def block(y):
        left, right = (jnp.concatenate([tile(c, z, y) for z in range(8)], axis=0) for c in range(2))
        halves = []
        for high in range(2):
            from_left = jnp.zeros((E, L), jnp.bool_)
            for s in range(8):
                away = (4 * high + s // 2 - y) % 8
                if away > 4 or (away == 0 and s % 2 == 0) or (away == 4 and s % 2 == 1):
                    from_left = jnp.logical_or(from_left, slot == s)
            halves.append(jnp.where(from_left, left, right))
        return jnp.concatenate(halves, axis=0)

    blocks = [block(y) for y in range(8)]
    parts = []
    for n in range(2):
        e0, o0, e1, o1 = blocks[4 * n : 4 * n + 4]
        ro0, re1 = pltpu.roll(o0, E, 1), pltpu.roll(e1, E, 1)
        parts.append(jnp.where(jnp.logical_or(low, early), e0, ro0))
        parts.append(jnp.where(low, ro0, re1))
        parts.append(jnp.where(jnp.logical_and(low, early), re1, o1))
    blended = jnp.concatenate(parts, axis=1).astype(BF)

    copies[0].wait()
    copies[1].wait()
    updated = (dot_nt(who_ref[...], blended) + stack_ref[...].astype(F32)).astype(BF).astype(F32)
    center = jnp.mean(updated, axis=0, keepdims=True)
    spread = jnp.mean(jnp.square(updated - center), axis=0, keepdims=True)
    normed = ((updated - center) * lax.rsqrt(spread + 1e-05)).astype(BF)
    copies[2].wait()
    packed = jnp.dot(wv_ref[...], normed, preferred_element_type=F32)

    mixed = []
    for h in range(H):
        q = (packed[E * h : E * h + E] * E**-0.5).astype(BF)
        k = packed[D + E * h : D + E * h + E].astype(BF)
        v = packed[2 * D + E * h : 2 * D + E * h + E].astype(BF)
        logits = dot_tn(k, q)
        e = jnp.exp(logits - jnp.max(logits, axis=0, keepdims=True))
        probs = (e / jnp.sum(e, axis=0, keepdims=True)).astype(BF)
        mixed.append(jnp.dot(v, probs, preferred_element_type=F32).astype(BF))
    mixed = jnp.concatenate(mixed, axis=0)

    copies[3].wait()
    result = (updated + jnp.dot(wvo_ref[...], mixed, preferred_element_type=F32)).astype(BF)
    place = (row // 8 % 2 * E + row // 16 * 8 + row % 8 == lane).astype(BF)
    out_ref[...] = dot_nt(place, result).astype(BF)

    one = lax.broadcasted_iota(jnp.int32, (1, L), 1) < E
    lines = []
    for n in range(4):
        e, o = tile(0, 0, 2 * n), tile(0, 0, 2 * n + 1)
        re, ro = pltpu.roll(e, E, 1), pltpu.roll(o, E, 1)
        lines.append(jnp.where(one, re[4:5], e[5:6]))
        lines.append(jnp.where(one, re[6:7], e[7:8]))
        lines.append(jnp.where(one, o[2:3], ro[3:4]))
    copies[4].wait()
    copies[5].wait()
    scores = jnp.concatenate(lines + [jnp.zeros((L - H, L), F32)], axis=0).T
    weights = jnp.concatenate([cw_ref[...].astype(F32), jnp.zeros((L - H, L), F32)], axis=0)
    pair = pair_ref[...].astype(F32) + jnp.dot(
        scores.astype(BF), weights.astype(BF), preferred_element_type=F32
    )
    pair_out_ref[...] = pair.astype(BF)


def around(x):
    pairs = [(2 * y + c, (y + 1 - 2 * c) % 8 * 2 + c) for y in range(8) for c in range(2)]
    return lax.ppermute(x, ("y", "c"), pairs)


def per_device(stack, spans, pair, w_triple, w_out, v_triple, v_out, offsets, contact_w):
    y, c = lax.axis_index("y"), lax.axis_index("c")
    y1, c1 = y[None].astype(jnp.int32), c[None].astype(jnp.int32)
    at = jnp.concatenate([y1, c1])
    pair_own = pair.reshape(L, 128)
    own_row = stack.reshape(L, D)

    column_weights = jnp.concatenate([v_triple.T, v_out.T, w_out.T, jnp.zeros((2, D), BF)], axis=0)
    gathered = lax.all_gather(column_weights, ROWS, axis=0, tiled=False)

    normed = normalize(own_row.astype(F32)).astype(BF)
    one = around(lax.all_gather(normed, "c", axis=0, tiled=False))
    two = around(one)

    bias = lax.dot_general(offsets, pair_own, (((0,), (1,)), ((), ())), preferred_element_type=F32).astype(BF)
    bias_pairs = jnp.stack([bias[first_head(n) : first_head(n) + 2] for n in range(8)])
    slices = w_triple.T.reshape(18, 2, 8, 48).transpose(2, 0, 1, 3).reshape(8, 1, 18, 96)
    slices = jnp.pad(slices, ((0, 0), (0, 0), (0, 0), (0, 32)))
    message = jnp.concatenate(
        [
            jnp.broadcast_to(slices, (8, 8, 18, 128)).reshape(64, 18, 128),
            own_row.reshape(64, 12, 128),
            jnp.broadcast_to(bias_pairs[None], (8, 8, 2, 128)).reshape(64, 2, 128),
        ],
        axis=1,
    )
    came = lax.all_to_all(message, CHIPS, 0, 0, tiled=True)
    source = lax.broadcasted_iota(jnp.int32, (2048, 384), 0)
    target = lax.broadcasted_iota(jnp.int32, (2048, 384), 1)
    column = (source // 32 * 2 + c) * 18 + source % 32
    wanted = target // 128 * D + first_head(y) * E + target % 128
    pick = jnp.logical_and(column == wanted, source % 32 < 18).astype(BF)
    came, one, pick = lax.optimization_barrier((came, one, pick))
    picked = dot_tn(came.reshape(2048, 128), pick)[:96].astype(BF)
    picked = lax.all_gather(picked, "c", axis=0, tiled=False)
    half = lax.dynamic_slice_in_dim(picked, c * 48, 48, axis=1)
    half, two = lax.optimization_barrier((half[0] + half[1], two))
    three = around(two)
    four = around(jnp.where(c == 0, three[1], three[0]))
    over_z = lax.all_to_all(jnp.broadcast_to(half, (8, 48, 384)), "z", 0, 0, tiled=True)
    w_heads = lax.all_gather(over_z, "c", axis=0, tiled=False).reshape(D, 384)

    rest = lax.all_gather(came[:, 18:, :], "c", axis=0, tiled=False)
    stack_own = rest[:, :, :12].reshape(2, 64, 2, D)
    stack_own = lax.dynamic_index_in_dim(stack_own, c, 2, keepdims=False).reshape(2, 8, 2, 4, D)
    stack_own = stack_own.transpose(2, 1, 3, 0, 4).reshape(R, D)
    bias_own = lax.dynamic_index_in_dim(rest[:, :, 12:], c, 2, keepdims=False)
    bias_own = bias_own.transpose(1, 0, 2).reshape(L, L)

    tied, values = pl.pallas_call(
        project_and_tie,
        out_shape=(
            jax.ShapeDtypeStruct((2, L, L), F32),
            jax.ShapeDtypeStruct((8, L, 2 * E), BF),
        ),
        in_specs=[SMEM] + [VMEM] * 6,
        out_specs=(VMEM, VMEM),
        compiler_params=params(),
    )(at, w_heads, normed, one, two, three, four)

    tied = lax.all_gather(tied, "c", axis=0, tiled=False)
    tied = lax.dynamic_index_in_dim(tied, c, 1, keepdims=False)
    tied = (tied[0] + tied[1]).astype(BF)
    parts = lax.all_to_all(jnp.broadcast_to(tied, (8, L, L)), "z", 0, 0, tiled=True)
    head = pl.pallas_call(
        attend,
        out_shape=jax.ShapeDtypeStruct((2, L, L), BF),
        in_specs=[SMEM, VMEM, VMEM],
        out_specs=VMEM,
        compiler_params=params(),
    )(spans, parts, bias_own)
    heads = lax.all_gather(head, "c", axis=0, tiled=False)
    message = pl.pallas_call(
        blend,
        out_shape=jax.ShapeDtypeStruct((L, 8, 2 * E), BF),
        in_specs=[SMEM, VMEM, VMEM],
        out_specs=VMEM,
        scratch_shapes=[pltpu.VMEM((L, 8, 2 * E), F32)],
        compiler_params=params(),
    )(y1, heads, values)
    came = lax.all_to_all(message.reshape(64, 16, 128), CHIPS, 0, 0, tiled=True)
    column_triple = gathered[:, :18].reshape(3 * D, D)
    column_out = gathered[:, 18:24].reshape(D, D)
    row_out = gathered[:, 24:30].reshape(D, D)
    came, column_triple, column_out, row_out = lax.optimization_barrier(
        (came, column_triple, column_out, row_out)
    )
    blended = lax.all_gather(came, "c", axis=0, tiled=False)

    alignment, pair_out = pl.pallas_call(
        column_block,
        out_shape=(jax.ShapeDtypeStruct((R, D), BF), jax.ShapeDtypeStruct((L, 128), BF)),
        in_specs=[SMEM, VMEM] + [ANY] * 6,
        out_specs=(VMEM, VMEM),
        scratch_shapes=[
            pltpu.VMEM((D, R), BF),
            pltpu.VMEM((D, D), BF),
            pltpu.VMEM((3 * D, D), BF),
            pltpu.VMEM((D, D), BF),
            pltpu.VMEM((L, 128), BF),
            pltpu.VMEM((H, 128), BF),
            pltpu.SemaphoreType.DMA((6,)),
        ],
        compiler_params=params(56),
    )(c1, blended, stack_own.T, row_out, column_triple, column_out, pair_own, contact_w)
    return alignment.reshape(R, 1, D), pair_out.reshape(1, L, 128)


def solution(mesh):
    torus = Mesh(mesh.devices.reshape(mesh.shape["aln"], 8, 8, 2), ALL)
    in_specs = (
        P(ALL, None, None),
        P("a"),
        P(ALL, None, None),
        P(None, ROWS),
        P(None, ROWS),
        P(None, ROWS),
        P(None, ROWS),
        P(),
        P(),
    )
    out_specs = (P("a", ROWS, None), P(ALL, None, None))
    return jax.shard_map(
        per_device, mesh=torus, in_specs=in_specs, out_specs=out_specs, check_vma=False
    )
```

```python
import jax
import jax.numpy as jnp
from jax import lax
from jax.experimental import pallas as pl
from jax.experimental.pallas import tpu as pltpu
from jax.sharding import Mesh
from jax.sharding import PartitionSpec as P

ALL = ("a", "z", "y", "c")
ROWS = ("z", "y", "c")
CHIPS = ("z", "y")
D, H, E, L, R = 768, 12, 64, 128, 128
BF, F32 = jnp.bfloat16, jnp.float32
VMEM = pl.BlockSpec(memory_space=pltpu.VMEM)
SMEM = pl.BlockSpec(memory_space=pltpu.SMEM)
ANY = pl.BlockSpec(memory_space=pl.ANY)


def params(mib=16):
    return pltpu.CompilerParams(vmem_limit_bytes=mib << 20)


def dot_nt(a, b):
    return lax.dot_general(a, b, (((1,), (1,)), ((), ())), preferred_element_type=F32)


def dot_tn(a, b):
    return lax.dot_general(a, b, (((0,), (0,)), ((), ())), preferred_element_type=F32)


def first_head(y):
    return 3 * (y // 2) + y % 2


def normalize(x):
    center = jnp.mean(x, axis=-1, keepdims=True)
    spread = jnp.mean(jnp.square(x - center), axis=-1, keepdims=True)
    return (x - center) * lax.rsqrt(spread + 1e-05)


def project_and_tie(at_ref, w_ref, own_ref, one_ref, two_ref, three_ref, four_ref, tied_ref, v_ref):
    w = w_ref[...]
    lane = lax.broadcasted_iota(jnp.int32, (L, 2 * E), 1)
    y, c = at_ref[0], at_ref[1]
    step = 2 * c - 1
    rows = [(own_ref, None, 0, c), (four_ref, None, 4, 1 - c)]
    for n, ref in enumerate((one_ref, two_ref, three_ref)):
        rows += [(ref, core, (n + 1) * step, core) for core in range(2)]
    tied = [jnp.zeros((L, L), F32), jnp.zeros((L, L), F32)]
    for ref, core, offset, source in rows:
        x = ref[...] if core is None else ref[core]
        packed = jnp.dot(x, w, preferred_element_type=F32)
        q = packed[:, : 2 * E] * E**-0.5
        k = packed[:, 2 * E : 4 * E].astype(BF)
        v_ref[2 * lax.rem(y + 8 + offset, 4) + source] = packed[:, 4 * E :].astype(BF)
        tied[0] += dot_nt(jnp.where(lane < E, q, 0.0).astype(BF), k)
        tied[1] += dot_nt(jnp.where(lane < E, 0.0, q).astype(BF), k)
    for h in range(2):
        tied_ref[h] = tied[h] * R**-0.5


def attend(span_ref, part_ref, bias_ref, out_ref):
    scores = bias_ref[...].astype(F32)
    for n in range(8):
        scores += part_ref[n].astype(F32)
    j = lax.broadcasted_iota(jnp.int32, (L, L), 1)
    masked = jnp.where(j < span_ref[0], scores, -1e30)
    e = jnp.exp(masked - jnp.max(masked, axis=1, keepdims=True))
    out_ref[0] = (e / jnp.sum(e, axis=1, keepdims=True)).astype(BF)
    out_ref[1] = scores.astype(BF)


def blend(y_ref, probs_ref, v_ref, out_ref, held):
    lane = lax.broadcasted_iota(jnp.int32, (L, 2 * E), 1)
    low = lane < E
    odd = lax.rem(y_ref[0], 2) == 1
    plain = [probs_ref[h, 1].astype(F32) for h in range(2)]
    moved = [pltpu.roll(s, E, 1) for s in plain]
    for n in range(8):
        v = v_ref[n]
        o = jnp.where(
            low,
            jnp.dot(probs_ref[0, 0], v, preferred_element_type=F32),
            jnp.dot(probs_ref[1, 0], v, preferred_element_type=F32),
        )
        h, half = (n % 4) // 2, n % 2
        if n < 4:
            extra = moved[h] if half else plain[h]
            o = jnp.where(jnp.logical_and(low, odd), extra, o)
        else:
            extra = plain[h] if half else moved[h]
            o = jnp.where(jnp.logical_or(low, odd), o, extra)
        held[:, n, :] = o
    out_ref[...] = held[...].astype(BF)


def column_block(
    c_ref, bl_ref, stack_ref, who_ref, far_ref, wvo_ref, pair_ref, cw_ref, out_ref, pair_out_ref, wv_ref, sem
):
    copy = pltpu.make_async_copy(far_ref, wv_ref, sem)
    copy.start()
    mine = c_ref[0]
    lane = lax.broadcasted_iota(jnp.int32, (L, L), 1)
    row = lax.broadcasted_iota(jnp.int32, (L, L), 0)
    low = lane < E
    early = lax.rem(row, 8) < 4

    slot = lax.rem(lax.broadcasted_iota(jnp.int32, (E, L), 0), 8)

    def tile(c, z, y):
        both = bl_ref[c, z * 8 + y].astype(F32)
        return jnp.where(mine == 0, both[:8], both[8:])

    def block(y):
        left, right = (jnp.concatenate([tile(c, z, y) for z in range(8)], axis=0) for c in range(2))
        halves = []
        for high in range(2):
            from_left = jnp.zeros((E, L), jnp.bool_)
            for s in range(8):
                away = (4 * high + s // 2 - y) % 8
                if away > 4 or (away == 0 and s % 2 == 0) or (away == 4 and s % 2 == 1):
                    from_left = jnp.logical_or(from_left, slot == s)
            halves.append(jnp.where(from_left, left, right))
        return jnp.concatenate(halves, axis=0)

    blocks = [block(y) for y in range(8)]
    parts = []
    for n in range(2):
        e0, o0, e1, o1 = blocks[4 * n : 4 * n + 4]
        ro0, re1 = pltpu.roll(o0, E, 1), pltpu.roll(e1, E, 1)
        parts.append(jnp.where(jnp.logical_or(low, early), e0, ro0))
        parts.append(jnp.where(low, ro0, re1))
        parts.append(jnp.where(jnp.logical_and(low, early), re1, o1))
    blended = jnp.concatenate(parts, axis=1).astype(BF)

    updated = (dot_nt(who_ref[...], blended) + stack_ref[...].astype(F32)).astype(BF).astype(F32)
    center = jnp.mean(updated, axis=0, keepdims=True)
    spread = jnp.mean(jnp.square(updated - center), axis=0, keepdims=True)
    normed = ((updated - center) * lax.rsqrt(spread + 1e-05)).astype(BF)
    copy.wait()
    packed = jnp.dot(wv_ref[...], normed, preferred_element_type=F32)

    mixed = []
    for h in range(H):
        q = (packed[E * h : E * h + E] * E**-0.5).astype(BF)
        k = packed[D + E * h : D + E * h + E].astype(BF)
        v = packed[2 * D + E * h : 2 * D + E * h + E].astype(BF)
        logits = dot_tn(k, q)
        e = jnp.exp(logits - jnp.max(logits, axis=0, keepdims=True))
        probs = (e / jnp.sum(e, axis=0, keepdims=True)).astype(BF)
        mixed.append(jnp.dot(v, probs, preferred_element_type=F32).astype(BF))
    mixed = jnp.concatenate(mixed, axis=0)

    result = (updated + jnp.dot(wvo_ref[...], mixed, preferred_element_type=F32)).astype(BF)
    place = (row // 8 % 2 * E + row // 16 * 8 + row % 8 == lane).astype(BF)
    out_ref[...] = dot_nt(place, result).astype(BF)

    one = lax.broadcasted_iota(jnp.int32, (1, L), 1) < E
    lines = []
    for n in range(4):
        e, o = tile(0, 0, 2 * n), tile(0, 0, 2 * n + 1)
        re, ro = pltpu.roll(e, E, 1), pltpu.roll(o, E, 1)
        lines.append(jnp.where(one, re[4:5], e[5:6]))
        lines.append(jnp.where(one, re[6:7], e[7:8]))
        lines.append(jnp.where(one, o[2:3], ro[3:4]))
    scores = jnp.concatenate(lines + [jnp.zeros((L - H, L), F32)], axis=0).T
    weights = jnp.concatenate([cw_ref[...].astype(F32), jnp.zeros((L - H, L), F32)], axis=0)
    pair = pair_ref[...].astype(F32) + jnp.dot(
        scores.astype(BF), weights.astype(BF), preferred_element_type=F32
    )
    pair_out_ref[...] = pair.astype(BF)


def around(x):
    pairs = [(2 * y + c, (y + 1 - 2 * c) % 8 * 2 + c) for y in range(8) for c in range(2)]
    return lax.ppermute(x, ("y", "c"), pairs)


def per_device(stack, spans, pair, w_triple, w_out, v_triple, v_out, offsets, contact_w):
    y, c = lax.axis_index("y"), lax.axis_index("c")
    y1, c1 = y[None].astype(jnp.int32), c[None].astype(jnp.int32)
    at = jnp.concatenate([y1, c1])
    pair_own = pair.reshape(L, 128)
    own_row = stack.reshape(L, D)

    column_weights = jnp.concatenate([v_triple.T, v_out.T, w_out.T, jnp.zeros((2, D), BF)], axis=0)
    gathered = lax.all_gather(column_weights, ROWS, axis=0, tiled=False)

    normed = normalize(own_row.astype(F32)).astype(BF)
    one = around(lax.all_gather(normed, "c", axis=0, tiled=False))
    two = around(one)

    bias = lax.dot_general(offsets, pair_own, (((0,), (1,)), ((), ())), preferred_element_type=F32).astype(BF)
    bias_pairs = jnp.stack([bias[first_head(n) : first_head(n) + 2] for n in range(8)])
    slices = w_triple.T.reshape(18, 2, 8, 48).transpose(2, 0, 1, 3).reshape(8, 1, 18, 96)
    slices = jnp.pad(slices, ((0, 0), (0, 0), (0, 0), (0, 32)))
    message = jnp.concatenate(
        [
            jnp.broadcast_to(slices, (8, 8, 18, 128)).reshape(64, 18, 128),
            own_row.reshape(64, 12, 128),
            jnp.broadcast_to(bias_pairs[None], (8, 8, 2, 128)).reshape(64, 2, 128),
        ],
        axis=1,
    )
    came = lax.all_to_all(message, CHIPS, 0, 0, tiled=True)
    source = lax.broadcasted_iota(jnp.int32, (2048, 384), 0)
    target = lax.broadcasted_iota(jnp.int32, (2048, 384), 1)
    column = (source // 32 * 2 + c) * 18 + source % 32
    wanted = target // 128 * D + first_head(y) * E + target % 128
    pick = jnp.logical_and(column == wanted, source % 32 < 18).astype(BF)
    came, one, pick = lax.optimization_barrier((came, one, pick))
    picked = dot_tn(came.reshape(2048, 128), pick)[:96].astype(BF)
    picked = lax.all_gather(picked, "c", axis=0, tiled=False)
    half = lax.dynamic_slice_in_dim(picked, c * 48, 48, axis=1)
    half, two = lax.optimization_barrier((half[0] + half[1], two))
    three = around(two)
    four = around(jnp.where(c == 0, three[1], three[0]))
    over_z = lax.all_to_all(jnp.broadcast_to(half, (8, 48, 384)), "z", 0, 0, tiled=True)
    w_heads = lax.all_gather(over_z, "c", axis=0, tiled=False).reshape(D, 384)

    rest = lax.all_gather(came[:, 18:, :], "c", axis=0, tiled=False)
    stack_own = rest[:, :, :12].reshape(2, 64, 2, D)
    stack_own = lax.dynamic_index_in_dim(stack_own, c, 2, keepdims=False).reshape(2, 8, 2, 4, D)
    stack_own = stack_own.transpose(2, 1, 3, 0, 4).reshape(R, D)
    bias_own = lax.dynamic_index_in_dim(rest[:, :, 12:], c, 2, keepdims=False)
    bias_own = bias_own.transpose(1, 0, 2).reshape(L, L)

    tied, values = pl.pallas_call(
        project_and_tie,
        out_shape=(
            jax.ShapeDtypeStruct((2, L, L), F32),
            jax.ShapeDtypeStruct((8, L, 2 * E), BF),
        ),
        in_specs=[SMEM] + [VMEM] * 6,
        out_specs=(VMEM, VMEM),
        compiler_params=params(),
    )(at, w_heads, normed, one, two, three, four)

    tied = lax.all_gather(tied, "c", axis=0, tiled=False)
    tied = lax.dynamic_index_in_dim(tied, c, 1, keepdims=False)
    tied = (tied[0] + tied[1]).astype(BF)
    parts = lax.all_to_all(jnp.broadcast_to(tied, (8, L, L)), "z", 0, 0, tiled=True)
    head = pl.pallas_call(
        attend,
        out_shape=jax.ShapeDtypeStruct((2, L, L), BF),
        in_specs=[SMEM, VMEM, VMEM],
        out_specs=VMEM,
        compiler_params=params(),
    )(spans, parts, bias_own)
    heads = lax.all_gather(head, "c", axis=0, tiled=False)
    message = pl.pallas_call(
        blend,
        out_shape=jax.ShapeDtypeStruct((L, 8, 2 * E), BF),
        in_specs=[SMEM, VMEM, VMEM],
        out_specs=VMEM,
        scratch_shapes=[pltpu.VMEM((L, 8, 2 * E), F32)],
        compiler_params=params(),
    )(y1, heads, values)
    came = lax.all_to_all(message.reshape(64, 16, 128), CHIPS, 0, 0, tiled=True)
    column_triple = gathered[:, :18].reshape(3 * D, D)
    column_out = gathered[:, 18:24].reshape(D, D)
    row_out = gathered[:, 24:30].reshape(D, D)
    came, column_triple = lax.optimization_barrier((came, column_triple))
    blended = lax.all_gather(came, "c", axis=0, tiled=False)

    alignment, pair_out = pl.pallas_call(
        column_block,
        out_shape=(jax.ShapeDtypeStruct((R, D), BF), jax.ShapeDtypeStruct((L, 128), BF)),
        in_specs=[SMEM] + [VMEM] * 3 + [ANY] + [VMEM] * 3,
        out_specs=(VMEM, VMEM),
        scratch_shapes=[pltpu.VMEM((3 * D, D), BF), pltpu.SemaphoreType.DMA],
        compiler_params=params(48),
    )(c1, blended, stack_own.T, row_out, column_triple, column_out, pair_own, contact_w)
    return alignment.reshape(R, 1, D), pair_out.reshape(1, L, 128)


def solution(mesh):
    torus = Mesh(mesh.devices.reshape(mesh.shape["aln"], 8, 8, 2), ALL)
    in_specs = (
        P(ALL, None, None),
        P("a"),
        P(ALL, None, None),
        P(None, ROWS),
        P(None, ROWS),
        P(None, ROWS),
        P(None, ROWS),
        P(),
        P(),
    )
    out_specs = (P("a", ROWS, None), P(ALL, None, None))
    return jax.shard_map(
        per_device, mesh=torus, in_specs=in_specs, out_specs=out_specs, check_vma=False
    )
```

```python
import jax
import jax.numpy as jnp
from jax import lax
from jax.experimental import pallas as pl
from jax.experimental.pallas import tpu as pltpu
from jax.sharding import Mesh
from jax.sharding import PartitionSpec as P

ALL = ("a", "z", "y", "c")
ROWS = ("z", "y", "c")
CHIPS = ("z", "y")
D, H, E, L, R = 768, 12, 64, 128, 128
BF, F32 = jnp.bfloat16, jnp.float32
VMEM = pl.BlockSpec(memory_space=pltpu.VMEM)
SMEM = pl.BlockSpec(memory_space=pltpu.SMEM)
ANY = pl.BlockSpec(memory_space=pl.ANY)


def params(mib=16):
    return pltpu.CompilerParams(vmem_limit_bytes=mib << 20)


def dot_nt(a, b):
    return lax.dot_general(a, b, (((1,), (1,)), ((), ())), preferred_element_type=F32)


def dot_tn(a, b):
    return lax.dot_general(a, b, (((0,), (0,)), ((), ())), preferred_element_type=F32)


def first_head(y):
    return 3 * (y // 2) + y % 2


def normalize(x):
    center = jnp.mean(x, axis=-1, keepdims=True)
    spread = jnp.mean(jnp.square(x - center), axis=-1, keepdims=True)
    return (x - center) * lax.rsqrt(spread + 1e-05)


def project_and_tie(at_ref, w_ref, own_ref, one_ref, two_ref, three_ref, four_ref, tied_ref, v_ref):
    w = w_ref[...]
    lane = lax.broadcasted_iota(jnp.int32, (L, 2 * E), 1)
    y, c = at_ref[0], at_ref[1]
    step = 2 * c - 1
    rows = [(own_ref, None, 0, c), (four_ref, None, 4, 1 - c)]
    for n, ref in enumerate((one_ref, two_ref, three_ref)):
        rows += [(ref, core, (n + 1) * step, core) for core in range(2)]
    tied = [jnp.zeros((L, L), F32), jnp.zeros((L, L), F32)]
    for ref, core, offset, source in rows:
        x = ref[...] if core is None else ref[core]
        packed = jnp.dot(x, w, preferred_element_type=F32)
        q = packed[:, : 2 * E] * E**-0.5
        k = packed[:, 2 * E : 4 * E].astype(BF)
        v_ref[2 * lax.rem(y + 8 + offset, 4) + source] = packed[:, 4 * E :].astype(BF)
        tied[0] += dot_nt(jnp.where(lane < E, q, 0.0).astype(BF), k)
        tied[1] += dot_nt(jnp.where(lane < E, 0.0, q).astype(BF), k)
    for h in range(2):
        tied_ref[h] = tied[h] * R**-0.5


def attend(span_ref, part_ref, bias_ref, out_ref):
    scores = bias_ref[...].astype(F32)
    for n in range(8):
        scores += part_ref[n].astype(F32)
    j = lax.broadcasted_iota(jnp.int32, (L, L), 1)
    masked = jnp.where(j < span_ref[0], scores, -1e30)
    e = jnp.exp(masked - jnp.max(masked, axis=1, keepdims=True))
    out_ref[0] = (e / jnp.sum(e, axis=1, keepdims=True)).astype(BF)
    out_ref[1] = scores.astype(BF)


def blend(y_ref, probs_ref, v_ref, out_ref, held):
    lane = lax.broadcasted_iota(jnp.int32, (L, 2 * E), 1)
    low = lane < E
    odd = lax.rem(y_ref[0], 2) == 1
    plain = [probs_ref[h, 1].astype(F32) for h in range(2)]
    moved = [pltpu.roll(s, E, 1) for s in plain]
    for n in range(8):
        v = v_ref[n]
        o = jnp.where(
            low,
            jnp.dot(probs_ref[0, 0], v, preferred_element_type=F32),
            jnp.dot(probs_ref[1, 0], v, preferred_element_type=F32),
        )
        h, half = (n % 4) // 2, n % 2
        if n < 4:
            extra = moved[h] if half else plain[h]
            o = jnp.where(jnp.logical_and(low, odd), extra, o)
        else:
            extra = plain[h] if half else moved[h]
            o = jnp.where(jnp.logical_or(low, odd), o, extra)
        held[:, n, :] = o
    out_ref[...] = held[...].astype(BF)


def pack(far_ref, out_ref, held, packed, in_sems, out_sems):
    copies = [
        pltpu.make_async_copy(far_ref.at[pl.ds(16 * n, 16)], held.at[pl.ds(16 * n, 16)], in_sems.at[n])
        for n in range(8)
    ]
    for copy in copies:
        copy.start()
    sent = []
    for n in range(8):
        copies[n].wait()
        for d in range(16 * n, 16 * n + 16):
            packed[18 * d : 18 * d + 18, :] = held[d, 0:18, :]
            packed[3 * D + 6 * d : 3 * D + 6 * d + 6, :] = held[d, 18:24, :]
            packed[4 * D + 6 * d : 4 * D + 6 * d + 6, :] = held[d, 24:30, :]
        for m, (start, rows) in enumerate(((288 * n, 288), (3 * D + 96 * n, 96), (4 * D + 96 * n, 96))):
            part = pl.ds(start, rows)
            sent.append(pltpu.make_async_copy(packed.at[part], out_ref.at[part], out_sems.at[3 * n + m]))
            sent[-1].start()
    for copy in sent:
        copy.wait()


def column_block(c_ref, bl_ref, stack_ref, far_ref, pair_ref, cw_ref, out_ref, pair_out_ref, w_ref, sems):
    order = (8, 9, 0, 1, 2, 3, 4, 5, 6, 7)
    copies = []
    for n, m in enumerate(order):
        part = pl.ds(384 * m, 384)
        copies.append(pltpu.make_async_copy(far_ref.at[part], w_ref.at[part], sems.at[n]))
        copies[n].start()
    mine = c_ref[0]
    lane = lax.broadcasted_iota(jnp.int32, (L, L), 1)
    row = lax.broadcasted_iota(jnp.int32, (L, L), 0)
    low = lane < E
    early = lax.rem(row, 8) < 4

    slot = lax.rem(lax.broadcasted_iota(jnp.int32, (E, L), 0), 8)

    def tile(c, z, y):
        both = bl_ref[c, z * 8 + y].astype(F32)
        return jnp.where(mine == 0, both[:8], both[8:])

    def block(y):
        left, right = (jnp.concatenate([tile(c, z, y) for z in range(8)], axis=0) for c in range(2))
        halves = []
        for high in range(2):
            from_left = jnp.zeros((E, L), jnp.bool_)
            for s in range(8):
                away = (4 * high + s // 2 - y) % 8
                if away > 4 or (away == 0 and s % 2 == 0) or (away == 4 and s % 2 == 1):
                    from_left = jnp.logical_or(from_left, slot == s)
            halves.append(jnp.where(from_left, left, right))
        return jnp.concatenate(halves, axis=0)

    blocks = [block(y) for y in range(8)]
    parts = []
    for n in range(2):
        e0, o0, e1, o1 = blocks[4 * n : 4 * n + 4]
        ro0, re1 = pltpu.roll(o0, E, 1), pltpu.roll(e1, E, 1)
        parts.append(jnp.where(jnp.logical_or(low, early), e0, ro0))
        parts.append(jnp.where(low, ro0, re1))
        parts.append(jnp.where(jnp.logical_and(low, early), re1, o1))
    blended = jnp.concatenate(parts, axis=1).astype(BF)

    for copy in copies[:2]:
        copy.wait()
    updated = (dot_nt(w_ref[4 * D :], blended) + stack_ref[...].astype(F32)).astype(BF).astype(F32)
    center = jnp.mean(updated, axis=0, keepdims=True)
    spread = jnp.mean(jnp.square(updated - center), axis=0, keepdims=True)
    normed = ((updated - center) * lax.rsqrt(spread + 1e-05)).astype(BF)
    for copy in copies[2:8]:
        copy.wait()
    packed = jnp.dot(w_ref[: 3 * D], normed, preferred_element_type=F32)

    mixed = []
    for h in range(H):
        q = (packed[E * h : E * h + E] * E**-0.5).astype(BF)
        k = packed[D + E * h : D + E * h + E].astype(BF)
        v = packed[2 * D + E * h : 2 * D + E * h + E].astype(BF)
        logits = dot_tn(k, q)
        e = jnp.exp(logits - jnp.max(logits, axis=0, keepdims=True))
        probs = (e / jnp.sum(e, axis=0, keepdims=True)).astype(BF)
        mixed.append(jnp.dot(v, probs, preferred_element_type=F32).astype(BF))
    mixed = jnp.concatenate(mixed, axis=0)

    for copy in copies[8:]:
        copy.wait()
    result = (updated + jnp.dot(w_ref[3 * D : 4 * D], mixed, preferred_element_type=F32)).astype(BF)
    place = (row // 8 % 2 * E + row // 16 * 8 + row % 8 == lane).astype(BF)
    out_ref[...] = dot_nt(place, result).astype(BF)

    one = lax.broadcasted_iota(jnp.int32, (1, L), 1) < E
    lines = []
    for n in range(4):
        e, o = tile(0, 0, 2 * n), tile(0, 0, 2 * n + 1)
        re, ro = pltpu.roll(e, E, 1), pltpu.roll(o, E, 1)
        lines.append(jnp.where(one, re[4:5], e[5:6]))
        lines.append(jnp.where(one, re[6:7], e[7:8]))
        lines.append(jnp.where(one, o[2:3], ro[3:4]))
    scores = jnp.concatenate(lines + [jnp.zeros((L - H, L), F32)], axis=0).T
    weights = jnp.concatenate([cw_ref[...].astype(F32), jnp.zeros((L - H, L), F32)], axis=0)
    pair = pair_ref[...].astype(F32) + jnp.dot(
        scores.astype(BF), weights.astype(BF), preferred_element_type=F32
    )
    pair_out_ref[...] = pair.astype(BF)


def around(x):
    pairs = [(2 * y + c, (y + 1 - 2 * c) % 8 * 2 + c) for y in range(8) for c in range(2)]
    return lax.ppermute(x, ("y", "c"), pairs)


def per_device(stack, spans, pair, w_triple, w_out, v_triple, v_out, offsets, contact_w):
    y, c = lax.axis_index("y"), lax.axis_index("c")
    y1, c1 = y[None].astype(jnp.int32), c[None].astype(jnp.int32)
    at = jnp.concatenate([y1, c1])
    pair_own = pair.reshape(L, 128)
    own_row = stack.reshape(L, D)

    column_weights = jnp.concatenate([v_triple.T, v_out.T, w_out.T, jnp.zeros((2, D), BF)], axis=0)
    gathered = lax.all_gather(column_weights, ROWS, axis=0, tiled=False)

    normed = normalize(own_row.astype(F32)).astype(BF)
    one = around(lax.all_gather(normed, "c", axis=0, tiled=False))
    two = around(one)

    bias = lax.dot_general(offsets, pair_own, (((0,), (1,)), ((), ())), preferred_element_type=F32).astype(BF)
    bias_pairs = jnp.stack([bias[first_head(n) : first_head(n) + 2] for n in range(8)])
    slices = w_triple.T.reshape(18, 2, 8, 48).transpose(2, 0, 1, 3).reshape(8, 1, 18, 96)
    slices = jnp.pad(slices, ((0, 0), (0, 0), (0, 0), (0, 32)))
    message = jnp.concatenate(
        [
            jnp.broadcast_to(slices, (8, 8, 18, 128)).reshape(64, 18, 128),
            own_row.reshape(64, 12, 128),
            jnp.broadcast_to(bias_pairs[None], (8, 8, 2, 128)).reshape(64, 2, 128),
        ],
        axis=1,
    )
    came = lax.all_to_all(message, CHIPS, 0, 0, tiled=True)
    source = lax.broadcasted_iota(jnp.int32, (2048, 384), 0)
    target = lax.broadcasted_iota(jnp.int32, (2048, 384), 1)
    column = (source // 32 * 2 + c) * 18 + source % 32
    wanted = target // 128 * D + first_head(y) * E + target % 128
    pick = jnp.logical_and(column == wanted, source % 32 < 18).astype(BF)
    came, one, pick = lax.optimization_barrier((came, one, pick))
    picked = dot_tn(came.reshape(2048, 128), pick)[:96].astype(BF)
    picked = lax.all_gather(picked, "c", axis=0, tiled=False)
    half = lax.dynamic_slice_in_dim(picked, c * 48, 48, axis=1)
    half, two = lax.optimization_barrier((half[0] + half[1], two))
    three = around(two)
    four = around(jnp.where(c == 0, three[1], three[0]))
    over_z = lax.all_to_all(jnp.broadcast_to(half, (8, 48, 384)), "z", 0, 0, tiled=True)
    w_heads = lax.all_gather(over_z, "c", axis=0, tiled=False).reshape(D, 384)

    rest = lax.all_gather(came[:, 18:, :], "c", axis=0, tiled=False)
    stack_own = rest[:, :, :12].reshape(2, 64, 2, D)
    stack_own = lax.dynamic_index_in_dim(stack_own, c, 2, keepdims=False).reshape(2, 8, 2, 4, D)
    stack_own = stack_own.transpose(2, 1, 3, 0, 4).reshape(R, D)
    bias_own = lax.dynamic_index_in_dim(rest[:, :, 12:], c, 2, keepdims=False)
    bias_own = bias_own.transpose(1, 0, 2).reshape(L, L)

    tied, values = pl.pallas_call(
        project_and_tie,
        out_shape=(
            jax.ShapeDtypeStruct((2, L, L), F32),
            jax.ShapeDtypeStruct((8, L, 2 * E), BF),
        ),
        in_specs=[SMEM] + [VMEM] * 6,
        out_specs=(VMEM, VMEM),
        compiler_params=params(),
    )(at, w_heads, normed, one, two, three, four)

    tied = lax.all_gather(tied, "c", axis=0, tiled=False)
    tied = lax.dynamic_index_in_dim(tied, c, 1, keepdims=False)
    tied = (tied[0] + tied[1]).astype(BF)
    parts = lax.all_to_all(jnp.broadcast_to(tied, (8, L, L)), "z", 0, 0, tiled=True)
    head = pl.pallas_call(
        attend,
        out_shape=jax.ShapeDtypeStruct((2, L, L), BF),
        in_specs=[SMEM, VMEM, VMEM],
        out_specs=VMEM,
        compiler_params=params(),
    )(spans, parts, bias_own)
    heads = lax.all_gather(head, "c", axis=0, tiled=False)
    message = pl.pallas_call(
        blend,
        out_shape=jax.ShapeDtypeStruct((L, 8, 2 * E), BF),
        in_specs=[SMEM, VMEM, VMEM],
        out_specs=VMEM,
        scratch_shapes=[pltpu.VMEM((L, 8, 2 * E), F32)],
        compiler_params=params(),
    )(y1, heads, values)
    came = lax.all_to_all(message.reshape(64, 16, 128), CHIPS, 0, 0, tiled=True)
    column_weights = pl.pallas_call(
        pack,
        out_shape=jax.ShapeDtypeStruct((5 * D, D), BF),
        in_specs=[ANY],
        out_specs=ANY,
        scratch_shapes=[
            pltpu.VMEM((128, 32, D), BF),
            pltpu.VMEM((5 * D, D), BF),
            pltpu.SemaphoreType.DMA((8,)),
            pltpu.SemaphoreType.DMA((24,)),
        ],
        compiler_params=params(56),
    )(gathered)
    came, column_weights = lax.optimization_barrier((came, column_weights))
    blended = lax.all_gather(came, "c", axis=0, tiled=False)

    alignment, pair_out = pl.pallas_call(
        column_block,
        out_shape=(jax.ShapeDtypeStruct((R, D), BF), jax.ShapeDtypeStruct((L, 128), BF)),
        in_specs=[SMEM, VMEM, VMEM, ANY, VMEM, VMEM],
        out_specs=(VMEM, VMEM),
        scratch_shapes=[pltpu.VMEM((5 * D, D), BF), pltpu.SemaphoreType.DMA((10,))],
        compiler_params=params(52),
    )(c1, blended, stack_own.T, column_weights, pair_own, contact_w)
    return alignment.reshape(R, 1, D), pair_out.reshape(1, L, 128)


def solution(mesh):
    torus = Mesh(mesh.devices.reshape(mesh.shape["aln"], 8, 8, 2), ALL)
    in_specs = (
        P(ALL, None, None),
        P("a"),
        P(ALL, None, None),
        P(None, ROWS),
        P(None, ROWS),
        P(None, ROWS),
        P(None, ROWS),
        P(),
        P(),
    )
    out_specs = (P("a", ROWS, None), P(ALL, None, None))
    return jax.shard_map(
        per_device, mesh=torus, in_specs=in_specs, out_specs=out_specs, check_vma=False
    )
```

```python
import jax
import jax.numpy as jnp
from jax import lax
from jax.experimental import pallas as pl
from jax.experimental.pallas import tpu as pltpu
from jax.sharding import Mesh
from jax.sharding import PartitionSpec as P

ALL = ("a", "z", "y", "c")
ROWS = ("z", "y", "c")
CHIPS = ("z", "y")
D, H, E, L, R = 768, 12, 64, 128, 128
BF, F32 = jnp.bfloat16, jnp.float32
VMEM = pl.BlockSpec(memory_space=pltpu.VMEM)
SMEM = pl.BlockSpec(memory_space=pltpu.SMEM)
ANY = pl.BlockSpec(memory_space=pl.ANY)


def params(mib=16):
    return pltpu.CompilerParams(vmem_limit_bytes=mib << 20)


def dot_nt(a, b):
    return lax.dot_general(a, b, (((1,), (1,)), ((), ())), preferred_element_type=F32)


def dot_tn(a, b):
    return lax.dot_general(a, b, (((0,), (0,)), ((), ())), preferred_element_type=F32)


def first_head(y):
    return 3 * (y // 2) + y % 2


def normalize(x):
    center = jnp.mean(x, axis=-1, keepdims=True)
    spread = jnp.mean(jnp.square(x - center), axis=-1, keepdims=True)
    return (x - center) * lax.rsqrt(spread + 1e-05)


def project_and_tie(at_ref, w_ref, own_ref, one_ref, two_ref, three_ref, four_ref, tied_ref, v_ref):
    w = w_ref[...]
    lane = lax.broadcasted_iota(jnp.int32, (L, 2 * E), 1)
    y, c = at_ref[0], at_ref[1]
    step = 2 * c - 1
    rows = [(own_ref, None, 0, c), (four_ref, None, 4, 1 - c)]
    for n, ref in enumerate((one_ref, two_ref, three_ref)):
        rows += [(ref, core, (n + 1) * step, core) for core in range(2)]
    tied = [jnp.zeros((L, L), F32), jnp.zeros((L, L), F32)]
    for ref, core, offset, source in rows:
        x = ref[...] if core is None else ref[core]
        packed = jnp.dot(x, w, preferred_element_type=F32)
        q = packed[:, : 2 * E] * E**-0.5
        k = packed[:, 2 * E : 4 * E].astype(BF)
        v_ref[2 * lax.rem(y + 8 + offset, 4) + source] = packed[:, 4 * E :].astype(BF)
        tied[0] += dot_nt(jnp.where(lane < E, q, 0.0).astype(BF), k)
        tied[1] += dot_nt(jnp.where(lane < E, 0.0, q).astype(BF), k)
    for h in range(2):
        tied_ref[h] = tied[h] * R**-0.5


def attend(span_ref, part_ref, bias_ref, out_ref):
    scores = bias_ref[...].astype(F32)
    for n in range(8):
        scores += part_ref[n].astype(F32)
    j = lax.broadcasted_iota(jnp.int32, (L, L), 1)
    masked = jnp.where(j < span_ref[0], scores, -1e30)
    e = jnp.exp(masked - jnp.max(masked, axis=1, keepdims=True))
    out_ref[0] = (e / jnp.sum(e, axis=1, keepdims=True)).astype(BF)
    out_ref[1] = scores.astype(BF)


def blend(at_ref, probs_ref, v_ref, out_ref, held):
    half = L // 2
    lane = lax.broadcasted_iota(jnp.int32, (half, 2 * E), 1)
    low = lane < E
    odd = lax.rem(at_ref[0], 2) == 1
    pick = (2 * lax.broadcasted_iota(jnp.int32, (half, L), 0) + at_ref[1] == lane).astype(BF)
    probs = [jnp.dot(pick, probs_ref[h, 0], preferred_element_type=F32).astype(BF) for h in range(2)]
    plain = [jnp.dot(pick, probs_ref[h, 1], preferred_element_type=F32) for h in range(2)]
    moved = [pltpu.roll(s, E, 1) for s in plain]
    for core in range(2):
        for n in range(8):
            v = v_ref[core, n]
            o = jnp.where(
                low,
                jnp.dot(probs[0], v, preferred_element_type=F32),
                jnp.dot(probs[1], v, preferred_element_type=F32),
            )
            h, second = (n % 4) // 2, n % 2
            if n < 4:
                extra = moved[h] if second else plain[h]
                o = jnp.where(jnp.logical_and(low, odd), extra, o)
            else:
                extra = plain[h] if second else moved[h]
                o = jnp.where(jnp.logical_or(low, odd), o, extra)
            held[:, 8 * core + n, :] = o
    out_ref[...] = held[...].astype(BF)


def pack(far_ref, out_ref, held, packed, in_sems, out_sems):
    copies = [
        pltpu.make_async_copy(far_ref.at[pl.ds(16 * n, 16)], held.at[pl.ds(16 * n, 16)], in_sems.at[n])
        for n in range(8)
    ]
    for copy in copies:
        copy.start()
    sent = []
    for n in range(8):
        copies[n].wait()
        for d in range(16 * n, 16 * n + 16):
            packed[18 * d : 18 * d + 18, :] = held[d, 0:18, :]
            packed[3 * D + 6 * d : 3 * D + 6 * d + 6, :] = held[d, 18:24, :]
            packed[4 * D + 6 * d : 4 * D + 6 * d + 6, :] = held[d, 24:30, :]
        for m, (start, rows) in enumerate(((288 * n, 288), (3 * D + 96 * n, 96), (4 * D + 96 * n, 96))):
            part = pl.ds(start, rows)
            sent.append(pltpu.make_async_copy(packed.at[part], out_ref.at[part], out_sems.at[3 * n + m]))
            sent[-1].start()
    for copy in sent:
        copy.wait()


def column_block(bl_ref, stack_ref, far_ref, pair_ref, cw_ref, out_ref, pair_out_ref, w_ref, sems):
    order = (8, 9, 0, 1, 2, 3, 4, 5, 6, 7)
    copies = []
    for n, m in enumerate(order):
        part = pl.ds(384 * m, 384)
        copies.append(pltpu.make_async_copy(far_ref.at[part], w_ref.at[part], sems.at[n]))
        copies[n].start()
    lane = lax.broadcasted_iota(jnp.int32, (L, L), 1)
    row = lax.broadcasted_iota(jnp.int32, (L, L), 0)
    low = lane < E
    early = lax.rem(row, 8) < 4

    slot = lax.rem(lax.broadcasted_iota(jnp.int32, (E, L), 0), 8)

    def tile(c, z, y):
        return bl_ref[z * 8 + y].astype(F32)[8 * c : 8 * c + 8]

    def block(y):
        left, right = (jnp.concatenate([tile(c, z, y) for z in range(8)], axis=0) for c in range(2))
        halves = []
        for high in range(2):
            from_left = jnp.zeros((E, L), jnp.bool_)
            for s in range(8):
                away = (4 * high + s // 2 - y) % 8
                if away > 4 or (away == 0 and s % 2 == 0) or (away == 4 and s % 2 == 1):
                    from_left = jnp.logical_or(from_left, slot == s)
            halves.append(jnp.where(from_left, left, right))
        return jnp.concatenate(halves, axis=0)

    blocks = [block(y) for y in range(8)]
    parts = []
    for n in range(2):
        e0, o0, e1, o1 = blocks[4 * n : 4 * n + 4]
        ro0, re1 = pltpu.roll(o0, E, 1), pltpu.roll(e1, E, 1)
        parts.append(jnp.where(jnp.logical_or(low, early), e0, ro0))
        parts.append(jnp.where(low, ro0, re1))
        parts.append(jnp.where(jnp.logical_and(low, early), re1, o1))
    blended = jnp.concatenate(parts, axis=1).astype(BF)

    for copy in copies[:2]:
        copy.wait()
    updated = (dot_nt(w_ref[4 * D :], blended) + stack_ref[...].astype(F32)).astype(BF).astype(F32)
    center = jnp.mean(updated, axis=0, keepdims=True)
    spread = jnp.mean(jnp.square(updated - center), axis=0, keepdims=True)
    normed = ((updated - center) * lax.rsqrt(spread + 1e-05)).astype(BF)
    for copy in copies[2:8]:
        copy.wait()
    packed = jnp.dot(w_ref[: 3 * D], normed, preferred_element_type=F32)

    mixed = []
    for h in range(H):
        q = (packed[E * h : E * h + E] * E**-0.5).astype(BF)
        k = packed[D + E * h : D + E * h + E].astype(BF)
        v = packed[2 * D + E * h : 2 * D + E * h + E].astype(BF)
        logits = dot_tn(k, q)
        e = jnp.exp(logits - jnp.max(logits, axis=0, keepdims=True))
        probs = (e / jnp.sum(e, axis=0, keepdims=True)).astype(BF)
        mixed.append(jnp.dot(v, probs, preferred_element_type=F32).astype(BF))
    mixed = jnp.concatenate(mixed, axis=0)

    for copy in copies[8:]:
        copy.wait()
    result = (updated + jnp.dot(w_ref[3 * D : 4 * D], mixed, preferred_element_type=F32)).astype(BF)
    place = (row // 8 % 2 * E + row // 16 * 8 + row % 8 == lane).astype(BF)
    out_ref[...] = dot_nt(place, result).astype(BF)

    one = lax.broadcasted_iota(jnp.int32, (1, L), 1) < E
    lines = []
    for n in range(4):
        e, o = tile(0, 0, 2 * n), tile(0, 0, 2 * n + 1)
        re, ro = pltpu.roll(e, E, 1), pltpu.roll(o, E, 1)
        lines.append(jnp.where(one, re[4:5], e[5:6]))
        lines.append(jnp.where(one, re[6:7], e[7:8]))
        lines.append(jnp.where(one, o[2:3], ro[3:4]))
    scores = jnp.concatenate(lines + [jnp.zeros((L - H, L), F32)], axis=0).T
    weights = jnp.concatenate([cw_ref[...].astype(F32), jnp.zeros((L - H, L), F32)], axis=0)
    pair = pair_ref[...].astype(F32) + jnp.dot(
        scores.astype(BF), weights.astype(BF), preferred_element_type=F32
    )
    pair_out_ref[...] = pair.astype(BF)


def around(x):
    pairs = [(2 * y + c, (y + 1 - 2 * c) % 8 * 2 + c) for y in range(8) for c in range(2)]
    return lax.ppermute(x, ("y", "c"), pairs)


def per_device(stack, spans, pair, w_triple, w_out, v_triple, v_out, offsets, contact_w):
    y, c = lax.axis_index("y"), lax.axis_index("c")
    y1, c1 = y[None].astype(jnp.int32), c[None].astype(jnp.int32)
    at = jnp.concatenate([y1, c1])
    pair_own = pair.reshape(L, 128)
    own_row = stack.reshape(L, D)

    column_weights = jnp.concatenate([v_triple.T, v_out.T, w_out.T, jnp.zeros((2, D), BF)], axis=0)
    gathered = lax.all_gather(column_weights, ROWS, axis=0, tiled=False)

    normed = normalize(own_row.astype(F32)).astype(BF)
    one = around(lax.all_gather(normed, "c", axis=0, tiled=False))
    two = around(one)

    bias = lax.dot_general(offsets, pair_own, (((0,), (1,)), ((), ())), preferred_element_type=F32).astype(BF)
    bias_pairs = jnp.stack([bias[first_head(n) : first_head(n) + 2] for n in range(8)])
    slices = w_triple.T.reshape(18, 2, 8, 48).transpose(2, 0, 1, 3).reshape(8, 1, 18, 96)
    slices = jnp.pad(slices, ((0, 0), (0, 0), (0, 0), (0, 32)))
    message = jnp.concatenate(
        [
            jnp.broadcast_to(slices, (8, 8, 18, 128)).reshape(64, 18, 128),
            own_row.reshape(64, 12, 128),
            jnp.broadcast_to(bias_pairs[None], (8, 8, 2, 128)).reshape(64, 2, 128),
        ],
        axis=1,
    )
    came = lax.all_to_all(message, CHIPS, 0, 0, tiled=True)
    source = lax.broadcasted_iota(jnp.int32, (2048, 384), 0)
    target = lax.broadcasted_iota(jnp.int32, (2048, 384), 1)
    column = (source // 32 * 2 + c) * 18 + source % 32
    wanted = target // 128 * D + first_head(y) * E + target % 128
    pick = jnp.logical_and(column == wanted, source % 32 < 18).astype(BF)
    came, one, pick = lax.optimization_barrier((came, one, pick))
    picked = dot_tn(came.reshape(2048, 128), pick)[:96].astype(BF)
    picked = lax.all_gather(picked, "c", axis=0, tiled=False)
    half = lax.dynamic_slice_in_dim(picked, c * 48, 48, axis=1)
    half = half[0] + half[1]
    three = around(lax.optimization_barrier((half, two))[1])
    four = around(jnp.where(c == 0, three[1], three[0]))
    over_z = lax.all_to_all(jnp.broadcast_to(half, (8, 48, 384)), "z", 0, 0, tiled=True)
    w_heads = lax.all_gather(over_z, "c", axis=0, tiled=False).reshape(D, 384)

    rest = lax.all_gather(came[:, 18:, :], "c", axis=0, tiled=False)
    stack_own = rest[:, :, :12].reshape(2, 64, 2, D)
    stack_own = lax.dynamic_index_in_dim(stack_own, c, 2, keepdims=False).reshape(2, 8, 2, 4, D)
    stack_own = stack_own.transpose(2, 1, 3, 0, 4).reshape(R, D)
    bias_own = lax.dynamic_index_in_dim(rest[:, :, 12:], c, 2, keepdims=False)
    bias_own = bias_own.transpose(1, 0, 2).reshape(L, L)

    tied, values = pl.pallas_call(
        project_and_tie,
        out_shape=(
            jax.ShapeDtypeStruct((2, L, L), F32),
            jax.ShapeDtypeStruct((8, L, 2 * E), BF),
        ),
        in_specs=[SMEM] + [VMEM] * 6,
        out_specs=(VMEM, VMEM),
        compiler_params=params(),
    )(at, w_heads, normed, one, two, three, four)

    tied = lax.all_gather(tied, "c", axis=0, tiled=False)
    tied = lax.dynamic_index_in_dim(tied, c, 1, keepdims=False)
    tied = (tied[0] + tied[1]).astype(BF)
    parts = lax.all_to_all(jnp.broadcast_to(tied, (8, L, L)), "z", 0, 0, tiled=True)
    head = pl.pallas_call(
        attend,
        out_shape=jax.ShapeDtypeStruct((2, L, L), BF),
        in_specs=[SMEM, VMEM, VMEM],
        out_specs=VMEM,
        compiler_params=params(),
    )(spans, parts, bias_own)
    heads = lax.all_gather(head, "c", axis=0, tiled=False)
    message = pl.pallas_call(
        blend,
        out_shape=jax.ShapeDtypeStruct((L // 2, 16, 2 * E), BF),
        in_specs=[SMEM, VMEM, VMEM],
        out_specs=VMEM,
        scratch_shapes=[pltpu.VMEM((L // 2, 16, 2 * E), F32)],
        compiler_params=params(),
    )(at, heads, lax.all_gather(values, "c", axis=0, tiled=False))
    came = lax.all_to_all(message, CHIPS, 0, 0, tiled=True)
    column_weights = pl.pallas_call(
        pack,
        out_shape=jax.ShapeDtypeStruct((5 * D, D), BF),
        in_specs=[ANY],
        out_specs=ANY,
        scratch_shapes=[
            pltpu.VMEM((128, 32, D), BF),
            pltpu.VMEM((5 * D, D), BF),
            pltpu.SemaphoreType.DMA((8,)),
            pltpu.SemaphoreType.DMA((24,)),
        ],
        compiler_params=params(56),
    )(gathered)
    blended, column_weights = lax.optimization_barrier((came, column_weights))

    alignment, pair_out = pl.pallas_call(
        column_block,
        out_shape=(jax.ShapeDtypeStruct((R, D), BF), jax.ShapeDtypeStruct((L, 128), BF)),
        in_specs=[VMEM, VMEM, ANY, VMEM, VMEM],
        out_specs=(VMEM, VMEM),
        scratch_shapes=[pltpu.VMEM((5 * D, D), BF), pltpu.SemaphoreType.DMA((10,))],
        compiler_params=params(52),
    )(blended, stack_own.T, column_weights, pair_own, contact_w)
    return alignment.reshape(R, 1, D), pair_out.reshape(1, L, 128)


def solution(mesh):
    torus = Mesh(mesh.devices.reshape(mesh.shape["aln"], 8, 8, 2), ALL)
    in_specs = (
        P(ALL, None, None),
        P("a"),
        P(ALL, None, None),
        P(None, ROWS),
        P(None, ROWS),
        P(None, ROWS),
        P(None, ROWS),
        P(),
        P(),
    )
    out_specs = (P("a", ROWS, None), P(ALL, None, None))
    return jax.shard_map(
        per_device, mesh=torus, in_specs=in_specs, out_specs=out_specs, check_vma=False
    )
```

```python
import jax
import jax.numpy as jnp
from jax import lax
from jax.experimental import pallas as pl
from jax.experimental.pallas import tpu as pltpu
from jax.sharding import Mesh
from jax.sharding import PartitionSpec as P

ALL = ("a", "z", "y", "c")
ROWS = ("z", "y", "c")
CHIPS = ("z", "y")
D, H, E, L, R = 768, 12, 64, 128, 128
BF, F32 = jnp.bfloat16, jnp.float32
VMEM = pl.BlockSpec(memory_space=pltpu.VMEM)
SMEM = pl.BlockSpec(memory_space=pltpu.SMEM)
ANY = pl.BlockSpec(memory_space=pl.ANY)


def params(mib=16):
    return pltpu.CompilerParams(vmem_limit_bytes=mib << 20)


def dot_nt(a, b):
    return lax.dot_general(a, b, (((1,), (1,)), ((), ())), preferred_element_type=F32)


def dot_tn(a, b):
    return lax.dot_general(a, b, (((0,), (0,)), ((), ())), preferred_element_type=F32)


def first_head(y):
    return 3 * (y // 2) + y % 2


def normalize(x):
    center = jnp.mean(x, axis=-1, keepdims=True)
    spread = jnp.mean(jnp.square(x - center), axis=-1, keepdims=True)
    return (x - center) * lax.rsqrt(spread + 1e-05)


def project_and_tie(at_ref, w_ref, own_ref, one_ref, two_ref, three_ref, four_ref, tied_ref, v_ref, held):
    w = w_ref[...]
    lane = lax.broadcasted_iota(jnp.int32, (L, 2 * E), 1)
    y, c = at_ref[0], at_ref[1]
    step = 2 * c - 1
    rows = [(own_ref, None, 0, c), (four_ref, None, 4, 1 - c)]
    for n, ref in enumerate((one_ref, two_ref, three_ref)):
        rows += [(ref, core, (n + 1) * step, core) for core in range(2)]
    tied = [jnp.zeros((L, L), F32), jnp.zeros((L, L), F32)]
    for ref, core, offset, source in rows:
        x = ref[...] if core is None else ref[core]
        packed = jnp.dot(x, w, preferred_element_type=F32)
        q = packed[:, : 2 * E] * E**-0.5
        k = packed[:, 2 * E : 4 * E].astype(BF)
        v_ref[2 * lax.rem(y + 8 + offset, 4) + source] = packed[:, 4 * E :].astype(BF)
        tied[0] += dot_nt(jnp.where(lane < E, q, 0.0).astype(BF), k)
        tied[1] += dot_nt(jnp.where(lane < E, 0.0, q).astype(BF), k)
    for h in range(2):
        held[...] = tied[h] * R**-0.5
        for core in range(2):
            tied_ref[core, h] = held[pl.ds(core, L // 2, stride=2), :]


def attend(at_ref, span_ref, part_ref, bias_ref, v_ref, out_ref, held):
    lane = lax.broadcasted_iota(jnp.int32, (L // 2, 2 * E), 1)
    low = lane < E
    odd = lax.rem(at_ref[0], 2) == 1
    probs, plain, moved = [], [], []
    for h in range(2):
        scores = bias_ref[h].astype(F32)
        for n in range(8):
            scores += part_ref[n, h].astype(F32)
        masked = jnp.where(lane < span_ref[0], scores, -1e30)
        e = jnp.exp(masked - jnp.max(masked, axis=1, keepdims=True))
        probs.append((e / jnp.sum(e, axis=1, keepdims=True)).astype(BF))
        plain.append(scores)
        moved.append(pltpu.roll(scores, E, 1))
    for core in range(2):
        for n in range(8):
            v = v_ref[core, n]
            o = jnp.where(
                low,
                jnp.dot(probs[0], v, preferred_element_type=F32),
                jnp.dot(probs[1], v, preferred_element_type=F32),
            )
            h, second = (n % 4) // 2, n % 2
            if n < 4:
                extra = moved[h] if second else plain[h]
                o = jnp.where(jnp.logical_and(low, odd), extra, o)
            else:
                extra = plain[h] if second else moved[h]
                o = jnp.where(jnp.logical_or(low, odd), o, extra)
            held[:, 8 * core + n, :] = o
    out_ref[...] = held[...].astype(BF)


def pack(far_ref, out_ref, held, packed, in_sems, out_sems):
    copies = [
        pltpu.make_async_copy(far_ref.at[pl.ds(16 * n, 16)], held.at[pl.ds(16 * n, 16)], in_sems.at[n])
        for n in range(8)
    ]
    for copy in copies:
        copy.start()
    sent = []
    for n in range(8):
        copies[n].wait()
        for d in range(16 * n, 16 * n + 16):
            packed[18 * d : 18 * d + 18, :] = held[d, 0:18, :]
            packed[3 * D + 6 * d : 3 * D + 6 * d + 6, :] = held[d, 18:24, :]
            packed[4 * D + 6 * d : 4 * D + 6 * d + 6, :] = held[d, 24:30, :]
        for m, (start, rows) in enumerate(((288 * n, 288), (3 * D + 96 * n, 96), (4 * D + 96 * n, 96))):
            part = pl.ds(start, rows)
            sent.append(pltpu.make_async_copy(packed.at[part], out_ref.at[part], out_sems.at[3 * n + m]))
            sent[-1].start()
    for copy in sent:
        copy.wait()


def column_block(bl_ref, stack_ref, far_ref, pair_ref, cw_ref, out_ref, pair_out_ref, w_ref, sems):
    order = (8, 9, 0, 1, 2, 3, 4, 5, 6, 7)
    copies = []
    for n, m in enumerate(order):
        part = pl.ds(384 * m, 384)
        copies.append(pltpu.make_async_copy(far_ref.at[part], w_ref.at[part], sems.at[n]))
        copies[n].start()
    lane = lax.broadcasted_iota(jnp.int32, (L, L), 1)
    row = lax.broadcasted_iota(jnp.int32, (L, L), 0)
    low = lane < E
    early = lax.rem(row, 8) < 4

    slot = lax.rem(lax.broadcasted_iota(jnp.int32, (E, L), 0), 8)

    def tile(c, z, y):
        return bl_ref[z * 8 + y].astype(F32)[8 * c : 8 * c + 8]

    def block(y):
        left, right = (jnp.concatenate([tile(c, z, y) for z in range(8)], axis=0) for c in range(2))
        halves = []
        for high in range(2):
            from_left = jnp.zeros((E, L), jnp.bool_)
            for s in range(8):
                away = (4 * high + s // 2 - y) % 8
                if away > 4 or (away == 0 and s % 2 == 0) or (away == 4 and s % 2 == 1):
                    from_left = jnp.logical_or(from_left, slot == s)
            halves.append(jnp.where(from_left, left, right))
        return jnp.concatenate(halves, axis=0)

    blocks = [block(y) for y in range(8)]
    parts = []
    for n in range(2):
        e0, o0, e1, o1 = blocks[4 * n : 4 * n + 4]
        ro0, re1 = pltpu.roll(o0, E, 1), pltpu.roll(e1, E, 1)
        parts.append(jnp.where(jnp.logical_or(low, early), e0, ro0))
        parts.append(jnp.where(low, ro0, re1))
        parts.append(jnp.where(jnp.logical_and(low, early), re1, o1))
    blended = jnp.concatenate(parts, axis=1).astype(BF)

    for copy in copies[:2]:
        copy.wait()
    updated = (dot_nt(w_ref[4 * D :], blended) + stack_ref[...].astype(F32)).astype(BF).astype(F32)
    center = jnp.mean(updated, axis=0, keepdims=True)
    spread = jnp.mean(jnp.square(updated - center), axis=0, keepdims=True)
    normed = ((updated - center) * lax.rsqrt(spread + 1e-05)).astype(BF)
    for copy in copies[2:8]:
        copy.wait()
    packed = jnp.dot(w_ref[: 3 * D], normed, preferred_element_type=F32)

    mixed = []
    for h in range(H):
        q = (packed[E * h : E * h + E] * E**-0.5).astype(BF)
        k = packed[D + E * h : D + E * h + E].astype(BF)
        v = packed[2 * D + E * h : 2 * D + E * h + E].astype(BF)
        logits = dot_tn(k, q)
        e = jnp.exp(logits - jnp.max(logits, axis=0, keepdims=True))
        probs = (e / jnp.sum(e, axis=0, keepdims=True)).astype(BF)
        mixed.append(jnp.dot(v, probs, preferred_element_type=F32).astype(BF))
    mixed = jnp.concatenate(mixed, axis=0)

    for copy in copies[8:]:
        copy.wait()
    result = (updated + jnp.dot(w_ref[3 * D : 4 * D], mixed, preferred_element_type=F32)).astype(BF)
    place = (row // 8 % 2 * E + row // 16 * 8 + row % 8 == lane).astype(BF)
    out_ref[...] = dot_nt(place, result).astype(BF)

    one = lax.broadcasted_iota(jnp.int32, (1, L), 1) < E
    lines = []
    for n in range(4):
        e, o = tile(0, 0, 2 * n), tile(0, 0, 2 * n + 1)
        re, ro = pltpu.roll(e, E, 1), pltpu.roll(o, E, 1)
        lines.append(jnp.where(one, re[4:5], e[5:6]))
        lines.append(jnp.where(one, re[6:7], e[7:8]))
        lines.append(jnp.where(one, o[2:3], ro[3:4]))
    scores = jnp.concatenate(lines + [jnp.zeros((L - H, L), F32)], axis=0).T
    weights = jnp.concatenate([cw_ref[...].astype(F32), jnp.zeros((L - H, L), F32)], axis=0)
    pair = pair_ref[...].astype(F32) + jnp.dot(
        scores.astype(BF), weights.astype(BF), preferred_element_type=F32
    )
    pair_out_ref[...] = pair.astype(BF)


def around(x):
    pairs = [(2 * y + c, (y + 1 - 2 * c) % 8 * 2 + c) for y in range(8) for c in range(2)]
    return lax.ppermute(x, ("y", "c"), pairs)


def per_device(stack, spans, pair, w_triple, w_out, v_triple, v_out, offsets, contact_w):
    y, c = lax.axis_index("y"), lax.axis_index("c")
    y1, c1 = y[None].astype(jnp.int32), c[None].astype(jnp.int32)
    at = jnp.concatenate([y1, c1])
    pair_own = pair.reshape(L, 128)
    own_row = stack.reshape(L, D)

    column_weights = jnp.concatenate([v_triple.T, v_out.T, w_out.T, jnp.zeros((2, D), BF)], axis=0)
    gathered = lax.all_gather(column_weights, ROWS, axis=0, tiled=False)

    normed = normalize(own_row.astype(F32)).astype(BF)
    one = around(lax.all_gather(normed, "c", axis=0, tiled=False))
    two = around(one)

    bias = lax.dot_general(offsets, pair_own, (((0,), (1,)), ((), ())), preferred_element_type=F32).astype(BF)
    bias_pairs = jnp.stack([bias[first_head(n) : first_head(n) + 2] for n in range(8)])
    slices = w_triple.T.reshape(18, 2, 8, 48).transpose(2, 0, 1, 3).reshape(8, 1, 18, 96)
    slices = jnp.pad(slices, ((0, 0), (0, 0), (0, 0), (0, 32)))
    message = jnp.concatenate(
        [
            jnp.broadcast_to(slices, (8, 8, 18, 128)).reshape(64, 18, 128),
            own_row.reshape(64, 12, 128),
            jnp.broadcast_to(bias_pairs[None], (8, 8, 2, 128)).reshape(64, 2, 128),
        ],
        axis=1,
    )
    came = lax.all_to_all(message, CHIPS, 0, 0, tiled=True)
    source = lax.broadcasted_iota(jnp.int32, (2048, 384), 0)
    target = lax.broadcasted_iota(jnp.int32, (2048, 384), 1)
    column = (source // 32 * 2 + c) * 18 + source % 32
    wanted = target // 128 * D + first_head(y) * E + target % 128
    pick = jnp.logical_and(column == wanted, source % 32 < 18).astype(BF)
    came, one, pick = lax.optimization_barrier((came, one, pick))
    picked = dot_tn(came.reshape(2048, 128), pick)[:96].astype(BF)
    picked = lax.all_gather(picked, "c", axis=0, tiled=False)
    half = lax.dynamic_slice_in_dim(picked, c * 48, 48, axis=1)
    half = half[0] + half[1]
    three = around(lax.optimization_barrier((half, two))[1])
    four = around(jnp.where(c == 0, three[1], three[0]))
    over_z = lax.all_to_all(jnp.broadcast_to(half, (8, 48, 384)), "z", 0, 0, tiled=True)
    w_heads = lax.all_gather(over_z, "c", axis=0, tiled=False).reshape(D, 384)

    stack_own = lax.all_gather(came[:, 18:30], "c", axis=0, tiled=False).reshape(2, 64, 2, D)
    stack_own = lax.dynamic_index_in_dim(stack_own, c, 2, keepdims=False).reshape(2, 8, 2, 4, D)
    stack_own = stack_own.transpose(2, 1, 3, 0, 4).reshape(R, D)
    bias_own = came[:, 30:].transpose(1, 0, 2)

    tied, values = pl.pallas_call(
        project_and_tie,
        out_shape=(
            jax.ShapeDtypeStruct((2, 2, L // 2, L), F32),
            jax.ShapeDtypeStruct((8, L, 2 * E), BF),
        ),
        scratch_shapes=[pltpu.VMEM((L, L), F32)],
        in_specs=[SMEM] + [VMEM] * 6,
        out_specs=(VMEM, VMEM),
        compiler_params=params(),
    )(at, w_heads, normed, one, two, three, four)

    tied = lax.all_gather(tied, "c", axis=0, tiled=False)
    tied = lax.dynamic_index_in_dim(tied, c, 1, keepdims=False)
    tied = (tied[0] + tied[1]).astype(BF)
    parts = lax.all_to_all(jnp.broadcast_to(tied, (8, 2, L // 2, L)), "z", 0, 0, tiled=True)
    message = pl.pallas_call(
        attend,
        out_shape=jax.ShapeDtypeStruct((L // 2, 16, 2 * E), BF),
        in_specs=[SMEM, SMEM, VMEM, VMEM, VMEM],
        out_specs=VMEM,
        scratch_shapes=[pltpu.VMEM((L // 2, 16, 2 * E), F32)],
        compiler_params=params(),
    )(at, spans, parts, bias_own, lax.all_gather(values, "c", axis=0, tiled=False))
    came = lax.all_to_all(message, CHIPS, 0, 0, tiled=True)
    column_weights = pl.pallas_call(
        pack,
        out_shape=jax.ShapeDtypeStruct((5 * D, D), BF),
        in_specs=[ANY],
        out_specs=ANY,
        scratch_shapes=[
            pltpu.VMEM((128, 32, D), BF),
            pltpu.VMEM((5 * D, D), BF),
            pltpu.SemaphoreType.DMA((8,)),
            pltpu.SemaphoreType.DMA((24,)),
        ],
        compiler_params=params(56),
    )(gathered)
    blended, column_weights = lax.optimization_barrier((came, column_weights))

    alignment, pair_out = pl.pallas_call(
        column_block,
        out_shape=(jax.ShapeDtypeStruct((R, D), BF), jax.ShapeDtypeStruct((L, 128), BF)),
        in_specs=[VMEM, VMEM, ANY, VMEM, VMEM],
        out_specs=(VMEM, VMEM),
        scratch_shapes=[pltpu.VMEM((5 * D, D), BF), pltpu.SemaphoreType.DMA((10,))],
        compiler_params=params(52),
    )(blended, stack_own.T, column_weights, pair_own, contact_w)
    return alignment.reshape(R, 1, D), pair_out.reshape(1, L, 128)


def solution(mesh):
    torus = Mesh(mesh.devices.reshape(mesh.shape["aln"], 8, 8, 2), ALL)
    in_specs = (
        P(ALL, None, None),
        P("a"),
        P(ALL, None, None),
        P(None, ROWS),
        P(None, ROWS),
        P(None, ROWS),
        P(None, ROWS),
        P(),
        P(),
    )
    out_specs = (P("a", ROWS, None), P(ALL, None, None))
    return jax.shard_map(
        per_device, mesh=torus, in_specs=in_specs, out_specs=out_specs, check_vma=False
    )
```

```python
import jax
import jax.numpy as jnp
from jax import lax
from jax.experimental import pallas as pl
from jax.experimental.pallas import tpu as pltpu
from jax.sharding import Mesh
from jax.sharding import PartitionSpec as P

ALL = ("a", "z", "y", "c")
ROWS = ("z", "y", "c")
CHIPS = ("z", "y")
D, H, E, L, R = 768, 12, 64, 128, 128
BF, F32 = jnp.bfloat16, jnp.float32
VMEM = pl.BlockSpec(memory_space=pltpu.VMEM)
SMEM = pl.BlockSpec(memory_space=pltpu.SMEM)
ANY = pl.BlockSpec(memory_space=pl.ANY)


def params(mib=16):
    return pltpu.CompilerParams(vmem_limit_bytes=mib << 20)


def dot_nt(a, b):
    return lax.dot_general(a, b, (((1,), (1,)), ((), ())), preferred_element_type=F32)


def dot_tn(a, b):
    return lax.dot_general(a, b, (((0,), (0,)), ((), ())), preferred_element_type=F32)


def first_head(y):
    return 3 * (y // 2) + y % 2


def normalize(x):
    center = jnp.mean(x, axis=-1, keepdims=True)
    spread = jnp.mean(jnp.square(x - center), axis=-1, keepdims=True)
    return (x - center) * lax.rsqrt(spread + 1e-05)


def project_and_tie(at_ref, w_ref, own_ref, one_ref, two_ref, three_ref, four_ref, tied_ref, v_ref, held):
    w = w_ref[...]
    lane = lax.broadcasted_iota(jnp.int32, (L, 2 * E), 1)
    y, c = at_ref[0], at_ref[1]
    step = 2 * c - 1
    rows = [(own_ref, None, 0, c), (four_ref, None, 4, 1 - c)]
    for n, ref in enumerate((one_ref, two_ref, three_ref)):
        rows += [(ref, core, (n + 1) * step, core) for core in range(2)]
    tied = [jnp.zeros((L, L), F32), jnp.zeros((L, L), F32)]
    for ref, core, offset, source in rows:
        x = ref[...] if core is None else ref[core]
        packed = jnp.dot(x, w, preferred_element_type=F32)
        q = packed[:, : 2 * E] * E**-0.5
        k = packed[:, 2 * E : 4 * E].astype(BF)
        v_ref[2 * lax.rem(y + 8 + offset, 4) + source] = packed[:, 4 * E :].astype(BF)
        tied[0] += dot_nt(jnp.where(lane < E, q, 0.0).astype(BF), k)
        tied[1] += dot_nt(jnp.where(lane < E, 0.0, q).astype(BF), k)
    for h in range(2):
        held[...] = tied[h] * R**-0.5
        for core in range(2):
            tied_ref[core, h] = held[pl.ds(core, L // 2, stride=2), :]


def attend(at_ref, span_ref, part_ref, bias_ref, v_ref, out_ref, held):
    lane = lax.broadcasted_iota(jnp.int32, (L // 2, 2 * E), 1)
    low = lane < E
    odd = lax.rem(at_ref[0], 2) == 1
    probs, plain, moved = [], [], []
    for h in range(2):
        scores = bias_ref[h].astype(F32)
        for n in range(8):
            scores += part_ref[n, h].astype(F32)
        masked = jnp.where(lane < span_ref[0], scores, -1e30)
        e = jnp.exp(masked - jnp.max(masked, axis=1, keepdims=True))
        probs.append((e / jnp.sum(e, axis=1, keepdims=True)).astype(BF))
        plain.append(scores)
        moved.append(pltpu.roll(scores, E, 1))
    for core in range(2):
        for n in range(8):
            v = v_ref[core, n]
            o = jnp.where(
                low,
                jnp.dot(probs[0], v, preferred_element_type=F32),
                jnp.dot(probs[1], v, preferred_element_type=F32),
            )
            h, second = (n % 4) // 2, n % 2
            if n < 4:
                extra = moved[h] if second else plain[h]
                o = jnp.where(jnp.logical_and(low, odd), extra, o)
            else:
                extra = plain[h] if second else moved[h]
                o = jnp.where(jnp.logical_or(low, odd), o, extra)
            held[:, 8 * core + n, :] = o
    out_ref[...] = held[...].astype(BF)


def pack(far_ref, triple_ref, out_ref, held, packed, in_sems, out_sems):
    copies = [
        pltpu.make_async_copy(far_ref.at[pl.ds(16 * n, 16)], held.at[pl.ds(16 * n, 16)], in_sems.at[n])
        for n in range(8)
    ]
    for copy in copies:
        copy.start()
    sent = []
    for n in range(8):
        copies[n].wait()
        for d in range(16 * n, 16 * n + 16):
            packed[18 * d : 18 * d + 18, :] = held[d, 0:18, :]
            out_ref[6 * d : 6 * d + 6, :] = held[d, 18:24, :]
            out_ref[D + 6 * d : D + 6 * d + 6, :] = held[d, 24:30, :]
        part = pl.ds(288 * n, 288)
        sent.append(pltpu.make_async_copy(packed.at[part], triple_ref.at[part], out_sems.at[n]))
        sent[n].start()
    for copy in sent:
        copy.wait()


def column_block(bl_ref, stack_ref, outs_ref, far_ref, pair_ref, cw_ref, out_ref, pair_out_ref, w_ref, sems):
    copies = []
    for n in range(6):
        part = pl.ds(384 * n, 384)
        copies.append(pltpu.make_async_copy(far_ref.at[part], w_ref.at[part], sems.at[n]))
        copies[n].start()
    lane = lax.broadcasted_iota(jnp.int32, (L, L), 1)
    row = lax.broadcasted_iota(jnp.int32, (L, L), 0)
    low = lane < E
    early = lax.rem(row, 8) < 4

    slot = lax.rem(lax.broadcasted_iota(jnp.int32, (E, L), 0), 8)

    def tile(c, z, y):
        return bl_ref[z * 8 + y].astype(F32)[8 * c : 8 * c + 8]

    def block(y):
        left, right = (jnp.concatenate([tile(c, z, y) for z in range(8)], axis=0) for c in range(2))
        halves = []
        for high in range(2):
            from_left = jnp.zeros((E, L), jnp.bool_)
            for s in range(8):
                away = (4 * high + s // 2 - y) % 8
                if away > 4 or (away == 0 and s % 2 == 0) or (away == 4 and s % 2 == 1):
                    from_left = jnp.logical_or(from_left, slot == s)
            halves.append(jnp.where(from_left, left, right))
        return jnp.concatenate(halves, axis=0)

    blocks = [block(y) for y in range(8)]
    parts = []
    for n in range(2):
        e0, o0, e1, o1 = blocks[4 * n : 4 * n + 4]
        ro0, re1 = pltpu.roll(o0, E, 1), pltpu.roll(e1, E, 1)
        parts.append(jnp.where(jnp.logical_or(low, early), e0, ro0))
        parts.append(jnp.where(low, ro0, re1))
        parts.append(jnp.where(jnp.logical_and(low, early), re1, o1))
    blended = jnp.concatenate(parts, axis=1).astype(BF)

    updated = (dot_nt(outs_ref[D:], blended) + stack_ref[...].astype(F32)).astype(BF).astype(F32)
    center = jnp.mean(updated, axis=0, keepdims=True)
    spread = jnp.mean(jnp.square(updated - center), axis=0, keepdims=True)
    normed = ((updated - center) * lax.rsqrt(spread + 1e-05)).astype(BF)
    for copy in copies:
        copy.wait()
    packed = jnp.dot(w_ref[...], normed, preferred_element_type=F32)

    mixed = []
    for h in range(H):
        q = (packed[E * h : E * h + E] * E**-0.5).astype(BF)
        k = packed[D + E * h : D + E * h + E].astype(BF)
        v = packed[2 * D + E * h : 2 * D + E * h + E].astype(BF)
        logits = dot_tn(k, q)
        e = jnp.exp(logits - jnp.max(logits, axis=0, keepdims=True))
        probs = (e / jnp.sum(e, axis=0, keepdims=True)).astype(BF)
        mixed.append(jnp.dot(v, probs, preferred_element_type=F32).astype(BF))
    mixed = jnp.concatenate(mixed, axis=0)

    result = (updated + jnp.dot(outs_ref[:D], mixed, preferred_element_type=F32)).astype(BF)
    place = (row // 8 % 2 * E + row // 16 * 8 + row % 8 == lane).astype(BF)
    out_ref[...] = dot_nt(place, result).astype(BF)

    one = lax.broadcasted_iota(jnp.int32, (1, L), 1) < E
    lines = []
    for n in range(4):
        e, o = tile(0, 0, 2 * n), tile(0, 0, 2 * n + 1)
        re, ro = pltpu.roll(e, E, 1), pltpu.roll(o, E, 1)
        lines.append(jnp.where(one, re[4:5], e[5:6]))
        lines.append(jnp.where(one, re[6:7], e[7:8]))
        lines.append(jnp.where(one, o[2:3], ro[3:4]))
    scores = jnp.concatenate(lines + [jnp.zeros((L - H, L), F32)], axis=0).T
    weights = jnp.concatenate([cw_ref[...].astype(F32), jnp.zeros((L - H, L), F32)], axis=0)
    pair = pair_ref[...].astype(F32) + jnp.dot(
        scores.astype(BF), weights.astype(BF), preferred_element_type=F32
    )
    pair_out_ref[...] = pair.astype(BF)


def around(x):
    pairs = [(2 * y + c, (y + 1 - 2 * c) % 8 * 2 + c) for y in range(8) for c in range(2)]
    return lax.ppermute(x, ("y", "c"), pairs)


def per_device(stack, spans, pair, w_triple, w_out, v_triple, v_out, offsets, contact_w):
    y, c = lax.axis_index("y"), lax.axis_index("c")
    y1, c1 = y[None].astype(jnp.int32), c[None].astype(jnp.int32)
    at = jnp.concatenate([y1, c1])
    pair_own = pair.reshape(L, 128)
    own_row = stack.reshape(L, D)

    column_weights = jnp.concatenate([v_triple.T, v_out.T, w_out.T, jnp.zeros((2, D), BF)], axis=0)
    gathered = lax.all_gather(column_weights, ROWS, axis=0, tiled=False)

    normed = normalize(own_row.astype(F32)).astype(BF)
    one = around(lax.all_gather(normed, "c", axis=0, tiled=False))
    two = around(one)

    bias = lax.dot_general(offsets, pair_own, (((0,), (1,)), ((), ())), preferred_element_type=F32).astype(BF)
    bias_pairs = jnp.stack([bias[first_head(n) : first_head(n) + 2] for n in range(8)])
    slices = w_triple.T.reshape(18, 2, 8, 48).transpose(2, 0, 1, 3).reshape(8, 1, 18, 96)
    slices = jnp.pad(slices, ((0, 0), (0, 0), (0, 0), (0, 32)))
    message = jnp.concatenate(
        [
            jnp.broadcast_to(slices, (8, 8, 18, 128)).reshape(64, 18, 128),
            own_row.reshape(64, 12, 128),
            jnp.broadcast_to(bias_pairs[None], (8, 8, 2, 128)).reshape(64, 2, 128),
        ],
        axis=1,
    )
    came = lax.all_to_all(message, CHIPS, 0, 0, tiled=True)
    source = lax.broadcasted_iota(jnp.int32, (2048, 384), 0)
    target = lax.broadcasted_iota(jnp.int32, (2048, 384), 1)
    column = (source // 32 * 2 + c) * 18 + source % 32
    wanted = target // 128 * D + first_head(y) * E + target % 128
    pick = jnp.logical_and(column == wanted, source % 32 < 18).astype(BF)
    came, one, pick = lax.optimization_barrier((came, one, pick))
    picked = dot_tn(came.reshape(2048, 128), pick)[:96].astype(BF)
    picked = lax.all_gather(picked, "c", axis=0, tiled=False)
    half = lax.dynamic_slice_in_dim(picked, c * 48, 48, axis=1)
    half = half[0] + half[1]
    three = around(lax.optimization_barrier((half, two))[1])
    four = around(jnp.where(c == 0, three[1], three[0]))
    over_z = lax.all_to_all(jnp.broadcast_to(half, (8, 48, 384)), "z", 0, 0, tiled=True)
    w_heads = lax.all_gather(over_z, "c", axis=0, tiled=False).reshape(D, 384)

    stack_own = lax.all_gather(came[:, 18:30], "c", axis=0, tiled=False).reshape(2, 64, 2, D)
    stack_own = lax.dynamic_index_in_dim(stack_own, c, 2, keepdims=False).reshape(2, 8, 2, 4, D)
    stack_own = stack_own.transpose(2, 1, 3, 0, 4).reshape(R, D)
    bias_own = came[:, 30:].transpose(1, 0, 2)

    tied, values = pl.pallas_call(
        project_and_tie,
        out_shape=(
            jax.ShapeDtypeStruct((2, 2, L // 2, L), F32),
            jax.ShapeDtypeStruct((8, L, 2 * E), BF),
        ),
        scratch_shapes=[pltpu.VMEM((L, L), F32)],
        in_specs=[SMEM] + [VMEM] * 6,
        out_specs=(VMEM, VMEM),
        compiler_params=params(),
    )(at, w_heads, normed, one, two, three, four)

    tied = lax.all_gather(tied, "c", axis=0, tiled=False)
    tied = lax.dynamic_index_in_dim(tied, c, 1, keepdims=False)
    tied = (tied[0] + tied[1]).astype(BF)
    parts = lax.all_to_all(jnp.broadcast_to(tied, (8, 2, L // 2, L)), "z", 0, 0, tiled=True)
    message = pl.pallas_call(
        attend,
        out_shape=jax.ShapeDtypeStruct((L // 2, 16, 2 * E), BF),
        in_specs=[SMEM, SMEM, VMEM, VMEM, VMEM],
        out_specs=VMEM,
        scratch_shapes=[pltpu.VMEM((L // 2, 16, 2 * E), F32)],
        compiler_params=params(),
    )(at, spans, parts, bias_own, lax.all_gather(values, "c", axis=0, tiled=False))
    came = lax.all_to_all(message, CHIPS, 0, 0, tiled=True)
    triple, outs = pl.pallas_call(
        pack,
        out_shape=(jax.ShapeDtypeStruct((3 * D, D), BF), jax.ShapeDtypeStruct((2 * D, D), BF)),
        in_specs=[ANY],
        out_specs=(ANY, VMEM),
        scratch_shapes=[
            pltpu.VMEM((128, 32, D), BF),
            pltpu.VMEM((3 * D, D), BF),
            pltpu.SemaphoreType.DMA((8,)),
            pltpu.SemaphoreType.DMA((8,)),
        ],
        compiler_params=params(48),
    )(gathered)
    blended, triple, outs = lax.optimization_barrier((came, triple, outs))

    alignment, pair_out = pl.pallas_call(
        column_block,
        out_shape=(jax.ShapeDtypeStruct((R, D), BF), jax.ShapeDtypeStruct((L, 128), BF)),
        in_specs=[VMEM, VMEM, VMEM, ANY, VMEM, VMEM],
        out_specs=(VMEM, VMEM),
        scratch_shapes=[pltpu.VMEM((3 * D, D), BF), pltpu.SemaphoreType.DMA((6,))],
        compiler_params=params(50),
    )(blended, stack_own.T, outs, triple, pair_own, contact_w)
    return alignment.reshape(R, 1, D), pair_out.reshape(1, L, 128)


def solution(mesh):
    torus = Mesh(mesh.devices.reshape(mesh.shape["aln"], 8, 8, 2), ALL)
    in_specs = (
        P(ALL, None, None),
        P("a"),
        P(ALL, None, None),
        P(None, ROWS),
        P(None, ROWS),
        P(None, ROWS),
        P(None, ROWS),
        P(),
        P(),
    )
    out_specs = (P("a", ROWS, None), P(ALL, None, None))
    return jax.shard_map(
        per_device, mesh=torus, in_specs=in_specs, out_specs=out_specs, check_vma=False
    )
```

```python
import jax
import jax.numpy as jnp
from jax import lax
from jax.experimental import pallas as pl
from jax.experimental.pallas import tpu as pltpu
from jax.sharding import Mesh
from jax.sharding import PartitionSpec as P

ALL = ("a", "z", "y", "c")
ROWS = ("z", "y", "c")
CHIPS = ("z", "y")
D, H, E, L, R = 768, 12, 64, 128, 128
BF, F32 = jnp.bfloat16, jnp.float32
VMEM = pl.BlockSpec(memory_space=pltpu.VMEM)
SMEM = pl.BlockSpec(memory_space=pltpu.SMEM)
ANY = pl.BlockSpec(memory_space=pl.ANY)


def params(mib=16):
    return pltpu.CompilerParams(vmem_limit_bytes=mib << 20)


def dot_nt(a, b):
    return lax.dot_general(a, b, (((1,), (1,)), ((), ())), preferred_element_type=F32)


def dot_tn(a, b):
    return lax.dot_general(a, b, (((0,), (0,)), ((), ())), preferred_element_type=F32)


def first_head(y):
    return 3 * (y // 2) + y % 2


def normalize(x):
    center = jnp.mean(x, axis=-1, keepdims=True)
    spread = jnp.mean(jnp.square(x - center), axis=-1, keepdims=True)
    return (x - center) * lax.rsqrt(spread + 1e-05)


def project_and_tie(at_ref, w_ref, own_ref, one_ref, two_ref, three_ref, four_ref, tied_ref, v_ref, held):
    w = w_ref[...]
    lane = lax.broadcasted_iota(jnp.int32, (L, 2 * E), 1)
    y, c = at_ref[0], at_ref[1]
    step = 2 * c - 1
    rows = [(own_ref, None, 0, c), (four_ref, None, 4, 1 - c)]
    for n, ref in enumerate((one_ref, two_ref, three_ref)):
        rows += [(ref, core, (n + 1) * step, core) for core in range(2)]
    tied = [jnp.zeros((L, L), F32), jnp.zeros((L, L), F32)]
    for ref, core, offset, source in rows:
        x = ref[...] if core is None else ref[core]
        packed = jnp.dot(x, w, preferred_element_type=F32)
        q = packed[:, : 2 * E] * E**-0.5
        k = packed[:, 2 * E : 4 * E].astype(BF)
        v_ref[2 * lax.rem(y + 8 + offset, 4) + source] = packed[:, 4 * E :].astype(BF)
        tied[0] += dot_nt(jnp.where(lane < E, q, 0.0).astype(BF), k)
        tied[1] += dot_nt(jnp.where(lane < E, 0.0, q).astype(BF), k)
    for h in range(2):
        held[...] = tied[h] * R**-0.5
        for core in range(2):
            tied_ref[core, h] = held[pl.ds(core, L // 2, stride=2), :]


def attend(at_ref, span_ref, part_ref, bias_ref, v_ref, out_ref, held):
    lane = lax.broadcasted_iota(jnp.int32, (L // 2, 2 * E), 1)
    low = lane < E
    odd = lax.rem(at_ref[0], 2) == 1
    probs, plain, moved = [], [], []
    for h in range(2):
        scores = bias_ref[h].astype(F32)
        for n in range(8):
            scores += part_ref[n, h].astype(F32)
        masked = jnp.where(lane < span_ref[0], scores, -1e30)
        e = jnp.exp(masked - jnp.max(masked, axis=1, keepdims=True))
        probs.append((e / jnp.sum(e, axis=1, keepdims=True)).astype(BF))
        plain.append(scores)
        moved.append(pltpu.roll(scores, E, 1))
    for core in range(2):
        for n in range(8):
            v = v_ref[core, n]
            o = jnp.where(
                low,
                jnp.dot(probs[0], v, preferred_element_type=F32),
                jnp.dot(probs[1], v, preferred_element_type=F32),
            )
            h, second = (n % 4) // 2, n % 2
            if n < 4:
                extra = moved[h] if second else plain[h]
                o = jnp.where(jnp.logical_and(low, odd), extra, o)
            else:
                extra = plain[h] if second else moved[h]
                o = jnp.where(jnp.logical_or(low, odd), o, extra)
            held[:, 8 * core + n, :] = o
    out_ref[...] = held[...].astype(BF)


def pack(far_ref, out_ref, held, packed, in_sems, out_sems):
    copies = [
        pltpu.make_async_copy(far_ref.at[pl.ds(16 * n, 16)], held.at[pl.ds(16 * n, 16)], in_sems.at[n])
        for n in range(8)
    ]
    for copy in copies:
        copy.start()
    sent = []
    for n in range(8):
        copies[n].wait()
        for d in range(16 * n, 16 * n + 16):
            packed[18 * d : 18 * d + 18, :] = held[d, 0:18, :]
            packed[3 * D + 6 * d : 3 * D + 6 * d + 6, :] = held[d, 18:24, :]
            packed[4 * D + 6 * d : 4 * D + 6 * d + 6, :] = held[d, 24:30, :]
        for m, (start, rows) in enumerate(((288 * n, 288), (3 * D + 96 * n, 96), (4 * D + 96 * n, 96))):
            part = pl.ds(start, rows)
            sent.append(pltpu.make_async_copy(packed.at[part], out_ref.at[part], out_sems.at[3 * n + m]))
            sent[-1].start()
    for copy in sent:
        copy.wait()


def column_block(bl_ref, stack_ref, far_ref, pair_ref, cw_ref, out_ref, pair_out_ref, w_ref, sems):
    order = (8, 9, 0, 1, 2, 3, 4, 5, 6, 7)
    copies = []
    for n, m in enumerate(order):
        part = pl.ds(384 * m, 384)
        copies.append(pltpu.make_async_copy(far_ref.at[part], w_ref.at[part], sems.at[n]))
        copies[n].start()
    lane = lax.broadcasted_iota(jnp.int32, (L, L), 1)
    row = lax.broadcasted_iota(jnp.int32, (L, L), 0)
    low = lane < E
    early = lax.rem(row, 8) < 4

    slot = lax.rem(lax.broadcasted_iota(jnp.int32, (E, L), 0), 8)

    def tile(c, z, y):
        return bl_ref[z * 8 + y].astype(F32)[8 * c : 8 * c + 8]

    def block(y):
        left, right = (jnp.concatenate([tile(c, z, y) for z in range(8)], axis=0) for c in range(2))
        halves = []
        for high in range(2):
            from_left = jnp.zeros((E, L), jnp.bool_)
            for s in range(8):
                away = (4 * high + s // 2 - y) % 8
                if away > 4 or (away == 0 and s % 2 == 0) or (away == 4 and s % 2 == 1):
                    from_left = jnp.logical_or(from_left, slot == s)
            halves.append(jnp.where(from_left, left, right))
        return jnp.concatenate(halves, axis=0)

    blocks = [block(y) for y in range(8)]
    parts = []
    for n in range(2):
        e0, o0, e1, o1 = blocks[4 * n : 4 * n + 4]
        ro0, re1 = pltpu.roll(o0, E, 1), pltpu.roll(e1, E, 1)
        parts.append(jnp.where(jnp.logical_or(low, early), e0, ro0))
        parts.append(jnp.where(low, ro0, re1))
        parts.append(jnp.where(jnp.logical_and(low, early), re1, o1))
    blended = jnp.concatenate(parts, axis=1).astype(BF)

    for copy in copies[:2]:
        copy.wait()
    updated = (dot_nt(w_ref[4 * D :], blended) + stack_ref[...].astype(F32)).astype(BF).astype(F32)
    center = jnp.mean(updated, axis=0, keepdims=True)
    spread = jnp.mean(jnp.square(updated - center), axis=0, keepdims=True)
    normed = ((updated - center) * lax.rsqrt(spread + 1e-05)).astype(BF)
    for copy in copies[2:8]:
        copy.wait()
    packed = jnp.dot(w_ref[: 3 * D], normed, preferred_element_type=F32)

    mixed = []
    for h in range(H):
        q = (packed[E * h : E * h + E] * E**-0.5).astype(BF)
        k = packed[D + E * h : D + E * h + E].astype(BF)
        v = packed[2 * D + E * h : 2 * D + E * h + E].astype(BF)
        logits = dot_tn(k, q)
        e = jnp.exp(logits - jnp.max(logits, axis=0, keepdims=True))
        probs = (e / jnp.sum(e, axis=0, keepdims=True)).astype(BF)
        mixed.append(jnp.dot(v, probs, preferred_element_type=F32).astype(BF))
    mixed = jnp.concatenate(mixed, axis=0)

    for copy in copies[8:]:
        copy.wait()
    result = (updated + jnp.dot(w_ref[3 * D : 4 * D], mixed, preferred_element_type=F32)).astype(BF)
    place = (row // 8 % 2 * E + row // 16 * 8 + row % 8 == lane).astype(BF)
    out_ref[...] = dot_nt(place, result).astype(BF)

    one = lax.broadcasted_iota(jnp.int32, (1, L), 1) < E
    lines = []
    for n in range(4):
        e, o = tile(0, 0, 2 * n), tile(0, 0, 2 * n + 1)
        re, ro = pltpu.roll(e, E, 1), pltpu.roll(o, E, 1)
        lines.append(jnp.where(one, re[4:5], e[5:6]))
        lines.append(jnp.where(one, re[6:7], e[7:8]))
        lines.append(jnp.where(one, o[2:3], ro[3:4]))
    scores = jnp.concatenate(lines + [jnp.zeros((L - H, L), F32)], axis=0).T
    weights = jnp.concatenate([cw_ref[...].astype(F32), jnp.zeros((L - H, L), F32)], axis=0)
    pair = pair_ref[...].astype(F32) + jnp.dot(
        scores.astype(BF), weights.astype(BF), preferred_element_type=F32
    )
    pair_out_ref[...] = pair.astype(BF)


def around(x):
    pairs = [(2 * y + c, (y + 1 - 2 * c) % 8 * 2 + c) for y in range(8) for c in range(2)]
    return lax.ppermute(x, ("y", "c"), pairs)


def per_device(stack, spans, pair, w_triple, w_out, v_triple, v_out, offsets, contact_w):
    y, c = lax.axis_index("y"), lax.axis_index("c")
    y1, c1 = y[None].astype(jnp.int32), c[None].astype(jnp.int32)
    at = jnp.concatenate([y1, c1])
    pair_own = pair.reshape(L, 128)
    own_row = stack.reshape(L, D)

    column_weights = jnp.concatenate([v_triple.T, v_out.T, w_out.T, jnp.zeros((2, D), BF)], axis=0)
    gathered = lax.all_gather(column_weights, ROWS, axis=0, tiled=False)

    normed = normalize(own_row.astype(F32)).astype(BF)
    one = around(lax.all_gather(normed, "c", axis=0, tiled=False))
    two = around(one)

    bias = lax.dot_general(offsets, pair_own, (((0,), (1,)), ((), ())), preferred_element_type=F32).astype(BF)
    bias_pairs = jnp.stack([bias[first_head(n) : first_head(n) + 2] for n in range(8)])
    slices = w_triple.T.reshape(18, 2, 8, 48).transpose(2, 0, 1, 3).reshape(8, 1, 18, 96)
    slices = jnp.pad(slices, ((0, 0), (0, 0), (0, 0), (0, 32)))
    message = jnp.concatenate(
        [
            jnp.broadcast_to(slices, (8, 8, 18, 128)).reshape(64, 18, 128),
            own_row.reshape(64, 12, 128),
            jnp.broadcast_to(bias_pairs[None], (8, 8, 2, 128)).reshape(64, 2, 128),
        ],
        axis=1,
    )
    came = lax.all_to_all(message, CHIPS, 0, 0, tiled=True)
    source = lax.broadcasted_iota(jnp.int32, (2048, 384), 0)
    target = lax.broadcasted_iota(jnp.int32, (2048, 384), 1)
    column = (source // 32 * 2 + c) * 18 + source % 32
    wanted = target // 128 * D + first_head(y) * E + target % 128
    pick = jnp.logical_and(column == wanted, source % 32 < 18).astype(BF)
    came, pick = lax.optimization_barrier((came, pick))
    picked = dot_tn(came.reshape(2048, 128), pick)[:96].astype(BF)
    picked = lax.all_gather(picked, "c", axis=0, tiled=False)
    half = lax.dynamic_slice_in_dim(picked, c * 48, 48, axis=1)
    half = half[0] + half[1]
    three = around(lax.optimization_barrier((half, two))[1])
    four = around(jnp.where(c == 0, three[1], three[0]))
    over_z = lax.all_to_all(jnp.broadcast_to(half, (8, 48, 384)), "z", 0, 0, tiled=True)
    w_heads = lax.all_gather(over_z, "c", axis=0, tiled=False).reshape(D, 384)

    stack_own = lax.all_gather(came[:, 18:30], "c", axis=0, tiled=False).reshape(2, 64, 2, D)
    stack_own = lax.dynamic_index_in_dim(stack_own, c, 2, keepdims=False).reshape(2, 8, 2, 4, D)
    stack_own = stack_own.transpose(2, 1, 3, 0, 4).reshape(R, D)
    bias_own = came[:, 30:].transpose(1, 0, 2)

    tied, values = pl.pallas_call(
        project_and_tie,
        out_shape=(
            jax.ShapeDtypeStruct((2, 2, L // 2, L), F32),
            jax.ShapeDtypeStruct((8, L, 2 * E), BF),
        ),
        scratch_shapes=[pltpu.VMEM((L, L), F32)],
        in_specs=[SMEM] + [VMEM] * 6,
        out_specs=(VMEM, VMEM),
        compiler_params=params(),
    )(at, w_heads, normed, one, two, three, four)

    tied = lax.all_gather(tied, "c", axis=0, tiled=False)
    tied = lax.dynamic_index_in_dim(tied, c, 1, keepdims=False)
    tied = (tied[0] + tied[1]).astype(BF)
    parts = lax.all_to_all(jnp.broadcast_to(tied, (8, 2, L // 2, L)), "z", 0, 0, tiled=True)
    message = pl.pallas_call(
        attend,
        out_shape=jax.ShapeDtypeStruct((L // 2, 16, 2 * E), BF),
        in_specs=[SMEM, SMEM, VMEM, VMEM, VMEM],
        out_specs=VMEM,
        scratch_shapes=[pltpu.VMEM((L // 2, 16, 2 * E), F32)],
        compiler_params=params(),
    )(at, spans, parts, bias_own, lax.all_gather(values, "c", axis=0, tiled=False))
    came = lax.all_to_all(message, CHIPS, 0, 0, tiled=True)
    column_weights = pl.pallas_call(
        pack,
        out_shape=jax.ShapeDtypeStruct((5 * D, D), BF),
        in_specs=[ANY],
        out_specs=ANY,
        scratch_shapes=[
            pltpu.VMEM((128, 32, D), BF),
            pltpu.VMEM((5 * D, D), BF),
            pltpu.SemaphoreType.DMA((8,)),
            pltpu.SemaphoreType.DMA((24,)),
        ],
        compiler_params=params(56),
    )(gathered)
    blended, column_weights = lax.optimization_barrier((came, column_weights))

    alignment, pair_out = pl.pallas_call(
        column_block,
        out_shape=(jax.ShapeDtypeStruct((R, D), BF), jax.ShapeDtypeStruct((L, 128), BF)),
        in_specs=[VMEM, VMEM, ANY, VMEM, VMEM],
        out_specs=(VMEM, VMEM),
        scratch_shapes=[pltpu.VMEM((5 * D, D), BF), pltpu.SemaphoreType.DMA((10,))],
        compiler_params=params(52),
    )(blended, stack_own.T, column_weights, pair_own, contact_w)
    return alignment.reshape(R, 1, D), pair_out.reshape(1, L, 128)


def solution(mesh):
    torus = Mesh(mesh.devices.reshape(mesh.shape["aln"], 8, 8, 2), ALL)
    in_specs = (
        P(ALL, None, None),
        P("a"),
        P(ALL, None, None),
        P(None, ROWS),
        P(None, ROWS),
        P(None, ROWS),
        P(None, ROWS),
        P(),
        P(),
    )
    out_specs = (P("a", ROWS, None), P(ALL, None, None))
    return jax.shard_map(
        per_device, mesh=torus, in_specs=in_specs, out_specs=out_specs, check_vma=False
    )
```
